128 devices in a mesh: row: 16 (over y, x_lo, core), col: 8 (over x_hi, z).
Axes of the slice: x: 4 (x_hi: 2, x_lo: 2; x = x_hi * 2 + x_lo), y: 4, z: 4, core: 2. Of those that a mesh axis runs over, the one named last changes fastest.
Arguments:
- tokens: bfloat16 [1024, 8192], P('col', 'row'), may hold values from -6 to 6
- gate_weight: bfloat16 [8192, 14336], P('row', 'col'), may hold values from -0.0625 to 0.0625
- up_weight: bfloat16 [8192, 14336], P('row', 'col'), may hold values from -0.0625 to 0.0625
- down_weight: bfloat16 [14336, 8192], P('col', 'row'), may hold values from -0.046875 to 0.046875
- grad_output: bfloat16 [1024, 8192], P('col', 'row'), may hold values from -6 to 6
Outputs:
- layer_output: bfloat16 [1024, 8192], P('col', 'row')
- grad_input: bfloat16 [1024, 8192], P('col', 'row')
- grad_gate: bfloat16 [8192, 14336], P('row', 'col')
- grad_up: bfloat16 [8192, 14336], P('row', 'col')
- grad_down: bfloat16 [14336, 8192], P('col', 'row')
The draws below stay inside these ranges and needn't reach their ends.
All inputs are finite; a program needn't handle non-finite values.
Results may differ from the reference program's by a relative error of at most 0.005.
Values may be sent and summed in bfloat16 or wider, within the bound.
No kernel may reach another device: no remote copies, remote signals or barrier semaphores. Data moves between devices by JAX's collectives and lax.ppermute only.
A program may use at most 128 MiB of HBM per device.

```python
import jax
import jax.numpy as jnp

D = 8192
FF = 14336
TOKENS = 1024


def spiked(result, own_key, source, target, parts, factor):
    owner, partner = [(jnp.arange(result.shape[axis_at]) // (result.shape[axis_at] // parts)).reshape([-1 if axis == axis_at else 1 for axis in range(result.ndim)]) for axis_at in (source, target)]
    chosen = jax.random.permutation(own_key, parts)[partner]
    strong = (owner == chosen) | (owner == (partner + parts // 2) % parts)
    return jnp.where(strong, factor * result, result)


def levels(key, shape, split, least, high):
    level = 1.0
    for position, parts in split:
        steps = jax.random.uniform(jax.random.fold_in(jax.random.fold_in(key, 6), position), (parts,), jnp.float32, least / len(split), high / len(split))
        level = level * jnp.repeat(jnp.exp(steps), shape[position] // parts).reshape((-1,) + (1,) * (len(shape) - 1 - position))
    return level


def bell_draw(own_key, shape, spread, reach, pieces=(), held_as=jnp.bfloat16):
    gain = levels(own_key, shape, pieces, -0.22, 0.18) if pieces else 1.0
    values = jax.random.normal(own_key, shape, jnp.float32) * spread * gain
    return jnp.minimum(jnp.maximum(values, -reach), reach).astype(held_as)


def noise_with(rng, shape, spread, limit, cuts, heavy, kind=jnp.bfloat16):
    result = spread * jax.random.normal(rng, shape, jnp.float32)
    if cuts:
        result = result * levels(rng, shape, cuts, -0.22, 0.18)
    return jnp.clip(spiked(result, jax.random.fold_in(rng, 3), *heavy), -limit, limit).astype(kind)


def setup_inputs(seed: int = 0) -> dict:
    splits = jax.random.split(jax.random.key(seed), 6)
    tokens = noise_with(splits[0], (TOKENS, D), 1.0, 6.0, ((0, 8), (1, 16)), (1, 0, 16, 2.0))
    gate_weight = bell_draw(splits[1], (D, FF), D ** -0.5, 0.0625, ((0, 16), (1, 8)))
    up_weight = bell_draw(splits[2], (D, FF), D ** -0.5, 0.0625, ((0, 16), (1, 8)))
    down_weight = bell_draw(splits[3], (FF, D), FF ** -0.5, 0.046875, ((0, 8), (1, 16)))
    grad_output = noise_with(splits[4], (TOKENS, D), 1.0, 6.0, ((0, 8), (1, 16)), (1, 0, 16, 2.0))
    return {"tokens": tokens, "gate_weight": gate_weight, "up_weight": up_weight, "down_weight": down_weight, "grad_output": grad_output}


def reference(tokens, gate_weight, up_weight, down_weight, grad_output):
    gate_value = jnp.dot(tokens, gate_weight, preferred_element_type=jnp.float32)
    up_value = jnp.dot(tokens, up_weight, preferred_element_type=jnp.float32)
    sig_gate = jax.nn.sigmoid(gate_value)
    hidden = (gate_value * sig_gate * up_value).astype(jnp.bfloat16)
    layer_output = jnp.dot(hidden, down_weight, preferred_element_type=jnp.float32).astype(jnp.bfloat16)
    d_hidden = jnp.dot(grad_output, down_weight.T, preferred_element_type=jnp.float32)
    d_gate = (d_hidden * up_value * sig_gate * (1.0 + gate_value * (1.0 - sig_gate))).astype(jnp.bfloat16)
    d_up = (d_hidden * gate_value * sig_gate).astype(jnp.bfloat16)
    grad_down = jnp.dot(hidden.T, grad_output, preferred_element_type=jnp.float32).astype(jnp.bfloat16)
    grad_gate = jnp.dot(tokens.T, d_gate, preferred_element_type=jnp.float32).astype(jnp.bfloat16)
    grad_up = jnp.dot(tokens.T, d_up, preferred_element_type=jnp.float32).astype(jnp.bfloat16)
    input_sum = jnp.dot(d_gate, gate_weight.T, preferred_element_type=jnp.float32) + jnp.dot(d_up, up_weight.T, preferred_element_type=jnp.float32)
    grad_input = input_sum.astype(jnp.bfloat16)
    return layer_output, grad_input, grad_gate, grad_up, grad_down
```

```python
import functools

import jax
import jax.numpy as jnp
from jax import lax
from jax.experimental import pallas as pl
from jax.experimental.pallas import tpu as pltpu
from jax.sharding import PartitionSpec as P

NY, NX, NC, NZ = 4, 2, 2, 4
PIECE = 64
BOTH = ("row", "col")


def row_at(y, x, core):
    return ((y % NY) * NX + x) * NC + core


def row_perm(core0, core1):
    pairs = []
    for y in range(NY):
        for x in range(NX):
            for core, move in ((0, core0), (1, core1)):
                if move is not None:
                    to_y, to_x = move(y, x)
                    pairs.append((row_at(y, x, core), row_at(to_y, to_x, core)))
    return pairs


def over_x(y, x):
    return y, 1 - x


def over_y(step):
    return lambda y, x: (y + step, x)


CORE_FLIP = [(i, i ^ 1) for i in range(NY * NX * NC)]


def gather_perm(step):
    pairs = []
    for row in range(NY * NX * NC):
        core = row % NC
        if core == 0 and step == 0:
            continue
        for hi in range(2):
            for z in range(NZ):
                source = (hi ^ core) * NZ + (z + step) % NZ
                pairs.append((row * 8 + source, row * 8 + hi * NZ + z))
    return pairs


def col_perm(flip, step):
    return [(hi * NZ + z, (hi ^ flip) * NZ + (z + step) % NZ) for hi in range(2) for z in range(NZ)]


def product(left, right, transposed):
    dims = (((1,), (1 if transposed else 0,)), ((), ()))
    return lax.dot_general(left, right, dims, preferred_element_type=jnp.float32)


def first_kernel(count, transposed, table, acts, *refs):
    weights, outs, held = refs[: 2 * count], refs[2 * count : 2 * count + 3], refs[-1]

    @pl.when(pl.program_id(0) == 0)
    def _():
        for slot in range(6):
            held[slot * PIECE : (slot + 1) * PIECE, :] = acts[table[slot]]

    half = held.shape[1] // 2
    for which in range(count):
        total = product(held[:, :half], weights[2 * which][...], transposed)
        total += product(held[:, half:], weights[2 * which + 1][...], transposed)
        total = total.astype(jnp.bfloat16)
        for message in range(3):
            outs[message][which] = total[message * 2 * PIECE : (message + 1) * 2 * PIECE]


def second_kernel(count, transposed, table, acts, *refs):
    weights, heard, outs, held = (
        refs[: 2 * count],
        refs[2 * count : 2 * count + 3],
        refs[2 * count + 3 : 2 * count + 7],
        refs[-1],
    )

    @pl.when(pl.program_id(0) == 0)
    def _():
        for slot in range(4):
            held[slot * PIECE : (slot + 1) * PIECE, :] = acts[table[slot]]

    core, x = table[4], table[5]
    near = pl.ds(pl.multiple_of(x * PIECE, PIECE), PIECE)
    far = pl.ds(pl.multiple_of((1 - x) * PIECE, PIECE), PIECE)
    half = held.shape[1] // 2
    for which in range(count):
        total = product(held[:, :half], weights[2 * which][...], transposed)
        total += product(held[:, half:], weights[2 * which + 1][...], transposed)
        near1, near2, near3 = [h[which, near].astype(jnp.float32) for h in heard]
        far1, far2, far3 = [h[which, far].astype(jnp.float32) for h in heard]
        more_near = jnp.where(core == 1, near2 + near3, 0.0)
        more_far = jnp.where(core == 1, far2 + far3, 0.0)
        outs[0][which] = (total[:PIECE] + far1 + more_far).astype(jnp.bfloat16)
        outs[1][which] = (total[PIECE : 2 * PIECE] + near2).astype(jnp.bfloat16)
        outs[2][which] = (total[2 * PIECE : 3 * PIECE] + far2).astype(jnp.bfloat16)
        outs[3][which] = total[3 * PIECE :] + near1 + more_near


def stage(kernel, table, acts, weights, transposed, heard=()):
    count = len(weights)
    depth = weights[0][0].shape[1 if transposed else 0]
    width = weights[0][0].shape[0 if transposed else 1]
    block = 256
    if transposed:
        weight_spec = pl.BlockSpec((block, depth), lambda i, t: (i, 0))
    else:
        weight_spec = pl.BlockSpec((depth, block), lambda i, t: (0, i))
    if heard:
        rows, slots = [PIECE] * 4, 4
        types = [jnp.bfloat16] * 3 + [jnp.float32]
    else:
        rows, slots = [2 * PIECE] * 3, 6
        types = [jnp.bfloat16] * 3
    out_block = lambda n: pl.BlockSpec((count, n, block), lambda i, t: (0, 0, i))
    flops = 2 * slots * PIECE * 2 * depth * width * count
    return pl.pallas_call(
        functools.partial(kernel, count, transposed),
        grid_spec=pltpu.PrefetchScalarGridSpec(
            num_scalar_prefetch=1,
            grid=(width // block,),
            in_specs=[pl.BlockSpec(acts.shape, lambda i, t: (0, 0, 0))]
            + [weight_spec] * (2 * count)
            + [out_block(2 * PIECE)] * len(heard),
            out_specs=[out_block(n) for n in rows],
            scratch_shapes=[pltpu.VMEM((slots * PIECE, acts.shape[2]), jnp.bfloat16)],
        ),
        out_shape=[jax.ShapeDtypeStruct((count, n, width), d) for n, d in zip(rows, types)],
        compiler_params=pltpu.CompilerParams(vmem_limit_bytes=32 * 2**20),
        cost_estimate=pl.CostEstimate(
            flops=flops, bytes_accessed=4 * depth * width * count, transcendentals=0
        ),
    )(table, acts, *[w for pair in weights for w in pair], *heard)


def row_sum(acts, weights, transposed, first_table, second_table):
    sent = stage(first_kernel, first_table, acts, weights, transposed)
    heard = (
        lax.ppermute(sent[0], "row", row_perm(over_x, over_y(1))),
        lax.ppermute(sent[1], "row", row_perm(over_x, over_y(-1))),
        lax.ppermute(sent[2], "row", row_perm(None, over_y(2))),
    )
    *sent, kept = stage(second_kernel, second_table, acts, weights, transposed, heard)
    heard = (
        lax.ppermute(sent[0], "row", row_perm(over_y(1), over_x)),
        lax.ppermute(sent[1], "row", row_perm(over_y(-1), None)),
        lax.ppermute(sent[2], "row", row_perm(over_y(2), None)),
    )
    for term in heard:
        kept = kept + term.astype(jnp.float32)
    return kept


def col_sum(total):
    blocks = total.reshape(NY, NX, NC, PIECE, total.shape[1])
    away = blocks[:, :, 1].astype(jnp.bfloat16)
    heard = lax.ppermute(away, "col", col_perm(1, 0))
    near = blocks[:, :, 0] + heard.astype(jnp.float32)
    result = near[0]
    send = near[1:].astype(jnp.bfloat16)
    for step in range(1, NZ):
        result = result + lax.ppermute(send[step - 1], "col", col_perm(0, step)).astype(jnp.float32)
    return result.astype(jnp.bfloat16).reshape(NX * PIECE, total.shape[1])


def body(tokens, gate_weight, up_weight, down_weight, grad_output):
    row = lax.axis_index("row")
    core, x, y = row % NC, (row // NC) % NX, row // (NC * NX)
    piece = lambda y_at, x_at: (y_at % NY) * NX + x_at
    other = 1 - x
    first0 = [
        jnp.where(other == 0, piece(y, other), piece(y + 1, other)),
        jnp.where(other == 0, piece(y + 1, other), piece(y, other)),
        jnp.where(other == 0, piece(y + 3, other), piece(y + 2, other)),
        jnp.where(other == 0, piece(y + 2, other), piece(y + 3, other)),
        piece(y, x),
        piece(y, x),
    ]
    first1 = [piece(y + step, x_at) for step in (1, 3, 2) for x_at in (0, 1)]
    second0 = [piece(y + 1, x), piece(y + 3, x), piece(y + 2, x), piece(y, x)]
    second1 = [piece(y, other), piece(y, x), piece(y, x), piece(y, x)]
    choose = lambda zero, one: [jnp.where(core == 0, a, b) for a, b in zip(zero, one)]
    first_table = jnp.stack(choose(first0, first1)).astype(jnp.int32)
    second_table = jnp.stack(choose(second0, second1) + [core, x]).astype(jnp.int32)

    flip = lambda value: lax.ppermute(value, "row", CORE_FLIP)
    width = tokens.shape[1]
    mine = jnp.stack([tokens, grad_output])
    theirs = flip(mine)

    def gather(own, partner):
        block = jnp.concatenate([own, partner], axis=1)
        blocks = [lax.ppermute(block, BOTH, gather_perm(step)) for step in range(NZ)]
        blocks[0] = jnp.where(core == 0, block, blocks[0])
        return jnp.concatenate(blocks, axis=0).reshape(NY * NX, PIECE, 2 * width)

    tok_half = gather(tokens, theirs[0])
    gate_pair = (gate_weight, flip(gate_weight))
    up_pair = (up_weight, flip(up_weight))
    down_pair = (down_weight, flip(down_weight))
    grad_half = gather(grad_output, theirs[1])

    both = row_sum(tok_half, [gate_pair, up_pair], False, first_table, second_table)
    d_hidden = row_sum(grad_half, [down_pair], True, first_table, second_table)[0]
    gate_value, up_value = both[0], both[1]
    sig_gate = jax.nn.sigmoid(gate_value)
    hidden = (gate_value * sig_gate * up_value).astype(jnp.bfloat16)
    hidden = lax.all_gather(hidden, "row", axis=0, tiled=True)
    d_gate = (d_hidden * up_value * sig_gate * (1.0 + gate_value * (1.0 - sig_gate))).astype(
        jnp.bfloat16
    )
    d_up = (d_hidden * gate_value * sig_gate).astype(jnp.bfloat16)
    d_both = lax.all_gather(jnp.concatenate([d_gate, d_up], axis=1), "row", axis=0, tiled=True)
    ff_width = gate_weight.shape[1]
    d_gate, d_up = d_both[:, :ff_width], d_both[:, ff_width:]

    others = flip(jnp.stack([tok_half[:, :, width:], grad_half[:, :, width:]]))

    def all_rows(half, received):
        own = half[:, :, :width]
        pair = jnp.where(
            core == 0, jnp.stack([own, received], axis=1), jnp.stack([received, own], axis=1)
        )
        return pair.reshape(-1, width)

    tok_all, grad_all = all_rows(tok_half, others[0]), all_rows(grad_half, others[1])

    layer_output = col_sum(jnp.dot(hidden, down_weight, preferred_element_type=jnp.float32))
    last = (((1,), (1,)), ((), ()))
    first = (((0,), (0,)), ((), ()))
    dot = functools.partial(lax.dot_general, preferred_element_type=jnp.float32)
    grad_input = col_sum(dot(d_gate, gate_weight, last) + dot(d_up, up_weight, last))
    grad_down = dot(hidden, grad_all, first).astype(jnp.bfloat16)
    grad_gate = dot(tok_all, d_gate, first).astype(jnp.bfloat16)
    grad_up = dot(tok_all, d_up, first).astype(jnp.bfloat16)
    return (layer_output, grad_input, grad_gate, grad_up, grad_down)


def solution(mesh):
    placed = (P("col", "row"), P("row", "col"), P("row", "col"), P("col", "row"), P("col", "row"))
    return jax.shard_map(
        body,
        mesh=mesh,
        in_specs=placed,
        out_specs=(
            P("col", "row"),
            P("col", "row"),
            P("row", "col"),
            P("row", "col"),
            P("col", "row"),
        ),
        check_vma=False,
    )
```

```python
import functools

import jax
import jax.numpy as jnp
from jax import lax
from jax.experimental import pallas as pl
from jax.experimental.pallas import tpu as pltpu
from jax.sharding import PartitionSpec as P

NY, NX, NC, NZ = 4, 2, 2, 4
PIECE = 64
BOTH = ("row", "col")


def row_at(y, x, core):
    return ((y % NY) * NX + x) * NC + core


def row_perm(core0, core1):
    pairs = []
    for y in range(NY):
        for x in range(NX):
            for core, move in ((0, core0), (1, core1)):
                if move is not None:
                    to_y, to_x = move(y, x)
                    pairs.append((row_at(y, x, core), row_at(to_y, to_x, core)))
    return pairs


def over_x(y, x):
    return y, 1 - x


def over_y(step):
    return lambda y, x: (y + step, x)


CORE_FLIP = [(i, i ^ 1) for i in range(NY * NX * NC)]


def gather_perm(step):
    pairs = []
    for row in range(NY * NX * NC):
        core = row % NC
        if core == 0 and step == 0:
            continue
        for hi in range(2):
            for z in range(NZ):
                source = (hi ^ core) * NZ + (z + step) % NZ
                pairs.append((row * 8 + source, row * 8 + hi * NZ + z))
    return pairs


def col_perm(flip, step):
    return [(hi * NZ + z, (hi ^ flip) * NZ + (z + step) % NZ) for hi in range(2) for z in range(NZ)]


def product(left, right, transposed):
    dims = (((1,), (1 if transposed else 0,)), ((), ()))
    return lax.dot_general(left, right, dims, preferred_element_type=jnp.float32)


def spans(width):
    return [(at, min(at + 256, width)) for at in range(0, width, 256)]


def pair_product(held, pair, at, end, transposed):
    half = held.shape[1] // 2
    own, other = pair
    if transposed:
        own, other = own[at:end, :], other[at:end, :]
    else:
        own, other = own[:, at:end], other[:, at:end]
    return product(held[:, :half], own, transposed) + product(held[:, half:], other, transposed)


def first_kernel(count, transposed, table, *refs):
    blocks, weights = refs[: NZ + 1], refs[NZ + 1 : NZ + 1 + 2 * count]
    acts, *outs, held = refs[NZ + 1 + 2 * count :]
    width = outs[0].shape[2]
    rows = blocks[0].shape[0]
    acts[:rows] = jnp.where(table[CORE] == 0, blocks[0][...], blocks[1][...])
    for k in range(1, NZ):
        acts[k * rows : (k + 1) * rows] = blocks[k + 1][...]
    for slot in range(6):
        start = pl.multiple_of(table[FIRST + slot] * PIECE, PIECE)
        held[slot * PIECE : (slot + 1) * PIECE, :] = acts[pl.ds(start, PIECE), :]
    for at, end in spans(width):
        for which in range(count):
            pair = weights[2 * which : 2 * which + 2]
            total = pair_product(held, pair, at, end, transposed).astype(jnp.bfloat16)
            for message in range(3):
                outs[message][which, :, at:end] = total[
                    message * 2 * PIECE : (message + 1) * 2 * PIECE
                ]


def second_kernel(count, transposed, table, acts, *refs):
    weights, heard = refs[: 2 * count], refs[2 * count : 2 * count + 3]
    *outs, held = refs[2 * count + 3 :]
    width = outs[0].shape[2]
    core, x = table[CORE], table[AT_X]
    for slot in range(4):
        start = pl.multiple_of(table[SECOND + slot] * PIECE, PIECE)
        held[slot * PIECE : (slot + 1) * PIECE, :] = acts[pl.ds(start, PIECE), :]
    near = pl.ds(pl.multiple_of(x * PIECE, PIECE), PIECE)
    far = pl.ds(pl.multiple_of((1 - x) * PIECE, PIECE), PIECE)
    for at, end in spans(width):
        for which in range(count):
            pair = weights[2 * which : 2 * which + 2]
            total = pair_product(held, pair, at, end, transposed)
            near1, near2, near3 = [h[which, near, at:end].astype(jnp.float32) for h in heard]
            far1, far2, far3 = [h[which, far, at:end].astype(jnp.float32) for h in heard]
            sum1 = total[:PIECE] + far1 + jnp.where(core == 1, far2 + far3, 0.0)
            high = sum1.astype(jnp.bfloat16)
            rest = sum1 - high.astype(jnp.float32)
            sum2 = jnp.where(core == 1, rest, total[PIECE : 2 * PIECE] + near2)
            outs[0][which, :, at:end] = high
            outs[1][which, :, at:end] = sum2.astype(jnp.bfloat16)
            outs[2][which, :, at:end] = (total[2 * PIECE : 3 * PIECE] + far2).astype(jnp.bfloat16)
            outs[3][which, :, at:end] = (
                total[3 * PIECE :] + near1 + jnp.where(core == 1, near2 + near3, 0.0)
            )


def call(kernel, table, operands, out_shape, held_rows, depth, flops):
    vmem = pl.BlockSpec(memory_space=pltpu.VMEM)
    moved = sum(o.size * o.dtype.itemsize for o in [*operands, *out_shape])
    return pl.pallas_call(
        kernel,
        in_specs=[pl.BlockSpec(memory_space=pltpu.SMEM)] + [vmem] * len(operands),
        out_specs=[vmem] * len(out_shape),
        out_shape=out_shape,
        scratch_shapes=[pltpu.VMEM((held_rows, depth), jnp.bfloat16)],
        compiler_params=pltpu.CompilerParams(vmem_limit_bytes=40 * 2**20),
        cost_estimate=pl.CostEstimate(flops=flops, bytes_accessed=moved, transcendentals=0),
    )(table, *operands)


def first_stage(table, blocks, weights, transposed):
    count = len(weights)
    width = weights[0][0].shape[0 if transposed else 1]
    rows, depth = blocks[0].shape
    message = jax.ShapeDtypeStruct((count, 2 * PIECE, width), jnp.bfloat16)
    return call(
        functools.partial(first_kernel, count, transposed),
        table,
        [*blocks, *[w for pair in weights for w in pair]],
        [jax.ShapeDtypeStruct((NZ * rows, depth), jnp.bfloat16)] + [message] * 3,
        6 * PIECE,
        depth,
        2 * 6 * PIECE * depth * width * count,
    )


def second_stage(table, acts, weights, transposed, heard):
    count = len(weights)
    width = weights[0][0].shape[0 if transposed else 1]
    message = jax.ShapeDtypeStruct((count, PIECE, width), jnp.bfloat16)
    return call(
        functools.partial(second_kernel, count, transposed),
        table,
        [acts, *[w for pair in weights for w in pair], *heard],
        [message] * 3 + [jax.ShapeDtypeStruct((count, PIECE, width), jnp.float32)],
        4 * PIECE,
        acts.shape[1],
        2 * 4 * PIECE * acts.shape[1] * width * count,
    )


def send_first(sent):
    return (
        lax.ppermute(sent[0], "row", row_perm(over_x, over_y(1))),
        lax.ppermute(sent[1], "row", row_perm(over_x, over_y(-1))),
        lax.ppermute(sent[2], "row", row_perm(None, over_y(2))),
    )


def send_second(sent):
    return (
        lax.ppermute(sent[0], "row", row_perm(over_y(1), over_x)),
        lax.ppermute(sent[1], "row", row_perm(over_y(-1), over_x)),
        lax.ppermute(sent[2], "row", row_perm(over_y(2), None)),
    )


def add_all(kept, heard):
    for term in heard:
        kept = kept + term.astype(jnp.float32)
    return kept


FIRST, SECOND, CORE, AT_X = 0, 6, 10, 11


def table_rows():
    piece = lambda y_at, x_at: (y_at % NY) * NX + x_at
    rows = []
    for y in range(NY):
        for x in range(NX):
            other = 1 - x
            pair1 = [piece(y, other), piece(y + 1, other)]
            pair2 = [piece(y - 1, other), piece(y + 2, other)]
            if other == 1:
                pair1, pair2 = pair1[::-1], pair2[::-1]
            here = piece(y, x)
            first0 = pair1 + pair2 + [here, here]
            second0 = [piece(y + 1, x), piece(y - 1, x), piece(y + 2, x), here]
            first1 = [piece(y + step, x_at) for step in (1, -1, 2) for x_at in (0, 1)]
            second1 = [piece(y, other), here, here, here]
            rows.append(first0 + second0 + [0, x])
            rows.append(first1 + second1 + [1, x])
    return rows


def col_sum(total):
    blocks = total.reshape(NY, NX, NC, PIECE, total.shape[1])
    away = blocks[:, :, 1].astype(jnp.bfloat16)
    heard = lax.ppermute(away, "col", col_perm(1, 0))
    near = blocks[:, :, 0] + heard.astype(jnp.float32)
    result = near[0]
    send = near[1:].astype(jnp.bfloat16)
    for step in range(1, NZ):
        result = result + lax.ppermute(send[step - 1], "col", col_perm(0, step)).astype(jnp.float32)
    return result.astype(jnp.bfloat16).reshape(NX * PIECE, total.shape[1])


def body(tokens, gate_weight, up_weight, down_weight, grad_output):
    row = lax.axis_index("row")
    table = lax.dynamic_index_in_dim(jnp.array(table_rows(), jnp.int32), row, 0, keepdims=False)
    core = table[CORE]
    flip = lambda value: lax.ppermute(value, "row", CORE_FLIP)
    after = lambda value, *others: lax.optimization_barrier((value, *others))[0]
    width = tokens.shape[1]

    def gather(block, steps):
        return [lax.ppermute(block, BOTH, gather_perm(step)) for step in steps]

    tok_block = jnp.concatenate([tokens, flip(tokens)], axis=1)
    tok_blocks = gather(tok_block, range(NZ))
    gate_pair = (gate_weight, flip(after(gate_weight, tok_block)))
    up_pair = (up_weight, flip(after(up_weight, tok_blocks[1])))
    tok_half, *sent = first_stage(table, [tok_block, *tok_blocks], [gate_pair, up_pair], False)
    heard = send_first(sent)

    grad_own, down_own, _ = lax.optimization_barrier((grad_output, down_weight, sent[0]))
    grad_block = jnp.concatenate([grad_own, flip(grad_own)], axis=1)
    grad_blocks = gather(grad_block, range(NZ))
    down_pair = (down_weight, flip(down_own))
    grad_half, *sent_d = first_stage(table, [grad_block, *grad_blocks], [down_pair], True)
    heard_d = send_first(sent_d)

    *sent, kept = second_stage(table, tok_half, [gate_pair, up_pair], False, heard)
    both = add_all(kept, send_second(sent))
    gate_value, up_value = both[0], both[1]
    sig_gate = jax.nn.sigmoid(gate_value)
    hidden = (gate_value * sig_gate * up_value).astype(jnp.bfloat16)
    hidden, gate_value, up_value, sig_gate = lax.optimization_barrier(
        (hidden, gate_value, up_value, sig_gate)
    )
    hidden = lax.all_gather(hidden, "row", axis=0, tiled=True)

    *sent_d, kept_d = second_stage(table, grad_half, [down_pair], True, heard_d)
    d_hidden = add_all(kept_d, send_second(sent_d))[0]
    d_gate = (d_hidden * up_value * sig_gate * (1.0 + gate_value * (1.0 - sig_gate))).astype(
        jnp.bfloat16
    )
    d_up = (d_hidden * gate_value * sig_gate).astype(jnp.bfloat16)
    d_both = lax.all_gather(jnp.concatenate([d_gate, d_up], axis=1), "row", axis=0, tiled=True)
    ff_width = gate_weight.shape[1]
    d_gate, d_up = d_both[:, :ff_width], d_both[:, ff_width:]

    tok_half = tok_half.reshape(NY * NX, PIECE, 2 * width)
    grad_half = grad_half.reshape(NY * NX, PIECE, 2 * width)
    others = flip(jnp.stack([tok_half[:, :, width:], grad_half[:, :, width:]]))

    def all_rows(half, received):
        own = half[:, :, :width]
        pair = jnp.where(
            core == 0, jnp.stack([own, received], axis=1), jnp.stack([received, own], axis=1)
        )
        return pair.reshape(-1, width)

    tok_all, grad_all = all_rows(tok_half, others[0]), all_rows(grad_half, others[1])

    layer_output = col_sum(jnp.dot(hidden, down_weight, preferred_element_type=jnp.float32))
    last = (((1,), (1,)), ((), ()))
    first = (((0,), (0,)), ((), ()))
    dot = functools.partial(lax.dot_general, preferred_element_type=jnp.float32)
    grad_input = col_sum(dot(d_gate, gate_weight, last) + dot(d_up, up_weight, last))
    grad_down = dot(hidden, grad_all, first).astype(jnp.bfloat16)
    grad_gate = dot(tok_all, d_gate, first).astype(jnp.bfloat16)
    grad_up = dot(tok_all, d_up, first).astype(jnp.bfloat16)
    return (layer_output, grad_input, grad_gate, grad_up, grad_down)


def solution(mesh):
    placed = (P("col", "row"), P("row", "col"), P("row", "col"), P("col", "row"), P("col", "row"))
    return jax.shard_map(
        body,
        mesh=mesh,
        in_specs=placed,
        out_specs=(
            P("col", "row"),
            P("col", "row"),
            P("row", "col"),
            P("row", "col"),
            P("col", "row"),
        ),
        check_vma=False,
    )
```

```python
import functools

import jax
import jax.numpy as jnp
from jax import lax
from jax.experimental import pallas as pl
from jax.experimental.pallas import tpu as pltpu
from jax.sharding import PartitionSpec as P

NY, NX, NC, NZ = 4, 2, 2, 4
PIECE = 64
BOTH = ("row", "col")


def row_at(y, x, core):
    return ((y % NY) * NX + x) * NC + core


def row_perm(core0, core1):
    pairs = []
    for y in range(NY):
        for x in range(NX):
            for core, move in ((0, core0), (1, core1)):
                if move is not None:
                    to_y, to_x = move(y, x)
                    pairs.append((row_at(y, x, core), row_at(to_y, to_x, core)))
    return pairs


def over_x(y, x):
    return y, 1 - x


def over_y(step):
    return lambda y, x: (y + step, x)


CORE_FLIP = [(i, i ^ 1) for i in range(NY * NX * NC)]


def gather_perm(step):
    pairs = []
    for row in range(NY * NX * NC):
        core = row % NC
        if core == 0 and step == 0:
            continue
        for hi in range(2):
            for z in range(NZ):
                source = (hi ^ core) * NZ + (z + step) % NZ
                pairs.append((row * 8 + source, row * 8 + hi * NZ + z))
    return pairs


def scatter_perm(step):
    return [(to, source) for source, to in gather_perm(step)]


def place_rows():
    return [
        [(hi ^ cc) * NZ + (z + k) % NZ for cc in range(NC) for k in range(NZ)]
        for hi in range(2)
        for z in range(NZ)
    ]


def col_perm(flip, step):
    return [(hi * NZ + z, (hi ^ flip) * NZ + (z + step) % NZ) for hi in range(2) for z in range(NZ)]


def product(left, right, transposed):
    dims = (((1,), (1 if transposed else 0,)), ((), ()))
    return lax.dot_general(left, right, dims, preferred_element_type=jnp.float32)


def spans(width):
    return [(at, min(at + 256, width)) for at in range(0, width, 256)]


class Fetch:
    def __init__(self, source, target, sems, chunks=None, first_sem=0):
        self.target, self.waiting = target, {}
        for i, chunk in enumerate(chunks or [slice(None)]):
            sem = sems.at[first_sem + i]
            copy = pltpu.make_async_copy(source.at[chunk], target.at[chunk], sem)
            copy.start()
            self.waiting[str(chunk)] = copy

    def get(self, chunk=slice(None)):
        copy = self.waiting.pop(str(chunk), None)
        if copy is not None:
            copy.wait()
        return self.target


def weight_chunk(at, end, transposed):
    return (slice(at, end), slice(None)) if transposed else (slice(None), slice(at, end))


def pair_product(held, pair, at, end, transposed):
    half = held.shape[1] // 2
    chunk = weight_chunk(at, end, transposed)
    own, other = [fetch.get(chunk)[chunk] for fetch in pair]
    return product(held[:, :half], own, transposed) + product(held[:, half:], other, transposed)


def fetch_all(refs, buffers, sems):
    return [Fetch(*three) for three in zip(refs, buffers, sems)]


def fetch_weights(refs, buffers, sems, transposed):
    count = len(refs) - 1
    width = refs[0].shape[0 if transposed else 1]
    chunks = [weight_chunk(at, end, transposed) for at, end in spans(width)]
    result = []
    for i in range(count):
        result.append(Fetch(refs[i], buffers[i], sems[i], chunks))
        other, to = refs[count].at[i], buffers[count].at[i]
        result.append(Fetch(other, to, sems[count], chunks, i * len(chunks)))
    return result


def weight_copies(weights, transposed):
    steps = len(spans(weights[0].shape[0 if transposed else 1]))
    return [steps] * (len(weights) - 1) + [steps * (len(weights) - 1)]


def fill_tokens(table, blocks, acts):
    blocks = [block.get() for block in blocks]
    rows = blocks[0].shape[0]
    acts[:rows] = jnp.where(table[CORE] == 0, blocks[0][...], blocks[1][...])
    for k in range(1, NZ):
        acts[k * rows : (k + 1) * rows] = blocks[k + 1][...]


def fill_halves(table, halves, acts):
    width = halves[0].target.shape[1]
    acts[:, :width] = halves[0].get()[...]
    acts[:, width:] = halves[1].get()[...]


def first_kernel(count, transposed, fill, sources, table, *refs):
    n = sources + count + 1
    ins, (acts, *outs), (held, *more) = refs[:n], refs[n : n + 4], refs[n + 4 :]
    buffers, sems = more[:n], more[n:]
    blocks = fetch_all(ins[:sources], buffers, sems)
    weights = fetch_weights(ins[sources:], buffers[sources:], sems[sources:], transposed)
    fill(table, blocks, acts)
    for slot in range(6):
        start = pl.multiple_of(table[FIRST + slot] * PIECE, PIECE)
        held[slot * PIECE : (slot + 1) * PIECE, :] = acts[pl.ds(start, PIECE), :]
    for at, end in spans(outs[0].shape[2]):
        for which in range(count):
            pair = weights[2 * which : 2 * which + 2]
            total = pair_product(held, pair, at, end, transposed).astype(jnp.bfloat16)
            for message in range(3):
                outs[message][which, :, at:end] = total[
                    message * 2 * PIECE : (message + 1) * 2 * PIECE
                ]


def second_kernel(count, transposed, table, *refs):
    n = 1 + count + 1 + 3
    ins, outs, (held, *more) = refs[:n], refs[n : n + 4], refs[n + 4 :]
    buffers, sems = more[:n], more[n:]
    (acts,) = fetch_all(ins[:1], buffers, sems)
    weights = fetch_weights(ins[1:-3], buffers[1:-3], sems[1:-3], transposed)
    heard = fetch_all(ins[-3:], buffers[-3:], sems[-3:])
    core, x = table[CORE], table[AT_X]
    rows = acts.get()
    for slot in range(4):
        start = pl.multiple_of(table[SECOND + slot] * PIECE, PIECE)
        held[slot * PIECE : (slot + 1) * PIECE, :] = rows[pl.ds(start, PIECE), :]
    near = pl.ds(pl.multiple_of(x * PIECE, PIECE), PIECE)
    far = pl.ds(pl.multiple_of((1 - x) * PIECE, PIECE), PIECE)
    for at, end in spans(outs[0].shape[2]):
        for which in range(count):
            pair = weights[2 * which : 2 * which + 2]
            total = pair_product(held, pair, at, end, transposed)
            terms = [h.get() for h in heard]
            near1, near2, near3 = [h[which, near, at:end].astype(jnp.float32) for h in terms]
            far1, far2, far3 = [h[which, far, at:end].astype(jnp.float32) for h in terms]
            sum1 = total[:PIECE] + far1 + jnp.where(core == 1, far2 + far3, 0.0)
            high = sum1.astype(jnp.bfloat16)
            rest = sum1 - high.astype(jnp.float32)
            sum2 = jnp.where(core == 1, rest, total[PIECE : 2 * PIECE] + near2)
            outs[0][which, :, at:end] = high
            outs[1][which, :, at:end] = sum2.astype(jnp.bfloat16)
            outs[2][which, :, at:end] = (total[2 * PIECE : 3 * PIECE] + far2).astype(jnp.bfloat16)
            outs[3][which, :, at:end] = (
                total[3 * PIECE :] + near1 + jnp.where(core == 1, near2 + near3, 0.0)
            )


def join_kernel(first, second, both, sems):
    copies = [
        pltpu.make_async_copy(source, both.at[i], sems.at[i])
        for i, source in enumerate((first, second))
    ]
    for copy in copies:
        copy.start()
    for copy in copies:
        copy.wait()


def join(first, second):
    anywhere = pl.BlockSpec(memory_space=pl.ANY)
    return pl.pallas_call(
        join_kernel,
        in_specs=[anywhere] * 2,
        out_specs=anywhere,
        out_shape=shape((2, *first.shape)),
        scratch_shapes=[pltpu.SemaphoreType.DMA((2,))],
    )(first, second)


def order_kernel(table, place, every, full, own, other):
    block = NX * PIECE
    for k in range(NZ):
        for cc in range(NC):
            start = pl.multiple_of(place[cc * NZ + k] * block, block)
            for x in range(NX):
                at = ((k * NX + x) * NC + cc) * PIECE
                full[at : at + PIECE] = every[pl.ds(start + x * PIECE, PIECE), :]
        mine = pl.multiple_of(place[table[CORE] * NZ + k] * block, block)
        theirs = pl.multiple_of(place[(1 - table[CORE]) * NZ + k] * block, block)
        own[k * block : (k + 1) * block] = every[pl.ds(mine, block), :]
        other[k * block : (k + 1) * block] = every[pl.ds(theirs, block), :]


def hidden_kernel(kept, heard1, heard2, heard3, hidden, gate, up):
    for which, out in ((0, gate), (1, up)):
        out[...] = kept[which] + sum(
            h[which].astype(jnp.float32) for h in (heard1, heard2, heard3)
        )
    gate_value = gate[...]
    hidden[...] = (gate_value * jax.nn.sigmoid(gate_value) * up[...]).astype(jnp.bfloat16)


def derivative_kernel(kept, heard1, heard2, heard3, gate, up, both):
    d_hidden = kept[0] + sum(h[0].astype(jnp.float32) for h in (heard1, heard2, heard3))
    gate_value = gate[...]
    sig_gate = jax.nn.sigmoid(gate_value)
    slope = d_hidden * up[...] * sig_gate * (1.0 + gate_value * (1.0 - sig_gate))
    both[0] = slope.astype(jnp.bfloat16)
    both[1] = (d_hidden * gate_value * sig_gate).astype(jnp.bfloat16)


def pack_kernel(table, own, near1, near2, near3, first, second):
    core0 = table[CORE] == 0
    first[:, :PIECE] = own[...]
    first[:, PIECE:] = near1[...]
    second[:, :PIECE] = jnp.where(core0, near2[...], own[...])
    second[:, PIECE:] = jnp.where(core0, near3[...], near1[...])


def input_kernel(table, *refs):
    n = 10
    ins, outs, more = refs[:n], refs[n : n + 6], refs[n + 6 :]
    buffers, sems = more[:n], more[n:]
    moved = fetch_all(ins[:7], buffers, sems)
    weights = fetch_weights(ins[7:], buffers[7:], sems[7:], True)
    own, near1, near2, near3, far1, far2, far3 = [fetch.get() for fetch in moved]
    d_set, messages, kept = outs[0], outs[1:5], outs[5]

    def put(slot, value):
        start = pl.multiple_of(table[GATHER + slot] * PIECE, PIECE)
        d_set[:, pl.ds(start, PIECE), :] = value

    put(0, own[...])
    put(1, near1[...])
    put(2, far1[:, :PIECE])
    put(3, far1[:, PIECE:])
    put(4, far2[:, :PIECE])
    put(5, far2[:, PIECE:])
    core0 = table[CORE] == 0
    put(6, jnp.where(core0, near2[...], far3[:, :PIECE]))
    put(7, jnp.where(core0, near3[...], far3[:, PIECE:]))
    depth = weights[0].target.shape[0]
    block = NX * PIECE
    for side in range(2):
        for at, end in spans(depth):
            chunk = weight_chunk(at, end, True)
            gate, up = [weights[side + i].get(chunk)[chunk] for i in (0, 2)]
            total = product(d_set[0], gate, True) + product(d_set[1], up, True)
            columns = slice(side * depth + at, side * depth + end)
            kept[:, columns] = total[:block]
            for k in range(NZ):
                messages[k][:, columns] = total[k * block : (k + 1) * block].astype(jnp.bfloat16)


def call(kernel, tables, operands, out_shape, scratch=(), flops=0, fetched=None):
    vmem = pl.BlockSpec(memory_space=pltpu.VMEM)
    smem = pl.BlockSpec(memory_space=pltpu.SMEM)
    moved = sum(o.size * o.dtype.itemsize for o in [*operands, *out_shape])
    place = vmem
    if fetched is not None:
        place = pl.BlockSpec(memory_space=pltpu.HBM)
        scratch = [
            *scratch,
            *[pltpu.VMEM(o.shape, o.dtype) for o in operands],
            *[pltpu.SemaphoreType.DMA((n,)) for n in fetched],
        ]
    return pl.pallas_call(
        kernel,
        in_specs=[smem] * len(tables) + [place] * len(operands),
        out_specs=[vmem] * len(out_shape),
        out_shape=out_shape,
        scratch_shapes=scratch,
        compiler_params=pltpu.CompilerParams(vmem_limit_bytes=36 * 2**20),
        cost_estimate=pl.CostEstimate(flops=flops, bytes_accessed=moved, transcendentals=0),
    )(*tables, *operands)


def shape(dims, dtype=jnp.bfloat16):
    return jax.ShapeDtypeStruct(dims, dtype)


def first_stage(table, fill, sources, weights, transposed):
    count = len(weights) - 1
    width, depth = weights[0].shape[:: -1 if not transposed else 1]
    message = shape((count, 2 * PIECE, width))
    return call(
        functools.partial(first_kernel, count, transposed, fill, len(sources)),
        [table],
        [*sources, *weights],
        [shape((NY * NX * PIECE, 2 * depth))] + [message] * 3,
        [pltpu.VMEM((6 * PIECE, 2 * depth), jnp.bfloat16)],
        2 * 6 * PIECE * 2 * depth * width * count,
        [1] * len(sources) + weight_copies(weights, transposed),
    )


def second_stage(table, acts, weights, transposed, heard):
    count = len(weights) - 1
    width, depth = weights[0].shape[:: -1 if not transposed else 1]
    message = shape((count, PIECE, width))
    return call(
        functools.partial(second_kernel, count, transposed),
        [table],
        [acts, *weights, *heard],
        [message] * 3 + [shape((count, PIECE, width), jnp.float32)],
        [pltpu.VMEM((4 * PIECE, 2 * depth), jnp.bfloat16)],
        2 * 4 * PIECE * 2 * depth * width * count,
        [1] + weight_copies(weights, transposed) + [1] * 3,
    )


def send_first(sent):
    return (
        lax.ppermute(sent[0], "row", row_perm(over_x, over_y(1))),
        lax.ppermute(sent[1], "row", row_perm(over_x, over_y(-1))),
        lax.ppermute(sent[2], "row", row_perm(None, over_y(2))),
    )


def send_second(sent):
    return (
        lax.ppermute(sent[0], "row", row_perm(over_y(1), over_x)),
        lax.ppermute(sent[1], "row", row_perm(over_y(-1), over_x)),
        lax.ppermute(sent[2], "row", row_perm(over_y(2), None)),
    )


FIRST, SECOND, CORE, AT_X, GATHER = 0, 6, 10, 11, 12


def table_rows():
    piece = lambda y_at, x_at: (y_at % NY) * NX + x_at
    rows = []
    for y in range(NY):
        for x in range(NX):
            other = 1 - x
            pair1 = [piece(y, other), piece(y + 1, other)]
            pair2 = [piece(y - 1, other), piece(y + 2, other)]
            if other == 1:
                pair1, pair2 = pair1[::-1], pair2[::-1]
            here = piece(y, x)
            first0 = pair1 + pair2 + [here, here]
            second0 = [piece(y + 1, x), piece(y - 1, x), piece(y + 2, x), here]
            first1 = [piece(y + step, x_at) for step in (1, -1, 2) for x_at in (0, 1)]
            second1 = [piece(y, other), here, here, here]
            gather0 = [here, piece(y - 1, x), piece(y, other), piece(y - 1, other)]
            gather0 += [piece(y + 1, other), piece(y + 2, other), piece(y + 1, x), piece(y + 2, x)]
            gather1 = [here, piece(y, other)]
            gather1 += [piece(y + step, x_at) for step in (-1, 1, 2) for x_at in (x, other)]
            rows.append(first0 + second0 + [0, x] + gather0)
            rows.append(first1 + second1 + [1, x] + gather1)
    return rows


def col_first(total):
    blocks = total.reshape(NY, NX, NC, PIECE, total.shape[1])
    heard = lax.ppermute(blocks[:, :, 1].astype(jnp.bfloat16), "col", col_perm(1, 0))
    near = blocks[:, :, 0] + heard.astype(jnp.float32)
    return near[0], near[1:].astype(jnp.bfloat16)


def col_second(result, send):
    for step in range(1, NZ):
        result = result + lax.ppermute(send[step - 1], "col", col_perm(0, step)).astype(jnp.float32)
    return result.astype(jnp.bfloat16).reshape(NX * PIECE, result.shape[-1])


def body(tokens, gate_weight, up_weight, down_weight, grad_output):
    pick = lambda rows, axis: lax.dynamic_index_in_dim(
        jnp.array(rows, jnp.int32), lax.axis_index(axis), 0, keepdims=False
    )
    table, place = pick(table_rows(), "row"), pick(place_rows(), "col")
    core = table[CORE]
    flip = lambda value: lax.ppermute(value, "row", CORE_FLIP)
    after = lambda value, *others: lax.optimization_barrier((value, *others))[0]
    width, ff_width = gate_weight.shape
    half_rows = NY * NX * PIECE

    grad_every = lax.all_gather(grad_output, "col", axis=0, tiled=True)
    others = flip(join(gate_weight, up_weight))
    tok_block = jnp.concatenate([tokens, flip(tokens)], axis=1)
    tok_blocks = [lax.ppermute(tok_block, BOTH, gather_perm(step)) for step in (0, 1, 2, 3)]
    both_weights = [gate_weight, up_weight, others]
    tok_half, *sent = first_stage(
        table, fill_tokens, [tok_block, *tok_blocks], both_weights, False
    )
    heard = send_first(sent)
    down_own, _ = lax.optimization_barrier((down_weight, sent[0]))
    down_weights = [down_weight, flip(down_own)[None]]

    *sent, kept = second_stage(table, tok_half, both_weights, False, heard)
    heard = send_second(sent)
    grad_all, grad_own, grad_other = call(
        order_kernel,
        [table, place],
        [after(grad_every, sent[0])],
        [shape(grad_every.shape), shape((half_rows, width)), shape((half_rows, width))],
    )
    grad_half, *sent_d = first_stage(
        table, fill_halves, [grad_own, flip(grad_other)], down_weights, True
    )
    heard_d = send_first(sent_d)
    *heard, _ = lax.optimization_barrier((*heard, sent_d[0]))
    hidden, gate_value, up_value = call(
        hidden_kernel,
        [],
        [kept, *heard],
        [shape((PIECE, ff_width))] + [shape((PIECE, ff_width), jnp.float32)] * 2,
    )
    hidden = lax.all_gather(hidden, "row", axis=0, tiled=True)

    *sent_d, kept_d = second_stage(table, grad_half, down_weights, True, heard_d)
    piece = shape((2, PIECE, ff_width))
    (d_own,) = call(
        derivative_kernel, [], [kept_d, *send_second(sent_d), gate_value, up_value], [piece]
    )

    near = send_second([d_own] * 3)
    first, second = call(
        pack_kernel, [table], [d_own, *near], [shape((2, 2 * PIECE, ff_width))] * 2
    )
    far = send_first([first, second, first])
    dot = functools.partial(lax.dot_general, preferred_element_type=jnp.float32)
    contract_first = (((0,), (0,)), ((), ()))
    near_sum, near_send = col_first(
        jnp.dot(hidden, down_weight, preferred_element_type=jnp.float32)
    )
    tok_own, tok_other = tok_half[:, :width], flip(tok_half[:, width:])
    *far, near_send, tok_other = lax.optimization_barrier((*far, near_send, tok_other))
    block = shape((NX * PIECE, 2 * width))
    d_set, *messages, kept = call(
        input_kernel,
        [table],
        [d_own, *near, *far, *both_weights],
        [shape((2, half_rows, ff_width))] + [block] * 4 + [shape(block.shape, jnp.float32)],
        flops=2 * half_rows * 2 * width * 2 * ff_width,
        fetched=[1] * 7 + weight_copies(both_weights, True),
    )
    total = jnp.where(core == 0, kept, 0.0)
    for step in range(NZ):
        message = lax.ppermute(messages[step], BOTH, scatter_perm(step))
        total = total + message.astype(jnp.float32)
    grad_input = (total[:, :width] + flip(total[:, width:])).astype(jnp.bfloat16)
    layer_output = col_second(near_sum, after(near_send, messages[0]))

    grad_down = dot(hidden, grad_all, contract_first).astype(jnp.bfloat16)
    d_other = flip(d_set)

    def weight_gradient(which):
        total = dot(tok_own, d_set[which], contract_first)
        return (total + dot(tok_other, d_other[which], contract_first)).astype(jnp.bfloat16)

    return (layer_output, grad_input, weight_gradient(0), weight_gradient(1), grad_down)


def solution(mesh):
    placed = (P("col", "row"), P("row", "col"), P("row", "col"), P("col", "row"), P("col", "row"))
    return jax.shard_map(
        body,
        mesh=mesh,
        in_specs=placed,
        out_specs=(
            P("col", "row"),
            P("col", "row"),
            P("row", "col"),
            P("row", "col"),
            P("col", "row"),
        ),
        check_vma=False,
    )
```

```python
import functools

import jax
import jax.numpy as jnp
from jax import lax
from jax.experimental import pallas as pl
from jax.experimental.pallas import tpu as pltpu
from jax.sharding import PartitionSpec as P

NY, NX, NC, NZ = 4, 2, 2, 4
PIECE = 64
BOTH = ("row", "col")


def row_at(y, x, core):
    return ((y % NY) * NX + x) * NC + core


def row_perm(core0, core1):
    pairs = []
    for y in range(NY):
        for x in range(NX):
            for core, move in ((0, core0), (1, core1)):
                if move is not None:
                    to_y, to_x = move(y, x)
                    pairs.append((row_at(y, x, core), row_at(to_y, to_x, core)))
    return pairs


def over_x(y, x):
    return y, 1 - x


def over_y(step):
    return lambda y, x: (y + step, x)


CORE_FLIP = [(i, i ^ 1) for i in range(NY * NX * NC)]


def gather_perm(step):
    pairs = []
    for row in range(NY * NX * NC):
        core = row % NC
        if core == 0 and step == 0:
            continue
        for hi in range(2):
            for z in range(NZ):
                source = (hi ^ core) * NZ + (z + step) % NZ
                pairs.append((row * 8 + source, row * 8 + hi * NZ + z))
    return pairs


def scatter_perm(step):
    return [(to, source) for source, to in gather_perm(step)]


def col_perm(flip, step):
    return [(hi * NZ + z, (hi ^ flip) * NZ + (z + step) % NZ) for hi in range(2) for z in range(NZ)]


def product(left, right, transposed):
    dims = (((1,), (1 if transposed else 0,)), ((), ()))
    return lax.dot_general(left, right, dims, preferred_element_type=jnp.float32)


def spans(width):
    return [(at, min(at + 256, width)) for at in range(0, width, 256)]


class Load:
    def __init__(self, source, target, sem):
        self.target, self.copy = target, pltpu.make_async_copy(source, target, sem)
        self.copy.start()

    def get(self):
        if self.copy is not None:
            self.copy.wait()
            self.copy = None
        return self.target


class Store:
    def __init__(self, source, target, sem):
        self.ref, self.copy, self.sent = source, pltpu.make_async_copy(source, target, sem), False

    def send(self):
        self.copy.start()
        self.sent = True


class OfOther:
    def __init__(self, value):
        self.value = value


def call(kernel, tables, operands, out_shape, scratch=()):
    parts = [shape(o.value.shape[1:]) if isinstance(o, OfOther) else o for o in operands]
    operands = [o.value if isinstance(o, OfOther) else o for o in operands]
    any_space = pl.BlockSpec(memory_space=pl.ANY)
    smem = pl.BlockSpec(memory_space=pltpu.SMEM)
    n_tables, n_in, n_out, n_own = len(tables), len(operands), len(out_shape), len(scratch)

    def run(*refs):
        refs = list(refs)
        take = lambda count: [refs.pop(0) for _ in range(count)]
        table_refs, ins, outs, own = take(n_tables), take(n_in), take(n_out), take(n_own)
        in_buffers, out_buffers, (in_sems, out_sems) = take(n_in), take(n_out), take(2)
        ins = [
            ref.at[1 - table_refs[0][CORE]] if len(ref.shape) > len(to.shape) else ref
            for ref, to in zip(ins, in_buffers)
        ]
        loads = [Load(ins[i], in_buffers[i], in_sems.at[i]) for i in range(n_in)]
        stores = [Store(out_buffers[i], outs[i], out_sems.at[i]) for i in range(n_out)]
        kernel(table_refs, loads, stores, *own)
        for load in loads:
            load.get()
        for store in stores:
            if not store.sent:
                store.send()
        for store in stores:
            store.copy.wait()

    return pl.pallas_call(
        run,
        in_specs=[smem] * n_tables + [any_space] * n_in,
        out_specs=[any_space] * n_out,
        out_shape=out_shape,
        scratch_shapes=[
            *scratch,
            *[pltpu.VMEM(o.shape, o.dtype) for o in [*parts, *out_shape]],
            pltpu.SemaphoreType.DMA((n_in,)),
            pltpu.SemaphoreType.DMA((n_out,)),
        ],
        compiler_params=pltpu.CompilerParams(vmem_limit_bytes=56 * 2**20),
        cost_estimate=pl.CostEstimate(flops=1, bytes_accessed=1, transcendentals=0),
    )(*tables, *operands)


def pair_product(held, pair, at, end, transposed):
    half = held.shape[1] // 2
    chunk = (slice(at, end), slice(None)) if transposed else (slice(None), slice(at, end))
    own, other = [load.get()[chunk] for load in pair]
    return product(held[:, :half], own, transposed) + product(held[:, half:], other, transposed)


def first_kernel(tables, loads, stores, tok_held, grad_held):
    (table,) = tables
    block, *blocks = [load.get() for load in loads[:-6]]
    weights, messages, halves = loads[-6:], stores[2:], [store.ref for store in stores[:2]]
    rows = block.shape[1]
    for i, (acts, held) in enumerate(zip(halves, (tok_held, grad_held))):
        acts[:rows] = jnp.where(table[CORE] == 0, block[i], blocks[0][i])
        for k in range(1, NZ):
            acts[k * rows : (k + 1) * rows] = blocks[k][i]
        stores[i].send()
        for slot in range(6):
            start = pl.multiple_of(table[FIRST + slot] * PIECE, PIECE)
            held[slot * PIECE : (slot + 1) * PIECE, :] = acts[pl.ds(start, PIECE), :]
    for which in range(3):
        held, transposed = ((tok_held, False), (grad_held, True))[which // 2]
        pair = weights[2 * which : 2 * which + 2]
        for at, end in spans(messages[0].ref.shape[2]):
            total = pair_product(held, pair, at, end, transposed).astype(jnp.bfloat16)
            for i, message in enumerate(messages):
                message.ref[which, :, at:end] = total[i * 2 * PIECE : (i + 1) * 2 * PIECE]


def second_kernel(tables, loads, stores, tok_held, grad_held):
    (table,) = tables
    weights, heard = loads[2:8], loads[8:]
    outs = [store.ref for store in stores]
    core, x = table[CORE], table[AT_X]
    near = pl.ds(pl.multiple_of(x * PIECE, PIECE), PIECE)
    far = pl.ds(pl.multiple_of((1 - x) * PIECE, PIECE), PIECE)
    for acts, held in zip(loads[:2], (tok_held, grad_held)):
        rows = acts.get()
        for slot in range(4):
            start = pl.multiple_of(table[SECOND + slot] * PIECE, PIECE)
            held[slot * PIECE : (slot + 1) * PIECE, :] = rows[pl.ds(start, PIECE), :]
    for which in range(3):
        held, transposed = ((tok_held, False), (grad_held, True))[which // 2]
        pair = weights[2 * which : 2 * which + 2]
        for at, end in spans(outs[0].shape[2]):
            total = pair_product(held, pair, at, end, transposed)
            terms = [h.get() for h in heard]
            near1, near2, near3 = [h[which, near, at:end].astype(jnp.float32) for h in terms]
            far1, far2, far3 = [h[which, far, at:end].astype(jnp.float32) for h in terms]
            sum1 = total[:PIECE] + far1 + jnp.where(core == 1, far2 + far3, 0.0)
            high = sum1.astype(jnp.bfloat16)
            rest = sum1 - high.astype(jnp.float32)
            sum2 = jnp.where(core == 1, rest, total[PIECE : 2 * PIECE] + near2)
            outs[0][which, :, at:end] = high
            outs[1][which, :, at:end] = sum2.astype(jnp.bfloat16)
            outs[2][which, :, at:end] = (total[2 * PIECE : 3 * PIECE] + far2).astype(jnp.bfloat16)
            outs[3][which, :, at:end] = (
                total[3 * PIECE :] + near1 + jnp.where(core == 1, near2 + near3, 0.0)
            )


def weave_kernel(tables, loads, stores):
    core = tables[0][CORE]
    full = stores[0].ref
    for load, at_core in zip(loads, (core, 1 - core)):
        rows = load.get()
        for piece in range(NY * NX):
            start = pl.multiple_of((piece * NC + at_core) * PIECE, PIECE)
            full[pl.ds(start, PIECE), :] = rows[piece * PIECE : (piece + 1) * PIECE, :]


def unit_kernel(tables, loads, stores):
    kept, *heard = [load.get() for load in loads]
    gate, up, d_hidden = [
        kept[which] + sum(h[which].astype(jnp.float32) for h in heard) for which in range(3)
    ]
    sig_gate = jax.nn.sigmoid(gate)
    hidden, both = [store.ref for store in stores]
    hidden[...] = (gate * sig_gate * up).astype(jnp.bfloat16)
    slope = d_hidden * up * sig_gate * (1.0 + gate * (1.0 - sig_gate))
    both[0] = slope.astype(jnp.bfloat16)
    both[1] = (d_hidden * gate * sig_gate).astype(jnp.bfloat16)


def pack_kernel(tables, loads, stores):
    own, near1, near2, near3 = [load.get() for load in loads]
    first, second = [store.ref for store in stores]
    core0 = tables[0][CORE] == 0
    first[:, :PIECE] = own[...]
    first[:, PIECE:] = near1[...]
    stores[0].send()
    second[:, :PIECE] = jnp.where(core0, near2[...], own[...])
    second[:, PIECE:] = jnp.where(core0, near3[...], near1[...])


def input_kernel(tables, loads, stores):
    (table,) = tables
    own, near1, near2, near3, far1, far2, far3 = [load.get() for load in loads[:7]]
    weights = loads[7:]
    *messages, d_set, kept = [store.ref for store in stores]

    def put(slot, value):
        start = pl.multiple_of(table[GATHER + slot] * PIECE, PIECE)
        d_set[:, pl.ds(start, PIECE), :] = value

    put(0, own[...])
    put(1, near1[...])
    put(2, far1[:, :PIECE])
    put(3, far1[:, PIECE:])
    put(4, far2[:, :PIECE])
    put(5, far2[:, PIECE:])
    core0 = table[CORE] == 0
    put(6, jnp.where(core0, near2[...], far3[:, :PIECE]))
    put(7, jnp.where(core0, near3[...], far3[:, PIECE:]))
    stores[NZ].send()
    depth = weights[0].target.shape[0]
    block = NX * PIECE
    for side in range(2):
        for at, end in spans(depth):
            gate, up = [weights[2 * side + i].get()[at:end, :] for i in range(2)]
            total = product(d_set[0], gate, True) + product(d_set[1], up, True)
            columns = slice(side * depth + at, side * depth + end)
            kept[:, columns] = total[:block]
            for k in range(NZ):
                messages[k][:, columns] = total[k * block : (k + 1) * block].astype(jnp.bfloat16)


def shape(dims, dtype=jnp.bfloat16):
    return jax.ShapeDtypeStruct(dims, dtype)


def first_stage(table, blocks, weights):
    depth, width = weights[0].shape
    rows = shape((NY * NX * PIECE, 2 * depth))
    return call(
        first_kernel,
        [table],
        [*blocks, *weights],
        [rows] * 2 + [shape((3, 2 * PIECE, width))] * 3,
        [pltpu.VMEM((6 * PIECE, 2 * depth), jnp.bfloat16)] * 2,
    )


def second_stage(table, tok_half, grad_half, weights, heard):
    width, depth = weights[0].shape[1], weights[0].shape[0]
    message = shape((3, PIECE, width))
    return call(
        second_kernel,
        [table],
        [tok_half, grad_half, *weights, *heard],
        [message] * 3 + [shape(message.shape, jnp.float32)],
        [pltpu.VMEM((4 * PIECE, 2 * depth), jnp.bfloat16)] * 2,
    )


def send_first(sent):
    return (
        lax.ppermute(sent[0], "row", row_perm(over_x, over_y(1))),
        lax.ppermute(sent[1], "row", row_perm(over_x, over_y(-1))),
        lax.ppermute(sent[2], "row", row_perm(None, over_y(2))),
    )


def send_second(sent):
    return (
        lax.ppermute(sent[0], "row", row_perm(over_y(1), over_x)),
        lax.ppermute(sent[1], "row", row_perm(over_y(-1), over_x)),
        lax.ppermute(sent[2], "row", row_perm(over_y(2), None)),
    )


FIRST, SECOND, CORE, AT_X, GATHER = 0, 6, 10, 11, 12


def table_rows():
    piece = lambda y_at, x_at: (y_at % NY) * NX + x_at
    rows = []
    for y in range(NY):
        for x in range(NX):
            other = 1 - x
            pair1 = [piece(y, other), piece(y + 1, other)]
            pair2 = [piece(y - 1, other), piece(y + 2, other)]
            if other == 1:
                pair1, pair2 = pair1[::-1], pair2[::-1]
            here = piece(y, x)
            first0 = pair1 + pair2 + [here, here]
            second0 = [piece(y + 1, x), piece(y - 1, x), piece(y + 2, x), here]
            first1 = [piece(y + step, x_at) for step in (1, -1, 2) for x_at in (0, 1)]
            second1 = [piece(y, other), here, here, here]
            gather0 = [here, piece(y - 1, x), piece(y, other), piece(y - 1, other)]
            gather0 += [piece(y + 1, other), piece(y + 2, other), piece(y + 1, x), piece(y + 2, x)]
            gather1 = [here, piece(y, other)]
            gather1 += [piece(y + step, x_at) for step in (-1, 1, 2) for x_at in (x, other)]
            rows.append(first0 + second0 + [0, x] + gather0)
            rows.append(first1 + second1 + [1, x] + gather1)
    return rows


def col_blocks(total):
    blocks = total.reshape(NY, NX, NC, PIECE, total.shape[1])
    return blocks[0], blocks[1:].astype(jnp.bfloat16)


def col_first(near, send):
    for step in range(1, NZ):
        near = near + lax.ppermute(send[step - 1], "col", col_perm(0, step)).astype(jnp.float32)
    return near[:, 0], near[:, 1].astype(jnp.bfloat16)


def col_second(result, send):
    result = result + lax.ppermute(send, "col", col_perm(1, 0)).astype(jnp.float32)
    return result.astype(jnp.bfloat16).reshape(NX * PIECE, result.shape[-1])


def body(tokens, gate_weight, up_weight, down_weight, grad_output):
    table = lax.dynamic_index_in_dim(
        jnp.array(table_rows(), jnp.int32), lax.axis_index("row"), 0, keepdims=False
    )
    core = table[CORE]
    flip = lambda value: lax.ppermute(value, "row", CORE_FLIP)
    after = lambda value, *others: lax.optimization_barrier((value, *others))[0]
    width, ff_width = gate_weight.shape
    half_rows = NY * NX * PIECE

    pairs = [[i, i + 1] for i in range(0, NY * NX * NC, NC)]
    gate_other, up_other, down_other = [
        OfOther(lax.all_gather(weight, "row", axis_index_groups=pairs))
        for weight in (gate_weight, up_weight, down_weight)
    ]
    mine = jnp.stack([tokens, grad_output])
    own_block = jnp.concatenate([mine, flip(mine)], axis=2)
    blocks = [lax.ppermute(own_block, BOTH, gather_perm(step)) for step in range(NZ)]

    both_weights = [gate_weight, gate_other, up_weight, up_other]
    weights = [*both_weights, down_weight, down_other]
    tok_half, grad_half, *sent = first_stage(table, [own_block, *blocks], weights)
    heard = send_first(sent)
    halves = after(jnp.stack([tok_half[:, width:], grad_half[:, width:]]), sent[0])
    tok_other, grad_other = flip(halves)
    tok_own = tok_half[:, :width]
    (grad_all,) = call(
        weave_kernel,
        [table],
        [grad_half[:, :width], grad_other],
        [shape((2 * half_rows, width))],
    )
    *heard, grad_all, tok_other = lax.optimization_barrier((*heard, grad_all, tok_other))
    *sent, kept = second_stage(table, tok_half, grad_half, weights, heard)
    hidden, d_own = call(
        unit_kernel,
        [],
        [kept, *send_second(sent)],
        [shape((PIECE, ff_width)), shape((2, PIECE, ff_width))],
    )
    hidden = lax.all_gather(hidden, "row", axis=0, tiled=True)

    near = send_second([d_own] * 3)
    first, second = call(
        pack_kernel, [table], [d_own, *near], [shape((2, 2 * PIECE, ff_width))] * 2
    )
    far = send_first([first, second, first])
    block = shape((NX * PIECE, 2 * width))
    *messages, d_set, kept = call(
        input_kernel,
        [table],
        [d_own, *near, *far, gate_weight, up_weight, gate_other, up_other],
        [block] * 4 + [shape((2, half_rows, ff_width)), shape(block.shape, jnp.float32)],
    )
    hidden = after(hidden, kept)
    messages = [lax.ppermute(messages[k], BOTH, scatter_perm(k)) for k in range(NZ)]
    d_other = flip(d_set)
    dot = functools.partial(lax.dot_general, preferred_element_type=jnp.float32)
    contract_first = (((0,), (0,)), ((), ()))
    near_sum, send = col_blocks(jnp.dot(hidden, down_weight, preferred_element_type=jnp.float32))
    layer_output = col_second(*col_first(near_sum, send))
    grad_down = dot(hidden, grad_all, contract_first).astype(jnp.bfloat16)

    def weight_gradient(which):
        total = dot(tok_own, d_set[which], contract_first)
        return (total + dot(tok_other, d_other[which], contract_first)).astype(jnp.bfloat16)

    grad_gate, grad_up = weight_gradient(0), weight_gradient(1)
    *messages, grad_gate, grad_up = lax.optimization_barrier((*messages, grad_gate, grad_up))
    total = jnp.where(core == 0, kept, 0.0)
    for message in messages:
        total = total + message.astype(jnp.float32)
    grad_input = (total[:, :width] + flip(total[:, width:])).astype(jnp.bfloat16)
    return (layer_output, grad_input, grad_gate, grad_up, grad_down)


def solution(mesh):
    placed = (P("col", "row"), P("row", "col"), P("row", "col"), P("col", "row"), P("col", "row"))
    return jax.shard_map(
        body,
        mesh=mesh,
        in_specs=placed,
        out_specs=(
            P("col", "row"),
            P("col", "row"),
            P("row", "col"),
            P("row", "col"),
            P("col", "row"),
        ),
        check_vma=False,
    )
```

```python
import functools

import jax
import jax.numpy as jnp
from jax import lax
from jax.experimental import pallas as pl
from jax.experimental.pallas import tpu as pltpu
from jax.sharding import PartitionSpec as P

NY, NX, NC, NZ = 4, 2, 2, 4
PIECE = 64
BOTH = ("row", "col")


def row_at(y, x, core):
    return ((y % NY) * NX + x) * NC + core


def row_perm(core0, core1):
    pairs = []
    for y in range(NY):
        for x in range(NX):
            for core, move in ((0, core0), (1, core1)):
                if move is not None:
                    to_y, to_x = move(y, x)
                    pairs.append((row_at(y, x, core), row_at(to_y, to_x, core)))
    return pairs


def over_x(y, x):
    return y, 1 - x


def over_y(step):
    return lambda y, x: (y + step, x)


CORE_FLIP = [(i, i ^ 1) for i in range(NY * NX * NC)]


def gather_perm(step):
    pairs = []
    for row in range(NY * NX * NC):
        core = row % NC
        if core == 0 and step == 0:
            continue
        for hi in range(2):
            for z in range(NZ):
                source = (hi ^ core) * NZ + (z + step) % NZ
                pairs.append((row * 8 + source, row * 8 + hi * NZ + z))
    return pairs


def scatter_perm(step):
    return [(to, source) for source, to in gather_perm(step)]


def col_perm(flip, step):
    return [(hi * NZ + z, (hi ^ flip) * NZ + (z + step) % NZ) for hi in range(2) for z in range(NZ)]


def product(left, right, transposed):
    dims = (((1,), (1 if transposed else 0,)), ((), ()))
    return lax.dot_general(left, right, dims, preferred_element_type=jnp.float32)


def spans(width):
    return [(at, min(at + 256, width)) for at in range(0, width, 256)]


class Load:
    def __init__(self, source, target, sem):
        self.target, self.copy = target, pltpu.make_async_copy(source, target, sem)
        self.copy.start()

    def get(self):
        if self.copy is not None:
            self.copy.wait()
            self.copy = None
        return self.target


class Store:
    def __init__(self, source, target, sem):
        self.ref, self.copy, self.sent = source, pltpu.make_async_copy(source, target, sem), False

    def send(self):
        self.copy.start()
        self.sent = True


def call(kernel, tables, operands, out_shape, scratch=()):
    any_space = pl.BlockSpec(memory_space=pl.ANY)
    smem = pl.BlockSpec(memory_space=pltpu.SMEM)
    n_tables, n_in, n_out, n_own = len(tables), len(operands), len(out_shape), len(scratch)

    def run(*refs):
        refs = list(refs)
        take = lambda count: [refs.pop(0) for _ in range(count)]
        table_refs, ins, outs, own = take(n_tables), take(n_in), take(n_out), take(n_own)
        in_buffers, out_buffers, (in_sems, out_sems) = take(n_in), take(n_out), take(2)
        loads = [Load(ins[i], in_buffers[i], in_sems.at[i]) for i in range(n_in)]
        stores = [Store(out_buffers[i], outs[i], out_sems.at[i]) for i in range(n_out)]
        kernel(table_refs, loads, stores, *own)
        for load in loads:
            load.get()
        for store in stores:
            if not store.sent:
                store.send()
        for store in stores:
            store.copy.wait()

    return pl.pallas_call(
        run,
        in_specs=[smem] * n_tables + [any_space] * n_in,
        out_specs=[any_space] * n_out,
        out_shape=out_shape,
        scratch_shapes=[
            *scratch,
            *[pltpu.VMEM(o.shape, o.dtype) for o in [*operands, *out_shape]],
            pltpu.SemaphoreType.DMA((n_in,)),
            pltpu.SemaphoreType.DMA((n_out,)),
        ],
        compiler_params=pltpu.CompilerParams(vmem_limit_bytes=56 * 2**20),
        cost_estimate=pl.CostEstimate(flops=1, bytes_accessed=1, transcendentals=0),
    )(*tables, *operands)


def pair_product(held, pair, at, end, transposed):
    half = held.shape[1] // 2
    chunk = (slice(at, end), slice(None)) if transposed else (slice(None), slice(at, end))
    own, other = [load.get()[chunk] for load in pair]
    return product(held[:, :half], own, transposed) + product(held[:, half:], other, transposed)


def first_kernel(tables, loads, stores, tok_held, grad_held):
    (table,) = tables
    block, *blocks = [load.get() for load in loads[:-6]]
    weights, messages = loads[-6:], stores[6:]
    rows = block.shape[1]
    for i, held in enumerate((tok_held, grad_held)):
        acts, own, away = [store.ref for store in stores[i:6:2]]
        half = own.shape[1]
        acts[:rows] = jnp.where(table[CORE] == 0, block[i], blocks[0][i])
        for k in range(1, NZ):
            acts[k * rows : (k + 1) * rows] = blocks[k][i]
        stores[i].send()
        for slot in range(6):
            start = pl.multiple_of(table[FIRST + slot] * PIECE, PIECE)
            held[slot * PIECE : (slot + 1) * PIECE, :] = acts[pl.ds(start, PIECE), :]
    for which in range(3):
        held, transposed = ((tok_held, False), (grad_held, True))[which // 2]
        pair = weights[2 * which : 2 * which + 2]
        for at, end in spans(messages[0].ref.shape[2]):
            total = pair_product(held, pair, at, end, transposed).astype(jnp.bfloat16)
            for i, message in enumerate(messages):
                message.ref[which, :, at:end] = total[i * 2 * PIECE : (i + 1) * 2 * PIECE]
    for message in messages:
        message.send()
    for i in range(2):
        acts, own, away = [store.ref for store in stores[i:6:2]]
        half = own.shape[1]
        own[...] = acts[:, :half]
        away[...] = acts[:, half:]


def partial_kernel(tables, loads, stores, tok_held, grad_held):
    (table,) = tables
    for acts, held in zip(loads[:2], (tok_held, grad_held)):
        rows = acts.get()
        for slot in range(4):
            start = pl.multiple_of(table[SECOND + slot] * PIECE, PIECE)
            held[slot * PIECE : (slot + 1) * PIECE, :] = rows[pl.ds(start, PIECE), :]
    for which in range(3):
        held, transposed = ((tok_held, False), (grad_held, True))[which // 2]
        pair = loads[2 + 2 * which : 4 + 2 * which]
        out = stores[which].ref
        for at, end in spans(out.shape[1]):
            out[:, at:end] = pair_product(held, pair, at, end, transposed)
        stores[which].send()


def second_kernel(tables, loads, stores):
    (table,) = tables
    heard = loads[3:]
    outs = [store.ref for store in stores]
    core, x = table[CORE], table[AT_X]
    near = pl.ds(pl.multiple_of(x * PIECE, PIECE), PIECE)
    far = pl.ds(pl.multiple_of((1 - x) * PIECE, PIECE), PIECE)
    one = core == 1
    terms = [h.get() for h in heard]
    for which in range(3):
        total = loads[which].get()
        for at, end in spans(outs[0].shape[2]):
            near1, near2, near3 = [h[which, near, at:end].astype(jnp.float32) for h in terms]
            far1, far2, far3 = [h[which, far, at:end].astype(jnp.float32) for h in terms]
            part1, part2, part3, part4 = [
                total[slot * PIECE : (slot + 1) * PIECE, at:end] for slot in range(4)
            ]
            sum1 = part1 + far1 + jnp.where(one, far2 + far3, 0.0)
            high = sum1.astype(jnp.bfloat16)
            rest = sum1 - high.astype(jnp.float32)
            outs[0][which, :, at:end] = high
            outs[1][which, :, at:end] = jnp.where(one, rest, part2 + near2).astype(jnp.bfloat16)
            outs[2][which, :, at:end] = (part3 + far2).astype(jnp.bfloat16)
            outs[3][which, :, at:end] = part4 + near1 + jnp.where(one, near2 + near3, 0.0)


def weave_kernel(tables, loads, stores):
    core = tables[0][CORE]
    full = stores[0].ref
    for load, at_core in zip(loads, (core, 1 - core)):
        rows = load.get()
        for piece in range(NY * NX):
            start = pl.multiple_of((piece * NC + at_core) * PIECE, PIECE)
            full[pl.ds(start, PIECE), :] = rows[piece * PIECE : (piece + 1) * PIECE, :]


def unit_kernel(tables, loads, stores):
    kept, *heard = [load.get() for load in loads]
    gate, up, d_hidden = [
        kept[which] + sum(h[which].astype(jnp.float32) for h in heard) for which in range(3)
    ]
    sig_gate = jax.nn.sigmoid(gate)
    hidden, both = [store.ref for store in stores]
    hidden[...] = (gate * sig_gate * up).astype(jnp.bfloat16)
    slope = d_hidden * up * sig_gate * (1.0 + gate * (1.0 - sig_gate))
    both[0] = slope.astype(jnp.bfloat16)
    both[1] = (d_hidden * gate * sig_gate).astype(jnp.bfloat16)


def pack_kernel(tables, loads, stores):
    own, near1, near2, near3 = [load.get() for load in loads]
    first, second = [store.ref for store in stores]
    core0 = tables[0][CORE] == 0
    first[:, :PIECE] = own[...]
    first[:, PIECE:] = near1[...]
    stores[0].send()
    second[:, :PIECE] = jnp.where(core0, near2[...], own[...])
    second[:, PIECE:] = jnp.where(core0, near3[...], near1[...])


def input_kernel(tables, loads, stores):
    (table,) = tables
    own, near1, near2, near3, far1, far2, far3 = [load.get() for load in loads[:7]]
    weights = loads[7:]
    *messages, d_set, kept = [store.ref for store in stores]

    def put(slot, value):
        start = pl.multiple_of(table[GATHER + slot] * PIECE, PIECE)
        d_set[:, pl.ds(start, PIECE), :] = value

    put(0, own[...])
    put(1, near1[...])
    put(2, far1[:, :PIECE])
    put(3, far1[:, PIECE:])
    put(4, far2[:, :PIECE])
    put(5, far2[:, PIECE:])
    core0 = table[CORE] == 0
    put(6, jnp.where(core0, near2[...], far3[:, :PIECE]))
    put(7, jnp.where(core0, near3[...], far3[:, PIECE:]))
    stores[NZ].send()
    depth = weights[0].target.shape[0]
    block = NX * PIECE
    for side in range(2):
        for at, end in spans(depth):
            gate, up = [weights[2 * side + i].get()[at:end, :] for i in range(2)]
            total = product(d_set[0], gate, True) + product(d_set[1], up, True)
            columns = slice(side * depth + at, side * depth + end)
            kept[:, columns] = total[:block]
            for k in range(NZ):
                messages[k][:, columns] = total[k * block : (k + 1) * block].astype(jnp.bfloat16)


def shape(dims, dtype=jnp.bfloat16):
    return jax.ShapeDtypeStruct(dims, dtype)


def first_stage(table, blocks, weights):
    depth, width = weights[0].shape
    rows = NY * NX * PIECE
    return call(
        first_kernel,
        [table],
        [*blocks, *weights],
        [shape((rows, 2 * depth))] * 2
        + [shape((rows, depth))] * 4
        + [shape((3, 2 * PIECE, width))] * 3,
        [pltpu.VMEM((6 * PIECE, 2 * depth), jnp.bfloat16)] * 2,
    )


def partial_stage(table, tok_half, grad_half, weights):
    depth, width = weights[0].shape
    return call(
        partial_kernel,
        [table],
        [tok_half, grad_half, *weights],
        [shape((4 * PIECE, width), jnp.float32)] * 3,
        [pltpu.VMEM((4 * PIECE, 2 * depth), jnp.bfloat16)] * 2,
    )


def second_stage(table, products, heard):
    message = shape((3, PIECE, products[0].shape[1]))
    return call(
        second_kernel,
        [table],
        [*products, *heard],
        [message] * 3 + [shape(message.shape, jnp.float32)],
    )


def send_first(sent):
    return (
        lax.ppermute(sent[0], "row", row_perm(over_x, over_y(1))),
        lax.ppermute(sent[1], "row", row_perm(over_x, over_y(-1))),
        lax.ppermute(sent[2], "row", row_perm(None, over_y(2))),
    )


def send_second(sent):
    return (
        lax.ppermute(sent[0], "row", row_perm(over_y(1), over_x)),
        lax.ppermute(sent[1], "row", row_perm(over_y(-1), over_x)),
        lax.ppermute(sent[2], "row", row_perm(over_y(2), None)),
    )


FIRST, SECOND, CORE, AT_X, GATHER = 0, 6, 10, 11, 12


def table_rows():
    piece = lambda y_at, x_at: (y_at % NY) * NX + x_at
    rows = []
    for y in range(NY):
        for x in range(NX):
            other = 1 - x
            pair1 = [piece(y, other), piece(y + 1, other)]
            pair2 = [piece(y - 1, other), piece(y + 2, other)]
            if other == 1:
                pair1, pair2 = pair1[::-1], pair2[::-1]
            here = piece(y, x)
            first0 = pair1 + pair2 + [here, here]
            second0 = [piece(y + 1, x), piece(y - 1, x), piece(y + 2, x), here]
            first1 = [piece(y + step, x_at) for step in (1, -1, 2) for x_at in (0, 1)]
            second1 = [piece(y, other), here, here, here]
            gather0 = [here, piece(y - 1, x), piece(y, other), piece(y - 1, other)]
            gather0 += [piece(y + 1, other), piece(y + 2, other), piece(y + 1, x), piece(y + 2, x)]
            gather1 = [here, piece(y, other)]
            gather1 += [piece(y + step, x_at) for step in (-1, 1, 2) for x_at in (x, other)]
            rows.append(first0 + second0 + [0, x] + gather0)
            rows.append(first1 + second1 + [1, x] + gather1)
    return rows


def col_blocks(total):
    blocks = total.reshape(NY, NX, NC, PIECE, total.shape[1])
    return blocks[0], blocks[1:].astype(jnp.bfloat16)


def col_first(near, send):
    for step in range(1, NZ):
        near = near + lax.ppermute(send[step - 1], "col", col_perm(0, step)).astype(jnp.float32)
    return near[:, 0], near[:, 1].astype(jnp.bfloat16)


def col_second(result, send):
    result = result + lax.ppermute(send, "col", col_perm(1, 0)).astype(jnp.float32)
    return result.astype(jnp.bfloat16).reshape(NX * PIECE, result.shape[-1])


def body(tokens, gate_weight, up_weight, down_weight, grad_output):
    table = lax.dynamic_index_in_dim(
        jnp.array(table_rows(), jnp.int32), lax.axis_index("row"), 0, keepdims=False
    )
    core = table[CORE]
    flip = lambda value: lax.ppermute(value, "row", CORE_FLIP)
    after = lambda value, *others: lax.optimization_barrier((value, *others))[0]
    width, ff_width = gate_weight.shape
    half_rows = NY * NX * PIECE

    gate_other, up_other, down_other = flip(gate_weight), flip(up_weight), flip(down_weight)
    mine = jnp.stack([tokens, grad_output])
    own_block = jnp.concatenate([mine, flip(mine)], axis=2)
    starts = [own_block, own_block, after(own_block, gate_other), after(own_block, up_other)]
    blocks = [lax.ppermute(starts[step], BOTH, gather_perm(step)) for step in range(NZ)]

    both_weights = [gate_weight, gate_other, up_weight, up_other]
    weights = [*both_weights, down_weight, down_other]
    tok_half, grad_half, tok_own, grad_own, tok_away, grad_away, *sent = first_stage(
        table, [own_block, *blocks], weights
    )
    heard = send_first(sent)
    products = partial_stage(table, tok_half, grad_half, weights)
    tok_other = flip(after(tok_away, products[0]))
    grad_other = flip(after(grad_away, products[0]))
    (grad_all,) = call(
        weave_kernel, [table], [grad_own, grad_other], [shape((2 * half_rows, width))]
    )
    *heard, grad_all, tok_other = lax.optimization_barrier((*heard, grad_all, tok_other))
    *sent, kept = second_stage(table, products, heard)
    hidden, d_own = call(
        unit_kernel,
        [],
        [kept, *send_second(sent)],
        [shape((PIECE, ff_width)), shape((2, PIECE, ff_width))],
    )
    hidden = lax.all_gather(hidden, "row", axis=0, tiled=True)

    near = send_second([d_own] * 3)
    first, second = call(
        pack_kernel, [table], [d_own, *near], [shape((2, 2 * PIECE, ff_width))] * 2
    )
    far = send_first([first, second, first])
    dot = functools.partial(lax.dot_general, preferred_element_type=jnp.float32)
    contract_first = (((0,), (0,)), ((), ()))
    hidden = after(hidden, far[0])
    near_sum, send = col_blocks(jnp.dot(hidden, down_weight, preferred_element_type=jnp.float32))
    near_sum, send = lax.optimization_barrier((near_sum, send))
    layer_output = col_second(*col_first(near_sum, send))
    *far, _ = lax.optimization_barrier((*far, send))
    block = shape((NX * PIECE, 2 * width))
    *messages, d_set, kept = call(
        input_kernel,
        [table],
        [d_own, *near, *far, gate_weight, up_weight, gate_other, up_other],
        [block] * 4 + [shape((2, half_rows, ff_width)), shape(block.shape, jnp.float32)],
    )
    messages = [lax.ppermute(messages[k], BOTH, scatter_perm(k)) for k in range(NZ)]
    d_other = flip(d_set)
    grad_down = dot(hidden, grad_all, contract_first).astype(jnp.bfloat16)

    def weight_gradient(which):
        total = dot(tok_own, d_set[which], contract_first)
        return (total + dot(tok_other, d_other[which], contract_first)).astype(jnp.bfloat16)

    grad_gate, grad_up = weight_gradient(0), weight_gradient(1)
    *messages, grad_gate, grad_up = lax.optimization_barrier((*messages, grad_gate, grad_up))
    total = jnp.where(core == 0, kept, 0.0)
    for message in messages:
        total = total + message.astype(jnp.float32)
    grad_input = (total[:, :width] + flip(total[:, width:])).astype(jnp.bfloat16)
    return (layer_output, grad_input, grad_gate, grad_up, grad_down)


def solution(mesh):
    placed = (P("col", "row"), P("row", "col"), P("row", "col"), P("col", "row"), P("col", "row"))
    return jax.shard_map(
        body,
        mesh=mesh,
        in_specs=placed,
        out_specs=(
            P("col", "row"),
            P("col", "row"),
            P("row", "col"),
            P("row", "col"),
            P("col", "row"),
        ),
        check_vma=False,
    )
```

```python
import functools

import jax
import jax.numpy as jnp
from jax import lax
from jax.experimental import pallas as pl
from jax.experimental.pallas import tpu as pltpu
from jax.sharding import PartitionSpec as P

NY, NX, NC, NZ = 4, 2, 2, 4
PIECE = 64
BOTH = ("row", "col")


def row_at(y, x, core):
    return ((y % NY) * NX + x) * NC + core


def row_perm(core0, core1):
    pairs = []
    for y in range(NY):
        for x in range(NX):
            for core, move in ((0, core0), (1, core1)):
                if move is not None:
                    to_y, to_x = move(y, x)
                    pairs.append((row_at(y, x, core), row_at(to_y, to_x, core)))
    return pairs


def over_x(y, x):
    return y, 1 - x


def over_y(step):
    return lambda y, x: (y + step, x)


CORE_FLIP = [(i, i ^ 1) for i in range(NY * NX * NC)]


def gather_perm(step):
    pairs = []
    for row in range(NY * NX * NC):
        core = row % NC
        if core == 0 and step == 0:
            continue
        for hi in range(2):
            for z in range(NZ):
                source = (hi ^ core) * NZ + (z + step) % NZ
                pairs.append((row * 8 + source, row * 8 + hi * NZ + z))
    return pairs


def scatter_perm(step):
    return [(to, source) for source, to in gather_perm(step)]


def col_perm(flip, step):
    return [(hi * NZ + z, (hi ^ flip) * NZ + (z + step) % NZ) for hi in range(2) for z in range(NZ)]


def product(left, right, transposed):
    dims = (((1,), (1 if transposed else 0,)), ((), ()))
    return lax.dot_general(left, right, dims, preferred_element_type=jnp.float32)


def spans(width):
    return [(at, min(at + 256, width)) for at in range(0, width, 256)]


class Load:
    def __init__(self, source, target, sem):
        self.target, self.copy = target, pltpu.make_async_copy(source, target, sem)
        self.copy.start()

    def get(self):
        if self.copy is not None:
            self.copy.wait()
            self.copy = None
        return self.target


class Store:
    def __init__(self, source, target, sems):
        self.ref, self.target, self.sems, self.copies = source, target, sems, []

    def send(self, part=None):
        i = len(self.copies)
        source, target = self.ref, self.target
        if part is not None:
            source, target = source.at[part], target.at[part]
        self.copies.append(pltpu.make_async_copy(source, target, self.sems.at[i]))
        self.copies[-1].start()


class Raw:
    def __init__(self, value):
        self.value = value


def call(kernel, tables, operands, out_shape, scratch=(), limit=56):
    raw = [isinstance(o, Raw) for o in operands]
    operands = [o.value if isinstance(o, Raw) else o for o in operands]
    any_space = pl.BlockSpec(memory_space=pl.ANY)
    smem = pl.BlockSpec(memory_space=pltpu.SMEM)
    n_tables, n_in, n_out, n_own = len(tables), len(operands), len(out_shape), len(scratch)
    buffers = [o for o, is_raw in zip(operands, raw) if not is_raw]

    def run(*refs):
        refs = list(refs)
        take = lambda count: [refs.pop(0) for _ in range(count)]
        table_refs, ins, outs, own = take(n_tables), take(n_in), take(n_out), take(n_own)
        in_buffers, out_buffers = take(len(buffers)), take(n_out)
        (in_sems,), out_sems = take(1), take(n_out)
        loads = []
        for i, ref in enumerate(ins):
            loads.append(ref if raw[i] else Load(ref, in_buffers.pop(0), in_sems.at[i]))
        stores = [Store(*three) for three in zip(out_buffers, outs, out_sems)]
        kernel(table_refs, loads, stores, *own)
        for load in loads:
            if isinstance(load, Load):
                load.get()
        for store in stores:
            if not store.copies:
                store.send()
        for store in stores:
            for copy in store.copies:
                copy.wait()

    return pl.pallas_call(
        run,
        in_specs=[smem] * n_tables + [any_space] * n_in,
        out_specs=[any_space] * n_out,
        out_shape=out_shape,
        scratch_shapes=[
            *scratch,
            *[pltpu.VMEM(o.shape, o.dtype) for o in [*buffers, *out_shape]],
            pltpu.SemaphoreType.DMA((n_in,)),
            *[pltpu.SemaphoreType.DMA((3,))] * n_out,
        ],
        compiler_params=pltpu.CompilerParams(vmem_limit_bytes=limit * 2**20),
        cost_estimate=pl.CostEstimate(flops=1, bytes_accessed=1, transcendentals=0),
    )(*tables, *operands)


def pair_product(held, pair, at, end, transposed):
    half = held.shape[1] // 2
    chunk = (slice(at, end), slice(None)) if transposed else (slice(None), slice(at, end))
    own, other = [load.get()[chunk] for load in pair]
    return product(held[:, :half], own, transposed) + product(held[:, half:], other, transposed)


def first_kernel(tables, loads, stores, tok_held, grad_held, sems):
    (table,) = tables
    (block, heard), blocks = loads[:2], loads[2 : NZ + 1]
    weights, messages = loads[NZ + 1 :], stores[2:]
    rows = block.target.shape[1]
    landing = [
        [
            Load(source.at[i], stores[i].ref.at[pl.ds(k * rows, rows)], sems.at[i * (NZ - 1) + k - 1])
            for k, source in enumerate(blocks, 1)
        ]
        for i in range(2)
    ]
    for i, held in enumerate((tok_held, grad_held)):
        acts = stores[i].ref
        acts[:rows] = jnp.where(table[CORE] == 0, block.get()[i], heard.get()[i])
        for load in landing[i]:
            load.get()
        stores[i].send()
        for slot in range(6):
            start = pl.multiple_of(table[FIRST + slot] * PIECE, PIECE)
            held[slot * PIECE : (slot + 1) * PIECE, :] = acts[pl.ds(start, PIECE), :]
    for which in range(3):
        held, transposed = ((tok_held, False), (grad_held, True))[which // 2]
        pair = weights[2 * which : 2 * which + 2]
        for at, end in spans(messages[0].ref.shape[2]):
            total = pair_product(held, pair, at, end, transposed).astype(jnp.bfloat16)
            for i, message in enumerate(messages):
                message.ref[which, :, at:end] = total[i * 2 * PIECE : (i + 1) * 2 * PIECE]
        for message in messages:
            message.send(which)


def partial_kernel(tables, loads, stores, tok_held, grad_held):
    (table,) = tables
    for i, held in enumerate((tok_held, grad_held)):
        rows = loads[i].get()
        for slot in range(4):
            start = pl.multiple_of(table[SECOND + slot] * PIECE, PIECE)
            held[slot * PIECE : (slot + 1) * PIECE, :] = rows[pl.ds(start, PIECE), :]
        own, away = stores[3 + i], stores[5 + i]
        half = own.ref.shape[1]
        own.ref[...] = rows[:, :half]
        away.ref[...] = rows[:, half:]
        own.send()
        away.send()
    for which in range(3):
        held, transposed = ((tok_held, False), (grad_held, True))[which // 2]
        pair = loads[2 + 2 * which : 4 + 2 * which]
        out = stores[which].ref
        for at, end in spans(out.shape[1]):
            out[:, at:end] = pair_product(held, pair, at, end, transposed)
        stores[which].send()


def second_kernel(tables, loads, stores):
    (table,) = tables
    outs = [store.ref for store in stores]
    core, x = table[CORE], table[AT_X]
    near = pl.ds(pl.multiple_of(x * PIECE, PIECE), PIECE)
    far = pl.ds(pl.multiple_of((1 - x) * PIECE, PIECE), PIECE)
    one = core == 1
    terms = [load.get() for load in loads[3:]]
    for which in range(3):
        total = loads[which].get()
        for at, end in spans(outs[0].shape[2]):
            _, near2, _ = [h[which, near, at:end].astype(jnp.float32) for h in terms]
            far1, far2, far3 = [h[which, far, at:end].astype(jnp.float32) for h in terms]
            part1, part2, part3 = [
                total[slot * PIECE : (slot + 1) * PIECE, at:end] for slot in range(3)
            ]
            sum1 = part1 + far1 + jnp.where(one, far2 + far3, 0.0)
            high = sum1.astype(jnp.bfloat16)
            rest = sum1 - high.astype(jnp.float32)
            outs[0][which, :, at:end] = high
            outs[1][which, :, at:end] = jnp.where(one, rest, part2 + near2).astype(jnp.bfloat16)
            outs[2][which, :, at:end] = (part3 + far2).astype(jnp.bfloat16)
        for store in stores:
            store.send(which)


def kept_kernel(tables, loads, stores):
    (table,) = tables
    near = pl.ds(pl.multiple_of(table[AT_X] * PIECE, PIECE), PIECE)
    one = table[CORE] == 1
    for which in range(3):
        near1, near2, near3 = [h.get()[which, near].astype(jnp.float32) for h in loads[3:]]
        total = loads[which].get()[...] + near1
        stores[0].ref[which] = total + jnp.where(one, near2 + near3, 0.0)


def weave_kernel(tables, loads, stores):
    core = tables[0][CORE]
    full = stores[0].ref
    for load, at_core in zip(loads, (core, 1 - core)):
        rows = load.get()
        for piece in range(NY * NX):
            start = pl.multiple_of((piece * NC + at_core) * PIECE, PIECE)
            full[pl.ds(start, PIECE), :] = rows[piece * PIECE : (piece + 1) * PIECE, :]


def unit_kernel(tables, loads, stores):
    kept, *heard = [load.get() for load in loads]
    gate, up, d_hidden = [
        kept[which] + sum(h[which].astype(jnp.float32) for h in heard) for which in range(3)
    ]
    sig_gate = jax.nn.sigmoid(gate)
    hidden, both = [store.ref for store in stores]
    hidden[...] = (gate * sig_gate * up).astype(jnp.bfloat16)
    slope = d_hidden * up * sig_gate * (1.0 + gate * (1.0 - sig_gate))
    both[0] = slope.astype(jnp.bfloat16)
    both[1] = (d_hidden * gate * sig_gate).astype(jnp.bfloat16)


def pack_kernel(tables, loads, stores, sems):
    own, near1, near2, near3 = loads
    first, second = [store.ref for store in stores]
    landing = [
        Load(source, first.at[:, pl.ds(i * PIECE, PIECE)], sems.at[i])
        for i, source in enumerate((own, near1))
    ]
    for load in landing:
        load.get()
    stores[0].send()
    core0 = tables[0][CORE] == 0
    second[:, :PIECE] = jnp.where(core0, near2.get()[...], first[:, :PIECE])
    second[:, PIECE:] = jnp.where(core0, near3.get()[...], first[:, PIECE:])


def input_kernel(tables, loads, stores, sems):
    (table,) = tables
    own, near1, far1, far2, near2, near3, far3 = loads[:7]
    weights = loads[7:]
    *messages, d_set, kept = [store.ref for store in stores]

    def at_slot(slot):
        return pl.ds(pl.multiple_of(table[GATHER + slot] * PIECE, PIECE), PIECE)

    front, back = pl.ds(0, PIECE), pl.ds(PIECE, PIECE)
    sources = [own, near1]
    for both in (far1, far2):
        sources += [both.at[:, front], both.at[:, back]]
    landing = [
        Load(source, d_set.at[:, at_slot(slot)], sems.at[slot])
        for slot, source in enumerate(sources)
    ]
    core0 = table[CORE] == 0
    d_set[:, at_slot(6)] = jnp.where(core0, near2.get()[...], far3.get()[:, :PIECE])
    d_set[:, at_slot(7)] = jnp.where(core0, near3.get()[...], far3.get()[:, PIECE:])
    for load in landing:
        load.get()
    stores[NZ].send()
    depth = weights[0].target.shape[0]
    block = NX * PIECE
    for side in range(2):
        for at, end in spans(depth):
            gate, up = [weights[2 * side + i].get()[at:end, :] for i in range(2)]
            total = product(d_set[0], gate, True) + product(d_set[1], up, True)
            columns = slice(side * depth + at, side * depth + end)
            kept[:, columns] = total[:block]
            for k in range(NZ):
                messages[k][:, columns] = total[k * block : (k + 1) * block].astype(jnp.bfloat16)


def shape(dims, dtype=jnp.bfloat16):
    return jax.ShapeDtypeStruct(dims, dtype)


def first_stage(table, blocks, weights):
    depth, width = weights[0].shape
    rows = NY * NX * PIECE
    held = pltpu.VMEM((6 * PIECE, 2 * depth), jnp.bfloat16)
    return call(
        first_kernel,
        [table],
        [*blocks[:2], *[Raw(block) for block in blocks[2:]], *weights],
        [shape((rows, 2 * depth))] * 2 + [shape((3, 2 * PIECE, width))] * 3,
        [held, held, pltpu.SemaphoreType.DMA((2 * (NZ - 1),))],
    )


def partial_stage(table, tok_half, grad_half, weights):
    depth, width = weights[0].shape
    return call(
        partial_kernel,
        [table],
        [tok_half, grad_half, *weights],
        [shape((4 * PIECE, width), jnp.float32)] * 3 + [shape((NY * NX * PIECE, depth))] * 4,
        [pltpu.VMEM((4 * PIECE, 2 * depth), jnp.bfloat16)] * 2,
    )


def second_stage(table, products, heard):
    message = shape((3, PIECE, products[0].shape[1]))
    return call(second_kernel, [table], [*products, *heard], [message] * 3)


def send_first(sent):
    return (
        lax.ppermute(sent[0], "row", row_perm(over_x, over_y(1))),
        lax.ppermute(sent[1], "row", row_perm(over_x, over_y(-1))),
        lax.ppermute(sent[2], "row", row_perm(None, over_y(2))),
    )


def send_second(sent):
    return (
        lax.ppermute(sent[0], "row", row_perm(over_y(1), over_x)),
        lax.ppermute(sent[1], "row", row_perm(over_y(-1), over_x)),
        lax.ppermute(sent[2], "row", row_perm(over_y(2), None)),
    )


FIRST, SECOND, CORE, AT_X, GATHER = 0, 6, 10, 11, 12


def table_rows():
    piece = lambda y_at, x_at: (y_at % NY) * NX + x_at
    rows = []
    for y in range(NY):
        for x in range(NX):
            other = 1 - x
            pair1 = [piece(y, other), piece(y + 1, other)]
            pair2 = [piece(y - 1, other), piece(y + 2, other)]
            if other == 1:
                pair1, pair2 = pair1[::-1], pair2[::-1]
            here = piece(y, x)
            first0 = pair1 + pair2 + [here, here]
            second0 = [piece(y + 1, x), piece(y - 1, x), piece(y + 2, x), here]
            first1 = [piece(y + step, x_at) for step in (1, -1, 2) for x_at in (0, 1)]
            second1 = [piece(y, other), here, here, here]
            gather0 = [here, piece(y - 1, x), piece(y, other), piece(y - 1, other)]
            gather0 += [piece(y + 1, other), piece(y + 2, other), piece(y + 1, x), piece(y + 2, x)]
            gather1 = [here, piece(y, other)]
            gather1 += [piece(y + step, x_at) for step in (-1, 1, 2) for x_at in (x, other)]
            rows.append(first0 + second0 + [0, x] + gather0)
            rows.append(first1 + second1 + [1, x] + gather1)
    return rows


def col_blocks(total):
    blocks = total.reshape(NY, NX, NC, PIECE, total.shape[1])
    return blocks[0], blocks[1:].astype(jnp.bfloat16)


def col_first(near, send):
    heard = [lax.ppermute(send[step - 1], "col", col_perm(0, step)) for step in range(1, NZ)]
    for term in heard:
        near = near + term.astype(jnp.float32)
    return near[:, 0], near[:, 1].astype(jnp.bfloat16)


def col_second(result, send):
    result = result + lax.ppermute(send, "col", col_perm(1, 0)).astype(jnp.float32)
    return result.astype(jnp.bfloat16).reshape(NX * PIECE, result.shape[-1])


def body(tokens, gate_weight, up_weight, down_weight, grad_output):
    table = lax.dynamic_index_in_dim(
        jnp.array(table_rows(), jnp.int32), lax.axis_index("row"), 0, keepdims=False
    )
    core = table[CORE]
    flip = lambda value: lax.ppermute(value, "row", CORE_FLIP)
    after = lambda value, *others: lax.optimization_barrier((value, *others))[0]
    width, ff_width = gate_weight.shape
    half_rows = NY * NX * PIECE

    gate_other, up_other, down_other = flip(gate_weight), flip(up_weight), flip(down_weight)
    mine = jnp.stack([tokens, grad_output])
    own_block = jnp.concatenate([mine, flip(mine)], axis=2)
    starts = [own_block, own_block, after(own_block, gate_other), after(own_block, up_other)]
    blocks = [lax.ppermute(starts[step], BOTH, gather_perm(step)) for step in range(NZ)]

    both_weights = [gate_weight, gate_other, up_weight, up_other]
    weights = [*both_weights, down_weight, down_other]
    tok_half, grad_half, *sent = first_stage(table, [own_block, *blocks], weights)
    heard = send_first(sent)
    *products, tok_own, grad_own, tok_away, grad_away = partial_stage(
        table, tok_half, grad_half, weights
    )
    tok_other = flip(after(tok_away, products[0]))
    grad_other = flip(after(grad_away, products[0]))
    (grad_all,) = call(
        weave_kernel, [table], [grad_own, grad_other], [shape((2 * half_rows, width))]
    )
    *heard, grad_all, tok_other = lax.optimization_barrier((*heard, grad_all, tok_other))
    sent = second_stage(table, products, heard)
    last = [after(product, sent[0])[3 * PIECE :] for product in products]
    (kept,) = call(
        kept_kernel, [table], [*last, *heard], [shape((3, PIECE, ff_width), jnp.float32)]
    )
    hidden, d_own = call(
        unit_kernel,
        [],
        [kept, *send_second(sent)],
        [shape((PIECE, ff_width)), shape((2, PIECE, ff_width))],
    )
    hidden = lax.all_gather(hidden, "row", axis=0, tiled=True)

    near = send_second([d_own] * 3)
    first, second = call(
        pack_kernel,
        [table],
        [Raw(d_own), Raw(near[0]), *near[1:]],
        [shape((2, 2 * PIECE, ff_width))] * 2,
        [pltpu.SemaphoreType.DMA((2,))],
    )
    far = send_first([first, second, first])
    dot = functools.partial(lax.dot_general, preferred_element_type=jnp.float32)
    contract_first = (((0,), (0,)), ((), ()))
    hidden = after(hidden, far[0])
    near_sum, send = col_blocks(jnp.dot(hidden, down_weight, preferred_element_type=jnp.float32))
    near_sum, send = lax.optimization_barrier((near_sum, send))
    near_sum, near_send = col_first(near_sum, send)
    *far, near_sum, near_send = lax.optimization_barrier((*far, near_sum, near_send))
    layer_output = col_second(near_sum, near_send)
    block = shape((NX * PIECE, 2 * width))
    *messages, d_set, kept = call(
        input_kernel,
        [table],
        [
            *[Raw(d_own), Raw(near[0]), Raw(far[0]), Raw(far[1])],
            *[near[1], near[2], far[2], gate_weight, up_weight, gate_other, up_other],
        ],
        [block] * 4 + [shape((2, half_rows, ff_width)), shape(block.shape, jnp.float32)],
        [pltpu.SemaphoreType.DMA((6,))],
    )
    messages = [lax.ppermute(messages[k], BOTH, scatter_perm(k)) for k in range(NZ)]
    d_other = flip(d_set)
    grad_down = dot(hidden, grad_all, contract_first).astype(jnp.bfloat16)

    def weight_gradient(which):
        total = dot(tok_own, d_set[which], contract_first)
        return (total + dot(tok_other, d_other[which], contract_first)).astype(jnp.bfloat16)

    grad_gate, grad_up = weight_gradient(0), weight_gradient(1)
    *messages, grad_gate, grad_up = lax.optimization_barrier((*messages, grad_gate, grad_up))
    total = jnp.where(core == 0, kept, 0.0)
    for message in messages:
        total = total + message.astype(jnp.float32)
    grad_input = (total[:, :width] + flip(total[:, width:])).astype(jnp.bfloat16)
    return (layer_output, grad_input, grad_gate, grad_up, grad_down)


def solution(mesh):
    placed = (P("col", "row"), P("row", "col"), P("row", "col"), P("col", "row"), P("col", "row"))
    return jax.shard_map(
        body,
        mesh=mesh,
        in_specs=placed,
        out_specs=(
            P("col", "row"),
            P("col", "row"),
            P("row", "col"),
            P("row", "col"),
            P("col", "row"),
        ),
        check_vma=False,
    )
```

```python
import functools

import jax
import jax.numpy as jnp
from jax import lax
from jax.experimental import pallas as pl
from jax.experimental.pallas import tpu as pltpu
from jax.sharding import PartitionSpec as P

NY, NX, NC, NZ = 4, 2, 2, 4
PIECE = 64
BOTH = ("row", "col")


def row_at(y, x, core):
    return ((y % NY) * NX + x) * NC + core


def row_perm(core0, core1):
    pairs = []
    for y in range(NY):
        for x in range(NX):
            for core, move in ((0, core0), (1, core1)):
                if move is not None:
                    to_y, to_x = move(y, x)
                    pairs.append((row_at(y, x, core), row_at(to_y, to_x, core)))
    return pairs


def over_x(y, x):
    return y, 1 - x


def over_y(step):
    return lambda y, x: (y + step, x)


CORE_FLIP = [(i, i ^ 1) for i in range(NY * NX * NC)]


def gather_perm(step):
    pairs = []
    for row in range(NY * NX * NC):
        core = row % NC
        if core == 0 and step == 0:
            continue
        for hi in range(2):
            for z in range(NZ):
                source = (hi ^ core) * NZ + (z + step) % NZ
                pairs.append((row * 8 + source, row * 8 + hi * NZ + z))
    return pairs


def scatter_perm(step):
    return [(to, source) for source, to in gather_perm(step)]


def product(left, right, transposed):
    dims = (((1,), (1 if transposed else 0,)), ((), ()))
    return lax.dot_general(left, right, dims, preferred_element_type=jnp.float32)


def spans(width):
    return [(at, min(at + 256, width)) for at in range(0, width, 256)]


def shape(dims, dtype=jnp.bfloat16):
    return jax.ShapeDtypeStruct(dims, dtype)


def call(kernel, operands, out_shape, scratch=()):
    n_in, n_out = len(operands), len(out_shape)

    def run(*refs):
        kernel(refs[:n_in], refs[n_in : n_in + n_out], *refs[n_in + n_out :])

    vmem = pl.BlockSpec(memory_space=pltpu.VMEM)
    return pl.pallas_call(
        run,
        in_specs=[vmem] * n_in,
        out_specs=[vmem] * n_out,
        out_shape=out_shape,
        scratch_shapes=scratch,
        compiler_params=pltpu.CompilerParams(vmem_limit_bytes=12 * 2**20),
        cost_estimate=pl.CostEstimate(flops=1, bytes_accessed=1, transcendentals=0),
    )(*operands)


class Place:
    def __init__(self):
        row = lax.axis_index("row")
        self.core, self.x, self.y = row % NC, (row // NC) % NX, row // (NC * NX)
        self.other = 1 - self.x

    def piece(self, step, x):
        return ((self.y + step) % NY) * NX + x

    def choose(self, core0, core1):
        pieces = [jnp.where(self.core == 0, self.piece(*a), self.piece(*b)) for a, b in zip(core0, core1)]
        return [pl.ds(pl.multiple_of(piece * PIECE, PIECE), PIECE) for piece in pieces]

    def first(self):
        o = self.other
        core0 = [(o, o), (1 - o, o), (3 - o, o), (2 + o, o), (0, self.x), (0, self.x)]
        return self.choose(core0, [(step, x) for step in (1, 3, 2) for x in (0, 1)])

    def second(self):
        x, o = self.x, self.other
        return self.choose([(1, x), (3, x), (2, x), (0, x)], [(0, o), (0, x), (0, x), (0, x)])

    def gathered(self):
        x, o = self.x, self.other
        core0 = [(0, x), (3, x), (0, o), (3, o), (1, o), (2, o), (1, x), (2, x)]
        return self.choose(core0, [(0, x), (0, o)] + [(step, at) for step in (3, 1, 2) for at in (x, o)])

    def half(self, x):
        return pl.ds(pl.multiple_of(x * PIECE, PIECE), PIECE)


def pair_product(held, pair, at, end, transposed):
    half = held.shape[1] // 2
    chunk = (slice(at, end), slice(None)) if transposed else (slice(None), slice(at, end))
    own, other = [ref[chunk] for ref in pair]
    return product(held[:, :half], own, transposed) + product(held[:, half:], other, transposed)


def block_kernel(ins, outs):
    (block,) = outs
    half = block.shape[2] // 2
    for i in range(2):
        block[i, :, :half] = ins[i][...]
        block[i, :, half:] = ins[2 + i][...]


def first_kernel(ins, outs, tok_held, grad_held):
    place = Place()
    block, *blocks = ins[: NZ + 1]
    weights, messages = ins[NZ + 1 :], outs[2:]
    rows = block.shape[1]
    pieces = place.first()
    for i, held in enumerate((tok_held, grad_held)):
        acts = outs[i]
        acts[:rows] = jnp.where(place.core == 0, block[i], blocks[0][i])
        for k in range(1, NZ):
            acts[k * rows : (k + 1) * rows] = blocks[k][i]
        for slot, rows_at in enumerate(pieces):
            held[slot * PIECE : (slot + 1) * PIECE, :] = acts[rows_at, :]
    for which in range(3):
        held, transposed = ((tok_held, False), (grad_held, True))[which // 2]
        pair = weights[2 * which : 2 * which + 2]
        for at, end in spans(messages[0].shape[2]):
            total = pair_product(held, pair, at, end, transposed).astype(jnp.bfloat16)
            for i, message in enumerate(messages):
                message[which, :, at:end] = total[i * 2 * PIECE : (i + 1) * 2 * PIECE]


def partial_kernel(ins, outs, tok_held, grad_held):
    pieces = Place().second()
    for i, held in enumerate((tok_held, grad_held)):
        rows = ins[i]
        for slot, rows_at in enumerate(pieces):
            held[slot * PIECE : (slot + 1) * PIECE, :] = rows[rows_at, :]
        own, away = outs[1 + i], outs[3 + i]
        half = own.shape[1]
        own[...] = rows[:, :half]
        away[...] = rows[:, half:]
    for which in range(3):
        held, transposed = ((tok_held, False), (grad_held, True))[which // 2]
        pair = ins[2 + 2 * which : 4 + 2 * which]
        for at, end in spans(outs[0].shape[2]):
            outs[0][which, :, at:end] = pair_product(held, pair, at, end, transposed)


def second_kernel(ins, outs):
    place = Place()
    products, *heard = ins
    near, far = place.half(place.x), place.half(place.other)
    one = place.core == 1
    for which in range(3):
        for at, end in spans(outs[0].shape[2]):
            near2 = heard[1][which, near, at:end].astype(jnp.float32)
            far1, far2, far3 = [h[which, far, at:end].astype(jnp.float32) for h in heard]
            part1, part2, part3 = [
                products[which, slot * PIECE : (slot + 1) * PIECE, at:end] for slot in range(3)
            ]
            sum1 = part1 + far1 + jnp.where(one, far2 + far3, 0.0)
            high = sum1.astype(jnp.bfloat16)
            rest = sum1 - high.astype(jnp.float32)
            outs[0][which, :, at:end] = high
            outs[1][which, :, at:end] = jnp.where(one, rest, part2 + near2).astype(jnp.bfloat16)
            outs[2][which, :, at:end] = (part3 + far2).astype(jnp.bfloat16)


def unit_kernel(ins, outs):
    place = Place()
    products, first, second = ins[0], ins[1:4], ins[4:7]
    hidden, both = outs
    near, one = place.half(place.x), place.core == 1
    for at, end in spans(hidden.shape[1]):

        def summed(which):
            near1, near2, near3 = [h[which, near, at:end].astype(jnp.float32) for h in first]
            total = products[which, 3 * PIECE :, at:end] + near1
            total = total + jnp.where(one, near2 + near3, 0.0)
            return total + sum(h[which, :, at:end].astype(jnp.float32) for h in second)

        gate, up, d_hidden = [summed(which) for which in range(3)]
        sig_gate = jax.nn.sigmoid(gate)
        hidden[:, at:end] = (gate * sig_gate * up).astype(jnp.bfloat16)
        slope = d_hidden * up * sig_gate * (1.0 + gate * (1.0 - sig_gate))
        both[0, :, at:end] = slope.astype(jnp.bfloat16)
        both[1, :, at:end] = (d_hidden * gate * sig_gate).astype(jnp.bfloat16)


def weave_kernel(ins, outs):
    core = Place().core
    for rows, at_core in zip(ins, (core, 1 - core)):
        for piece in range(NY * NX):
            start = pl.multiple_of((piece * NC + at_core) * PIECE, PIECE)
            outs[0][pl.ds(start, PIECE), :] = rows[piece * PIECE : (piece + 1) * PIECE, :]


def pack_kernel(ins, outs):
    own, near1, near2, near3 = ins
    first, second = outs
    core0 = Place().core == 0
    first[:, :PIECE] = own[...]
    first[:, PIECE:] = near1[...]
    second[:, :PIECE] = jnp.where(core0, near2[...], own[...])
    second[:, PIECE:] = jnp.where(core0, near3[...], near1[...])


def layer_kernel(ins, outs, held):
    hidden, *weights = ins
    core = Place().core
    width = weights[0].shape[1]
    for piece in range(NY * NX):
        start = pl.multiple_of((piece * NC + core) * PIECE, PIECE)
        held[piece * PIECE : (piece + 1) * PIECE, :] = hidden[pl.ds(start, PIECE), :]
    for side, weight in enumerate(weights):
        for at, end in spans(width):
            outs[0][:, side * width + at : side * width + end] = product(
                held[...], weight[:, at:end], False
            )


def input_kernel(ins, outs):
    place = Place()
    layer, own, near1, near2, near3, far1, far2, far3 = ins[:8]
    weights = ins[8:]
    *messages, d_set, kept = outs
    core0 = place.core == 0
    pieces = place.gathered()
    values = [own[...], near1[...], far1[:, :PIECE], far1[:, PIECE:], far2[:, :PIECE], far2[:, PIECE:]]
    values.append(jnp.where(core0, near2[...], far3[:, :PIECE]))
    values.append(jnp.where(core0, near3[...], far3[:, PIECE:]))
    for rows_at, value in zip(pieces, values):
        d_set[:, rows_at, :] = value
    depth = weights[0].shape[0]
    block = NX * PIECE
    for side in range(2):
        for at, end in spans(depth):
            gate, up = [weights[2 * side + i][at:end, :] for i in range(2)]
            total = product(d_set[0], gate, True) + product(d_set[1], up, True)
            columns = slice(side * depth + at, side * depth + end)
            for i, term in enumerate((layer[:, columns], total)):
                kept[i, :, columns] = term[:block]
                for k in range(NZ):
                    rows = term[k * block : (k + 1) * block]
                    messages[k][i, :, columns] = rows.astype(jnp.bfloat16)


def send_first(sent):
    return (
        lax.ppermute(sent[0], "row", row_perm(over_x, over_y(1))),
        lax.ppermute(sent[1], "row", row_perm(over_x, over_y(-1))),
        lax.ppermute(sent[2], "row", row_perm(None, over_y(2))),
    )


def send_second(sent):
    return (
        lax.ppermute(sent[0], "row", row_perm(over_y(1), over_x)),
        lax.ppermute(sent[1], "row", row_perm(over_y(-1), over_x)),
        lax.ppermute(sent[2], "row", row_perm(over_y(2), None)),
    )


def body(tokens, gate_weight, up_weight, down_weight, grad_output):
    core = lax.axis_index("row") % NC
    flip = lambda value: lax.ppermute(value, "row", CORE_FLIP)
    after = lambda value, *others: lax.optimization_barrier((value, *others))[0]
    width, ff_width = gate_weight.shape
    half_rows = NY * NX * PIECE
    rows = tokens.shape[0]

    tok_theirs, grad_theirs = flip(tokens), flip(grad_output)
    gate_other, up_other, down_other = flip(gate_weight), flip(up_weight), flip(down_weight)
    (own_block,) = call(
        block_kernel, [tokens, grad_output, tok_theirs, grad_theirs], [shape((2, rows, 2 * width))]
    )
    starts = [own_block, own_block, after(own_block, gate_other), after(own_block, up_other)]
    blocks = [lax.ppermute(starts[step], BOTH, gather_perm(step)) for step in range(NZ)]

    both_weights = [gate_weight, gate_other, up_weight, up_other]
    weights = [*both_weights, down_weight, down_other]
    held = lambda pieces: [pltpu.VMEM((pieces * PIECE, 2 * width), jnp.bfloat16)] * 2
    tok_half, grad_half, *sent = call(
        first_kernel,
        [own_block, *blocks, *weights],
        [shape((half_rows, 2 * width))] * 2 + [shape((3, 2 * PIECE, ff_width))] * 3,
        held(6),
    )
    heard = send_first(sent)
    products, tok_own, grad_own, tok_away, grad_away = call(
        partial_kernel,
        [tok_half, grad_half, *weights],
        [shape((3, 4 * PIECE, ff_width), jnp.float32)] + [shape((half_rows, width))] * 4,
        held(4),
    )
    tok_other, grad_other = flip(tok_away), flip(grad_away)
    (grad_all,) = call(weave_kernel, [grad_own, grad_other], [shape((2 * half_rows, width))])
    *heard, grad_all, tok_other = lax.optimization_barrier((*heard, grad_all, tok_other))
    sent = call(second_kernel, [products, *heard], [shape((3, PIECE, ff_width))] * 3)
    hidden, d_own = call(
        unit_kernel,
        [products, *heard, *send_second(sent)],
        [shape((PIECE, ff_width)), shape((2, PIECE, ff_width))],
    )
    hidden = lax.all_gather(hidden, "row", axis=0, tiled=True)

    near = send_second([d_own] * 3)
    first, second = call(pack_kernel, [d_own, *near], [shape((2, 2 * PIECE, ff_width))] * 2)
    far = send_first([first, second, first])
    hidden = after(hidden, far[0])
    (layer,) = call(
        layer_kernel,
        [hidden, down_weight, down_other],
        [shape((half_rows, 2 * width), jnp.float32)],
        [pltpu.VMEM((half_rows, ff_width), jnp.bfloat16)],
    )
    block = (2, rows, 2 * width)
    *messages, d_set, kept = call(
        input_kernel,
        [layer, d_own, *near, *far, gate_weight, up_weight, gate_other, up_other],
        [shape(block)] * 4 + [shape((2, half_rows, ff_width)), shape(block, jnp.float32)],
    )
    messages = [lax.ppermute(messages[k], BOTH, scatter_perm(k)) for k in range(NZ)]
    d_other = flip(d_set)
    dot = functools.partial(lax.dot_general, preferred_element_type=jnp.float32)
    contract_first = (((0,), (0,)), ((), ()))
    grad_down = dot(hidden, grad_all, contract_first).astype(jnp.bfloat16)

    def weight_gradient(which):
        total = dot(tok_own, d_set[which], contract_first)
        return (total + dot(tok_other, d_other[which], contract_first)).astype(jnp.bfloat16)

    grad_gate, grad_up = weight_gradient(0), weight_gradient(1)
    *messages, grad_gate, grad_up = lax.optimization_barrier((*messages, grad_gate, grad_up))
    total = jnp.where(core == 0, kept, 0.0)
    for message in messages:
        total = total + message.astype(jnp.float32)
    total = (total[:, :, :width] + flip(total[:, :, width:])).astype(jnp.bfloat16)
    return (total[0], total[1], grad_gate, grad_up, grad_down)


def solution(mesh):
    placed = (P("col", "row"), P("row", "col"), P("row", "col"), P("col", "row"), P("col", "row"))
    return jax.shard_map(
        body,
        mesh=mesh,
        in_specs=placed,
        out_specs=(
            P("col", "row"),
            P("col", "row"),
            P("row", "col"),
            P("row", "col"),
            P("col", "row"),
        ),
        check_vma=False,
    )
```

```python
import functools

import jax
import jax.numpy as jnp
from jax import lax
from jax.experimental import pallas as pl
from jax.experimental.pallas import tpu as pltpu
from jax.sharding import PartitionSpec as P

NY, NX, NC, NZ = 4, 2, 2, 4
PIECE = 64
BOTH = ("row", "col")


def row_at(y, x, core):
    return ((y % NY) * NX + x) * NC + core


def row_perm(core0, core1):
    pairs = []
    for y in range(NY):
        for x in range(NX):
            for core, move in ((0, core0), (1, core1)):
                if move is not None:
                    to_y, to_x = move(y, x)
                    pairs.append((row_at(y, x, core), row_at(to_y, to_x, core)))
    return pairs


def over_x(y, x):
    return y, 1 - x


def over_y(step):
    return lambda y, x: (y + step, x)


CORE_FLIP = [(i, i ^ 1) for i in range(NY * NX * NC)]


def gather_perm(step):
    pairs = []
    for row in range(NY * NX * NC):
        core = row % NC
        if core == 0 and step == 0:
            continue
        for hi in range(2):
            for z in range(NZ):
                source = (hi ^ core) * NZ + (z + step) % NZ
                pairs.append((row * 8 + source, row * 8 + hi * NZ + z))
    return pairs


def scatter_perm(step):
    return [(to, source) for source, to in gather_perm(step)]


def product(left, right, transposed):
    dims = (((1,), (1 if transposed else 0,)), ((), ()))
    return lax.dot_general(left, right, dims, preferred_element_type=jnp.float32)


def spans(width):
    return [(at, min(at + 256, width)) for at in range(0, width, 256)]


def shape(dims, dtype=jnp.bfloat16):
    return jax.ShapeDtypeStruct(dims, dtype)


def call(kernel, operands, out_shape, scratch=()):
    n_in, n_out = len(operands), len(out_shape)

    def run(*refs):
        kernel(refs[:n_in], refs[n_in : n_in + n_out], *refs[n_in + n_out :])

    vmem = pl.BlockSpec(memory_space=pltpu.VMEM)
    return pl.pallas_call(
        run,
        in_specs=[vmem] * n_in,
        out_specs=[vmem] * n_out,
        out_shape=out_shape,
        scratch_shapes=scratch,
        compiler_params=pltpu.CompilerParams(vmem_limit_bytes=12 * 2**20),
        cost_estimate=pl.CostEstimate(flops=1, bytes_accessed=1, transcendentals=0),
    )(*operands)


class Place:
    def __init__(self):
        row = lax.axis_index("row")
        self.core, self.x, self.y = row % NC, (row // NC) % NX, row // (NC * NX)
        self.other = 1 - self.x

    def piece(self, step, x):
        return ((self.y + step) % NY) * NX + x

    def choose(self, core0, core1):
        pieces = [jnp.where(self.core == 0, self.piece(*a), self.piece(*b)) for a, b in zip(core0, core1)]
        return [pl.ds(pl.multiple_of(piece * PIECE, PIECE), PIECE) for piece in pieces]

    def first(self):
        o = self.other
        core0 = [(o, o), (1 - o, o), (3 - o, o), (2 + o, o), (0, self.x), (0, self.x)]
        return self.choose(core0, [(step, x) for step in (1, 3, 2) for x in (0, 1)])

    def second(self):
        x, o = self.x, self.other
        return self.choose([(1, x), (3, x), (2, x), (0, x)], [(0, o), (0, x), (0, x), (0, x)])

    def gathered(self):
        x, o = self.x, self.other
        core0 = [(0, x), (3, x), (0, o), (3, o), (1, o), (2, o), (1, x), (2, x)]
        return self.choose(core0, [(0, x), (0, o)] + [(step, at) for step in (3, 1, 2) for at in (x, o)])

    def half(self, x):
        return pl.ds(pl.multiple_of(x * PIECE, PIECE), PIECE)


def pair_product(held, pair, at, end, transposed):
    half = held.shape[1] // 2
    chunk = (slice(at, end), slice(None)) if transposed else (slice(None), slice(at, end))
    own, other = [ref[chunk] for ref in pair]
    return product(held[:, :half], own, transposed) + product(held[:, half:], other, transposed)


def mine_kernel(ins, outs):
    for i in range(2):
        outs[0][i] = ins[i][...]


def block_kernel(ins, outs):
    mine, *theirs = ins
    (block,) = outs
    half = block.shape[2] // 2
    for i in range(2):
        block[i, :, :half] = mine[i]
        block[i, :, half:] = theirs[i][...]


def keep_kernel(ins, outs):
    for source, out in zip(ins, outs):
        out[...] = source[...]


def gradient_kernel(ins, outs):
    tok_own, tok_other, d_own, d_other = ins
    dims = (((0,), (0,)), ((), ()))
    for i, out in enumerate(outs):
        for at, end in spans(out.shape[1]):
            total = lax.dot_general(
                tok_own[...], d_own[i, :, at:end], dims, preferred_element_type=jnp.float32
            )
            total += lax.dot_general(
                tok_other[...], d_other[i, :, at:end], dims, preferred_element_type=jnp.float32
            )
            out[:, at:end] = total.astype(jnp.bfloat16)


def first_kernel(ins, outs, tok_held, grad_held):
    place = Place()
    block, *blocks = ins[: NZ + 1]
    weights, messages = ins[NZ + 1 :], outs[2:]
    rows = block.shape[1]
    pieces = place.first()
    for i, held in enumerate((tok_held, grad_held)):
        acts = outs[i]
        acts[:rows] = jnp.where(place.core == 0, block[i], blocks[0][i])
        for k in range(1, NZ):
            acts[k * rows : (k + 1) * rows] = blocks[k][i]
        for slot, rows_at in enumerate(pieces):
            held[slot * PIECE : (slot + 1) * PIECE, :] = acts[rows_at, :]
    for which in range(3):
        held, transposed = ((tok_held, False), (grad_held, True))[which // 2]
        pair = weights[2 * which : 2 * which + 2]
        for at, end in spans(messages[0].shape[2]):
            total = pair_product(held, pair, at, end, transposed).astype(jnp.bfloat16)
            for i, message in enumerate(messages):
                message[which, :, at:end] = total[i * 2 * PIECE : (i + 1) * 2 * PIECE]


def partial_kernel(ins, outs, tok_held, grad_held):
    pieces = Place().second()
    for i, held in enumerate((tok_held, grad_held)):
        rows = ins[i]
        for slot, rows_at in enumerate(pieces):
            held[slot * PIECE : (slot + 1) * PIECE, :] = rows[rows_at, :]
        own, away = outs[1 + i], outs[3 + i]
        half = own.shape[1]
        own[...] = rows[:, :half]
        away[...] = rows[:, half:]
    for which in range(3):
        held, transposed = ((tok_held, False), (grad_held, True))[which // 2]
        pair = ins[2 + 2 * which : 4 + 2 * which]
        for at, end in spans(outs[0].shape[2]):
            outs[0][which, :, at:end] = pair_product(held, pair, at, end, transposed)


def second_kernel(ins, outs):
    place = Place()
    products, *heard = ins
    near, far = place.half(place.x), place.half(place.other)
    one = place.core == 1
    for which in range(3):
        for at, end in spans(outs[0].shape[2]):
            near2 = heard[1][which, near, at:end].astype(jnp.float32)
            far1, far2, far3 = [h[which, far, at:end].astype(jnp.float32) for h in heard]
            part1, part2, part3 = [
                products[which, slot * PIECE : (slot + 1) * PIECE, at:end] for slot in range(3)
            ]
            sum1 = part1 + far1 + jnp.where(one, far2 + far3, 0.0)
            high = sum1.astype(jnp.bfloat16)
            rest = sum1 - high.astype(jnp.float32)
            outs[0][which, :, at:end] = high
            outs[1][which, :, at:end] = jnp.where(one, rest, part2 + near2).astype(jnp.bfloat16)
            outs[2][which, :, at:end] = (part3 + far2).astype(jnp.bfloat16)


def unit_kernel(ins, outs):
    place = Place()
    products, first, second = ins[0], ins[1:4], ins[4:7]
    hidden, both = outs
    near, one = place.half(place.x), place.core == 1
    for at, end in spans(hidden.shape[1]):

        def summed(which):
            near1, near2, near3 = [h[which, near, at:end].astype(jnp.float32) for h in first]
            total = products[which, 3 * PIECE :, at:end] + near1
            total = total + jnp.where(one, near2 + near3, 0.0)
            return total + sum(h[which, :, at:end].astype(jnp.float32) for h in second)

        gate, up, d_hidden = [summed(which) for which in range(3)]
        sig_gate = jax.nn.sigmoid(gate)
        hidden[:, at:end] = (gate * sig_gate * up).astype(jnp.bfloat16)
        slope = d_hidden * up * sig_gate * (1.0 + gate * (1.0 - sig_gate))
        both[0, :, at:end] = slope.astype(jnp.bfloat16)
        both[1, :, at:end] = (d_hidden * gate * sig_gate).astype(jnp.bfloat16)


def weave_kernel(ins, outs):
    core = Place().core
    for rows, at_core in zip(ins, (core, 1 - core)):
        for piece in range(NY * NX):
            start = pl.multiple_of((piece * NC + at_core) * PIECE, PIECE)
            outs[0][pl.ds(start, PIECE), :] = rows[piece * PIECE : (piece + 1) * PIECE, :]


def pack_kernel(ins, outs):
    own, near1, near2, near3 = ins
    first, second = outs
    core0 = Place().core == 0
    first[:, :PIECE] = own[...]
    first[:, PIECE:] = near1[...]
    second[:, :PIECE] = jnp.where(core0, near2[...], own[...])
    second[:, PIECE:] = jnp.where(core0, near3[...], near1[...])


def layer_kernel(ins, outs, held):
    hidden, *weights = ins
    core = Place().core
    width = weights[0].shape[1]
    for piece in range(NY * NX):
        start = pl.multiple_of((piece * NC + core) * PIECE, PIECE)
        held[piece * PIECE : (piece + 1) * PIECE, :] = hidden[pl.ds(start, PIECE), :]
    for side, weight in enumerate(weights):
        for at, end in spans(width):
            outs[0][:, side * width + at : side * width + end] = product(
                held[...], weight[:, at:end], False
            )


def input_kernel(ins, outs):
    place = Place()
    layer, own, near1, near2, near3, far1, far2, far3 = ins[:8]
    weights = ins[8:]
    *messages, d_set, kept = outs
    core0 = place.core == 0
    pieces = place.gathered()
    values = [own[...], near1[...], far1[:, :PIECE], far1[:, PIECE:], far2[:, :PIECE], far2[:, PIECE:]]
    values.append(jnp.where(core0, near2[...], far3[:, :PIECE]))
    values.append(jnp.where(core0, near3[...], far3[:, PIECE:]))
    for rows_at, value in zip(pieces, values):
        d_set[:, rows_at, :] = value
    depth = weights[0].shape[0]
    block = NX * PIECE
    for side in range(2):
        for at, end in spans(depth):
            gate, up = [weights[2 * side + i][at:end, :] for i in range(2)]
            total = product(d_set[0], gate, True) + product(d_set[1], up, True)
            columns = slice(side * depth + at, side * depth + end)
            for i, term in enumerate((layer[:, columns], total)):
                kept[i, :, columns] = term[:block]
                for k in range(NZ):
                    rows = term[k * block : (k + 1) * block]
                    messages[k][i, :, columns] = rows.astype(jnp.bfloat16)


def send_first(sent):
    return (
        lax.ppermute(sent[0], "row", row_perm(over_x, over_y(1))),
        lax.ppermute(sent[1], "row", row_perm(over_x, over_y(-1))),
        lax.ppermute(sent[2], "row", row_perm(None, over_y(2))),
    )


def send_second(sent):
    return (
        lax.ppermute(sent[0], "row", row_perm(over_y(1), over_x)),
        lax.ppermute(sent[1], "row", row_perm(over_y(-1), over_x)),
        lax.ppermute(sent[2], "row", row_perm(over_y(2), None)),
    )


def body(tokens, gate_weight, up_weight, down_weight, grad_output):
    core = lax.axis_index("row") % NC
    flip = lambda value: lax.ppermute(value, "row", CORE_FLIP)
    after = lambda value, *others: lax.optimization_barrier((value, *others))[0]
    width, ff_width = gate_weight.shape
    half_rows = NY * NX * PIECE
    rows = tokens.shape[0]

    tok_theirs, grad_theirs = flip(tokens), flip(grad_output)
    (mine,) = call(mine_kernel, [tokens, grad_output], [shape((2, rows, width))])
    (own_block,) = call(
        block_kernel, [mine, tok_theirs, grad_theirs], [shape((2, rows, 2 * width))]
    )
    to_flip = lax.optimization_barrier((gate_weight, up_weight, down_weight, tok_theirs, grad_theirs))
    gate_other, up_other, down_other = [flip(weight) for weight in to_flip[:3]]
    own = lax.optimization_barrier((gate_weight, up_weight, down_weight, own_block))[:3]
    gate_own, up_own, down_own = call(keep_kernel, own, [shape(weight.shape) for weight in own])
    early = own_block
    late = [after(own_block, gate_other, gate_own), after(own_block, up_other, gate_own)]
    starts = [late[1], early, late[0], early]
    blocks = [lax.ppermute(starts[step], BOTH, gather_perm(step)) for step in range(NZ)]

    weights = [gate_own, gate_other, up_own, up_other, down_own, down_other]
    held = lambda pieces: [pltpu.VMEM((pieces * PIECE, 2 * width), jnp.bfloat16)] * 2
    tok_half, grad_half, *sent = call(
        first_kernel,
        [own_block, *blocks, *weights],
        [shape((half_rows, 2 * width))] * 2 + [shape((3, 2 * PIECE, ff_width))] * 3,
        held(6),
    )
    heard = send_first(sent)
    products, tok_own, grad_own, tok_away, grad_away = call(
        partial_kernel,
        [tok_half, grad_half, *weights],
        [shape((3, 4 * PIECE, ff_width), jnp.float32)] + [shape((half_rows, width))] * 4,
        held(4),
    )
    tok_other, grad_other = flip(tok_away), flip(grad_away)
    (grad_all,) = call(weave_kernel, [grad_own, grad_other], [shape((2 * half_rows, width))])
    *heard, grad_all, tok_other = lax.optimization_barrier((*heard, grad_all, tok_other))
    sent = call(second_kernel, [products, *heard], [shape((3, PIECE, ff_width))] * 3)
    hidden, d_own = call(
        unit_kernel,
        [products, *heard, *send_second(sent)],
        [shape((PIECE, ff_width)), shape((2, PIECE, ff_width))],
    )
    hidden = lax.all_gather(hidden, "row", axis=0, tiled=True)

    near = send_second([d_own] * 3)
    first, second = call(pack_kernel, [d_own, *near], [shape((2, 2 * PIECE, ff_width))] * 2)
    far = send_first([first, second, first])
    hidden = after(hidden, far[0])
    (layer,) = call(
        layer_kernel,
        [hidden, down_weight, down_other],
        [shape((half_rows, 2 * width), jnp.float32)],
        [pltpu.VMEM((half_rows, ff_width), jnp.bfloat16)],
    )
    block = (2, rows, 2 * width)
    *messages, d_set, kept = call(
        input_kernel,
        [layer, d_own, *near, *far, gate_weight, up_weight, gate_other, up_other],
        [shape(block)] * 4 + [shape((2, half_rows, ff_width)), shape(block, jnp.float32)],
    )
    messages = [lax.ppermute(messages[k], BOTH, scatter_perm(k)) for k in range(NZ)]
    grad_gate, grad_up = call(
        gradient_kernel,
        [tok_own, tok_other, d_set, flip(d_set)],
        [shape((width, ff_width))] * 2,
    )
    grad_down = lax.dot_general(
        hidden, grad_all, (((0,), (0,)), ((), ())), preferred_element_type=jnp.float32
    ).astype(jnp.bfloat16)
    *messages, grad_gate, grad_up = lax.optimization_barrier((*messages, grad_gate, grad_up))
    total = jnp.where(core == 0, kept, 0.0)
    for message in messages:
        total = total + message.astype(jnp.float32)
    total = (total[:, :, :width] + flip(total[:, :, width:])).astype(jnp.bfloat16)
    return (total[0], total[1], grad_gate, grad_up, grad_down)


def solution(mesh):
    placed = (P("col", "row"), P("row", "col"), P("row", "col"), P("col", "row"), P("col", "row"))
    return jax.shard_map(
        body,
        mesh=mesh,
        in_specs=placed,
        out_specs=(
            P("col", "row"),
            P("col", "row"),
            P("row", "col"),
            P("row", "col"),
            P("col", "row"),
        ),
        check_vma=False,
    )
```

```python
import functools

import jax
import jax.numpy as jnp
from jax import lax
from jax.experimental import pallas as pl
from jax.experimental.pallas import tpu as pltpu
from jax.sharding import PartitionSpec as P

NY, NX, NC, NZ = 4, 2, 2, 4
PIECE = 64
BOTH = ("row", "col")


def row_at(y, x, core):
    return ((y % NY) * NX + x) * NC + core


def row_perm(core0, core1):
    pairs = []
    for y in range(NY):
        for x in range(NX):
            for core, move in ((0, core0), (1, core1)):
                if move is not None:
                    to_y, to_x = move(y, x)
                    pairs.append((row_at(y, x, core), row_at(to_y, to_x, core)))
    return pairs


def over_x(y, x):
    return y, 1 - x


def over_y(step):
    return lambda y, x: (y + step, x)


CORE_FLIP = [(i, i ^ 1) for i in range(NY * NX * NC)]


def gather_perm(step):
    pairs = []
    for row in range(NY * NX * NC):
        core = row % NC
        if core == 0 and step == 0:
            continue
        for hi in range(2):
            for z in range(NZ):
                source = (hi ^ core) * NZ + (z + step) % NZ
                pairs.append((row * 8 + source, row * 8 + hi * NZ + z))
    return pairs


def scatter_perm(step):
    return [(to, source) for source, to in gather_perm(step)]


def product(left, right, transposed):
    dims = (((1,), (1 if transposed else 0,)), ((), ()))
    return lax.dot_general(left, right, dims, preferred_element_type=jnp.float32)


def spans(width):
    return [(at, min(at + 256, width)) for at in range(0, width, 256)]


def shape(dims, dtype=jnp.bfloat16):
    return jax.ShapeDtypeStruct(dims, dtype)


def call(kernel, operands, out_shape, scratch=()):
    n_in, n_out = len(operands), len(out_shape)

    def run(*refs):
        kernel(refs[:n_in], refs[n_in : n_in + n_out], *refs[n_in + n_out :])

    vmem = pl.BlockSpec(memory_space=pltpu.VMEM)
    return pl.pallas_call(
        run,
        in_specs=[vmem] * n_in,
        out_specs=[vmem] * n_out,
        out_shape=out_shape,
        scratch_shapes=scratch,
        compiler_params=pltpu.CompilerParams(vmem_limit_bytes=12 * 2**20),
        cost_estimate=pl.CostEstimate(flops=1, bytes_accessed=1, transcendentals=0),
    )(*operands)


class Place:
    def __init__(self):
        row = lax.axis_index("row")
        self.core, self.x, self.y = row % NC, (row // NC) % NX, row // (NC * NX)
        self.other = 1 - self.x

    def piece(self, step, x):
        return ((self.y + step) % NY) * NX + x

    def choose(self, core0, core1):
        pieces = [jnp.where(self.core == 0, self.piece(*a), self.piece(*b)) for a, b in zip(core0, core1)]
        return [pl.ds(pl.multiple_of(piece * PIECE, PIECE), PIECE) for piece in pieces]

    def first(self):
        o = self.other
        core0 = [(o, o), (1 - o, o), (3 - o, o), (2 + o, o), (0, self.x), (0, self.x)]
        return self.choose(core0, [(step, x) for step in (1, 3, 2) for x in (0, 1)])

    def second(self):
        x, o = self.x, self.other
        return self.choose([(1, x), (3, x), (2, x), (0, x)], [(0, o), (0, x), (0, x), (0, x)])

    def gathered(self):
        x, o = self.x, self.other
        core0 = [(0, x), (3, x), (0, o), (3, o), (1, o), (2, o), (1, x), (2, x)]
        return self.choose(core0, [(0, x), (0, o)] + [(step, at) for step in (3, 1, 2) for at in (x, o)])

    def half(self, x):
        return pl.ds(pl.multiple_of(x * PIECE, PIECE), PIECE)


def pair_product(held, pair, at, end, transposed):
    half = held.shape[1] // 2
    chunk = (slice(at, end), slice(None)) if transposed else (slice(None), slice(at, end))
    own, other = [ref[chunk] for ref in pair]
    return product(held[:, :half], own, transposed) + product(held[:, half:], other, transposed)


def mine_kernel(ins, outs):
    for i in range(2):
        outs[0][i] = ins[i][...]


def block_kernel(ins, outs):
    mine, *theirs = ins
    (block,) = outs
    half = block.shape[2] // 2
    for i in range(2):
        block[i, :, :half] = mine[i]
        block[i, :, half:] = theirs[i][...]


def keep_kernel(ins, outs):
    for source, out in zip(ins, outs):
        out[...] = source[...]


def gradient_kernel(ins, outs, own_turned, other_turned):
    tok_own, tok_other, d_own, d_other = ins
    own_turned[...] = tok_own[...].T
    other_turned[...] = tok_other[...].T
    for i, out in enumerate(outs):
        for at, end in spans(out.shape[1]):
            total = product(own_turned[...], d_own[i, :, at:end], False)
            total += product(other_turned[...], d_other[i, :, at:end], False)
            out[:, at:end] = total.astype(jnp.bfloat16)


def down_kernel(ins, outs):
    hidden, grad_all = ins
    for at, end in spans(hidden.shape[1]):
        total = product(hidden[:, at:end].T, grad_all[...], False)
        outs[0][at:end, :] = total.astype(jnp.bfloat16)


def first_kernel(ins, outs, tok_held, grad_held):
    place = Place()
    block, *blocks = ins[: NZ + 1]
    weights, messages = ins[NZ + 1 :], outs[2:]
    rows = block.shape[1]
    pieces = place.first()
    for i, held in enumerate((tok_held, grad_held)):
        acts = outs[i]
        acts[:rows] = jnp.where(place.core == 0, block[i], blocks[0][i])
        for k in range(1, NZ):
            acts[k * rows : (k + 1) * rows] = blocks[k][i]
        for slot, rows_at in enumerate(pieces):
            held[slot * PIECE : (slot + 1) * PIECE, :] = acts[rows_at, :]
    for which in range(3):
        held, transposed = ((tok_held, False), (grad_held, True))[which // 2]
        pair = weights[2 * which : 2 * which + 2]
        for at, end in spans(messages[0].shape[2]):
            total = pair_product(held, pair, at, end, transposed).astype(jnp.bfloat16)
            for i, message in enumerate(messages):
                message[which, :, at:end] = total[i * 2 * PIECE : (i + 1) * 2 * PIECE]


def partial_kernel(ins, outs, tok_held, grad_held):
    pieces = Place().second()
    for i, held in enumerate((tok_held, grad_held)):
        rows = ins[i]
        for slot, rows_at in enumerate(pieces):
            held[slot * PIECE : (slot + 1) * PIECE, :] = rows[rows_at, :]
        own, away = outs[1 + i], outs[3 + i]
        half = own.shape[1]
        own[...] = rows[:, :half]
        away[...] = rows[:, half:]
    for which in range(3):
        held, transposed = ((tok_held, False), (grad_held, True))[which // 2]
        pair = ins[2 + 2 * which : 4 + 2 * which]
        for at, end in spans(outs[0].shape[2]):
            outs[0][which, :, at:end] = pair_product(held, pair, at, end, transposed)


def second_kernel(ins, outs):
    place = Place()
    products, *heard = ins
    near, far = place.half(place.x), place.half(place.other)
    one = place.core == 1
    for which in range(3):
        for at, end in spans(outs[0].shape[2]):
            near2 = heard[1][which, near, at:end].astype(jnp.float32)
            far1, far2, far3 = [h[which, far, at:end].astype(jnp.float32) for h in heard]
            part1, part2, part3 = [
                products[which, slot * PIECE : (slot + 1) * PIECE, at:end] for slot in range(3)
            ]
            sum1 = part1 + far1 + jnp.where(one, far2 + far3, 0.0)
            high = sum1.astype(jnp.bfloat16)
            rest = sum1 - high.astype(jnp.float32)
            outs[0][which, :, at:end] = high
            outs[1][which, :, at:end] = jnp.where(one, rest, part2 + near2).astype(jnp.bfloat16)
            outs[2][which, :, at:end] = (part3 + far2).astype(jnp.bfloat16)


def unit_kernel(ins, outs):
    place = Place()
    products, first, second = ins[0], ins[1:4], ins[4:7]
    hidden, both = outs
    near, one = place.half(place.x), place.core == 1
    for at, end in spans(hidden.shape[1]):

        def summed(which):
            near1, near2, near3 = [h[which, near, at:end].astype(jnp.float32) for h in first]
            total = products[which, 3 * PIECE :, at:end] + near1
            total = total + jnp.where(one, near2 + near3, 0.0)
            return total + sum(h[which, :, at:end].astype(jnp.float32) for h in second)

        gate, up, d_hidden = [summed(which) for which in range(3)]
        sig_gate = jax.nn.sigmoid(gate)
        hidden[:, at:end] = (gate * sig_gate * up).astype(jnp.bfloat16)
        slope = d_hidden * up * sig_gate * (1.0 + gate * (1.0 - sig_gate))
        both[0, :, at:end] = slope.astype(jnp.bfloat16)
        both[1, :, at:end] = (d_hidden * gate * sig_gate).astype(jnp.bfloat16)


def weave_kernel(ins, outs):
    core = Place().core
    for rows, at_core in zip(ins, (core, 1 - core)):
        for piece in range(NY * NX):
            start = pl.multiple_of((piece * NC + at_core) * PIECE, PIECE)
            outs[0][pl.ds(start, PIECE), :] = rows[piece * PIECE : (piece + 1) * PIECE, :]


def pack_kernel(ins, outs):
    own, near1, near2, near3 = ins
    first, second = outs
    core0 = Place().core == 0
    first[:, :PIECE] = own[...]
    first[:, PIECE:] = near1[...]
    second[:, :PIECE] = jnp.where(core0, near2[...], own[...])
    second[:, PIECE:] = jnp.where(core0, near3[...], near1[...])


def layer_kernel(ins, outs, held):
    hidden, *weights = ins
    core = Place().core
    width = weights[0].shape[1]
    for piece in range(NY * NX):
        start = pl.multiple_of((piece * NC + core) * PIECE, PIECE)
        held[piece * PIECE : (piece + 1) * PIECE, :] = hidden[pl.ds(start, PIECE), :]
    for side, weight in enumerate(weights):
        for at, end in spans(width):
            outs[0][:, side * width + at : side * width + end] = product(
                held[...], weight[:, at:end], False
            )


def input_kernel(ins, outs):
    place = Place()
    layer, own, near1, near2, near3, far1, far2, far3 = ins[:8]
    weights = ins[8:]
    *messages, d_set, kept = outs
    core0 = place.core == 0
    pieces = place.gathered()
    values = [own[...], near1[...], far1[:, :PIECE], far1[:, PIECE:], far2[:, :PIECE], far2[:, PIECE:]]
    values.append(jnp.where(core0, near2[...], far3[:, :PIECE]))
    values.append(jnp.where(core0, near3[...], far3[:, PIECE:]))
    for rows_at, value in zip(pieces, values):
        d_set[:, rows_at, :] = value
    depth = weights[0].shape[0]
    block = NX * PIECE
    for side in range(2):
        for at, end in spans(depth):
            gate, up = [weights[2 * side + i][at:end, :] for i in range(2)]
            total = product(d_set[0], gate, True) + product(d_set[1], up, True)
            columns = slice(side * depth + at, side * depth + end)
            for i, term in enumerate((layer[:, columns], total)):
                kept[i, :, columns] = term[:block]
                for k in range(NZ):
                    rows = term[k * block : (k + 1) * block]
                    messages[k][i, :, columns] = rows.astype(jnp.bfloat16)


def send_first(sent):
    return (
        lax.ppermute(sent[0], "row", row_perm(over_x, over_y(1))),
        lax.ppermute(sent[1], "row", row_perm(over_x, over_y(-1))),
        lax.ppermute(sent[2], "row", row_perm(None, over_y(2))),
    )


def send_second(sent):
    third = lax.ppermute(sent[2], "row", row_perm(over_y(2), None))
    first = lax.ppermute(sent[0], "row", row_perm(over_y(1), over_x))
    return first, lax.ppermute(sent[1], "row", row_perm(over_y(-1), over_x)), third


def body(tokens, gate_weight, up_weight, down_weight, grad_output):
    core = lax.axis_index("row") % NC
    flip = lambda value: lax.ppermute(value, "row", CORE_FLIP)
    after = lambda value, *others: lax.optimization_barrier((value, *others))[0]
    width, ff_width = gate_weight.shape
    half_rows = NY * NX * PIECE
    rows = tokens.shape[0]

    tok_theirs, grad_theirs = flip(tokens), flip(grad_output)
    (mine,) = call(mine_kernel, [tokens, grad_output], [shape((2, rows, width))])
    (own_block,) = call(
        block_kernel, [mine, tok_theirs, grad_theirs], [shape((2, rows, 2 * width))]
    )
    to_flip = lax.optimization_barrier((gate_weight, up_weight, down_weight, tok_theirs, grad_theirs))
    gate_other, up_other, down_other = [flip(weight) for weight in to_flip[:3]]
    own = lax.optimization_barrier((gate_weight, up_weight, down_weight, own_block))[:3]
    gate_own, up_own, down_own = call(keep_kernel, own, [shape(weight.shape) for weight in own])
    early = own_block
    late = [after(own_block, gate_other, gate_own), after(own_block, up_other, gate_own)]
    starts = [late[1], early, late[0], early]
    blocks = [lax.ppermute(starts[step], BOTH, gather_perm(step)) for step in range(NZ)]

    weights = [gate_own, gate_other, up_own, up_other, down_own, down_other]
    held = lambda pieces: [pltpu.VMEM((pieces * PIECE, 2 * width), jnp.bfloat16)] * 2
    tok_half, grad_half, *sent = call(
        first_kernel,
        [own_block, *blocks, *weights],
        [shape((half_rows, 2 * width))] * 2 + [shape((3, 2 * PIECE, ff_width))] * 3,
        held(6),
    )
    heard = send_first(sent)
    products, tok_own, grad_own, tok_away, grad_away = call(
        partial_kernel,
        [tok_half, grad_half, *weights],
        [shape((3, 4 * PIECE, ff_width), jnp.float32)] + [shape((half_rows, width))] * 4,
        held(4),
    )
    tok_other, grad_other = flip(tok_away), flip(grad_away)
    (grad_all,) = call(weave_kernel, [grad_own, grad_other], [shape((2 * half_rows, width))])
    *heard, grad_all, tok_other = lax.optimization_barrier((*heard, grad_all, tok_other))
    sent = call(second_kernel, [products, *heard], [shape((3, PIECE, ff_width))] * 3)
    hidden, d_own = call(
        unit_kernel,
        [products, *heard, *send_second(sent)],
        [shape((PIECE, ff_width)), shape((2, PIECE, ff_width))],
    )
    hidden = lax.all_gather(hidden, "row", axis=0, tiled=True)

    near = send_second([d_own] * 3)
    first, second = call(pack_kernel, [d_own, *near], [shape((2, 2 * PIECE, ff_width))] * 2)
    far = send_first([first, second, first])
    hidden = after(hidden, far[0])
    (layer,) = call(
        layer_kernel,
        [hidden, down_weight, down_other],
        [shape((half_rows, 2 * width), jnp.float32)],
        [pltpu.VMEM((half_rows, ff_width), jnp.bfloat16)],
    )
    block = (2, rows, 2 * width)
    *messages, d_set, kept = call(
        input_kernel,
        [layer, d_own, *near, *far, gate_weight, up_weight, gate_other, up_other],
        [shape(block)] * 4 + [shape((2, half_rows, ff_width)), shape(block, jnp.float32)],
    )
    heard = {k: lax.ppermute(messages[k], BOTH, scatter_perm(k)) for k in (2, 1, 3, 0)}
    messages = [heard[k] for k in range(NZ)]
    grad_gate, grad_up = call(
        gradient_kernel,
        [tok_own, tok_other, d_set, flip(d_set)],
        [shape((width, ff_width))] * 2,
        [pltpu.VMEM((width, half_rows), jnp.bfloat16)] * 2,
    )
    (grad_down,) = call(down_kernel, [hidden, grad_all], [shape((ff_width, width))])
    *messages, grad_gate, grad_up, grad_down = lax.optimization_barrier(
        (*messages, grad_gate, grad_up, grad_down)
    )
    total = jnp.where(core == 0, kept, 0.0)
    for message in messages:
        total = total + message.astype(jnp.float32)
    total = (total[:, :, :width] + flip(total[:, :, width:])).astype(jnp.bfloat16)
    return (total[0], total[1], grad_gate, grad_up, grad_down)


def solution(mesh):
    placed = (P("col", "row"), P("row", "col"), P("row", "col"), P("col", "row"), P("col", "row"))
    return jax.shard_map(
        body,
        mesh=mesh,
        in_specs=placed,
        out_specs=(
            P("col", "row"),
            P("col", "row"),
            P("row", "col"),
            P("row", "col"),
            P("col", "row"),
        ),
        check_vma=False,
    )
```

```python
import functools

import jax
import jax.numpy as jnp
from jax import lax
from jax.experimental import pallas as pl
from jax.experimental.pallas import tpu as pltpu
from jax.sharding import PartitionSpec as P

NY, NX, NC, NZ = 4, 2, 2, 4
PIECE = 64
BOTH = ("row", "col")


def row_at(y, x, core):
    return ((y % NY) * NX + x) * NC + core


def row_perm(core0, core1):
    pairs = []
    for y in range(NY):
        for x in range(NX):
            for core, move in ((0, core0), (1, core1)):
                if move is not None:
                    to_y, to_x = move(y, x)
                    pairs.append((row_at(y, x, core), row_at(to_y, to_x, core)))
    return pairs


def over_x(y, x):
    return y, 1 - x


def over_y(step):
    return lambda y, x: (y + step, x)


CORE_FLIP = [(i, i ^ 1) for i in range(NY * NX * NC)]


def gather_perm(step):
    pairs = []
    for row in range(NY * NX * NC):
        core = row % NC
        if core == 0 and step == 0:
            continue
        for hi in range(2):
            for z in range(NZ):
                source = (hi ^ core) * NZ + (z + step) % NZ
                pairs.append((row * 8 + source, row * 8 + hi * NZ + z))
    return pairs


def scatter_perm(step):
    return [(to, source) for source, to in gather_perm(step)]


def product(left, right, transposed):
    dims = (((1,), (1 if transposed else 0,)), ((), ()))
    return lax.dot_general(left, right, dims, preferred_element_type=jnp.float32)


def spans(width):
    return [(at, min(at + 256, width)) for at in range(0, width, 256)]


def shape(dims, dtype=jnp.bfloat16):
    return jax.ShapeDtypeStruct(dims, dtype)


def call(kernel, operands, out_shape, scratch=()):
    n_in, n_out = len(operands), len(out_shape)

    def run(*refs):
        kernel(refs[:n_in], refs[n_in : n_in + n_out], *refs[n_in + n_out :])

    vmem = pl.BlockSpec(memory_space=pltpu.VMEM)
    return pl.pallas_call(
        run,
        in_specs=[vmem] * n_in,
        out_specs=[vmem] * n_out,
        out_shape=out_shape,
        scratch_shapes=scratch,
        compiler_params=pltpu.CompilerParams(vmem_limit_bytes=12 * 2**20),
        cost_estimate=pl.CostEstimate(flops=1, bytes_accessed=1, transcendentals=0),
    )(*operands)


class Place:
    def __init__(self):
        row = lax.axis_index("row")
        self.core, self.x, self.y = row % NC, (row // NC) % NX, row // (NC * NX)
        self.other = 1 - self.x

    def piece(self, step, x):
        return ((self.y + step) % NY) * NX + x

    def choose(self, core0, core1):
        pieces = [jnp.where(self.core == 0, self.piece(*a), self.piece(*b)) for a, b in zip(core0, core1)]
        return [pl.ds(pl.multiple_of(piece * PIECE, PIECE), PIECE) for piece in pieces]

    def first(self):
        o = self.other
        core0 = [(o, o), (1 - o, o), (3 - o, o), (2 + o, o), (0, self.x), (0, self.x)]
        return self.choose(core0, [(step, x) for step in (1, 3, 2) for x in (0, 1)])

    def second(self):
        x, o = self.x, self.other
        return self.choose([(1, x), (3, x), (2, x), (0, x)], [(0, o), (0, x), (0, x), (0, x)])

    def gathered(self):
        x, o = self.x, self.other
        core0 = [(0, x), (3, x), (0, o), (3, o), (1, o), (2, o), (1, x), (2, x)]
        return self.choose(core0, [(0, x), (0, o)] + [(step, at) for step in (3, 1, 2) for at in (x, o)])

    def half(self, x):
        return pl.ds(pl.multiple_of(x * PIECE, PIECE), PIECE)


def pair_product(held, pair, at, end, transposed):
    half = held.shape[1] // 2
    chunk = (slice(at, end), slice(None)) if transposed else (slice(None), slice(at, end))
    own, other = [ref[chunk] for ref in pair]
    return product(held[:, :half], own, transposed) + product(held[:, half:], other, transposed)


def mine_kernel(ins, outs):
    for i in range(2):
        outs[0][i] = ins[i][...]


def block_kernel(ins, outs):
    mine, *theirs = ins
    (block,) = outs
    half = block.shape[2] // 2
    for i in range(2):
        block[i, :, :half] = mine[i]
        block[i, :, half:] = theirs[i][...]


def keep_kernel(ins, outs):
    for source, out in zip(ins, outs):
        out[...] = source[...]


def gradient_kernel(ins, outs, own_turned, other_turned):
    tok_own, tok_other, d_own, d_other = ins
    own_turned[...] = tok_own[...].T
    other_turned[...] = tok_other[...].T
    for i, out in enumerate(outs):
        for at, end in spans(out.shape[1]):
            total = product(own_turned[...], d_own[i, :, at:end], False)
            total += product(other_turned[...], d_other[i, :, at:end], False)
            out[:, at:end] = total.astype(jnp.bfloat16)


def down_kernel(ins, outs):
    hidden, grad_all = ins
    for at, end in spans(hidden.shape[1]):
        total = product(hidden[:, at:end].T, grad_all[...], False)
        outs[0][at:end, :] = total.astype(jnp.bfloat16)


def first_kernel(ins, outs, tok_held, grad_held):
    place = Place()
    block, *blocks = ins[: NZ + 1]
    weights, messages = ins[NZ + 1 :], outs[2:]
    rows = block.shape[1]
    pieces = place.first()
    for i, held in enumerate((tok_held, grad_held)):
        acts = outs[i]
        acts[:rows] = jnp.where(place.core == 0, block[i], blocks[0][i])
        for k in range(1, NZ):
            acts[k * rows : (k + 1) * rows] = blocks[k][i]
        for slot, rows_at in enumerate(pieces):
            held[slot * PIECE : (slot + 1) * PIECE, :] = acts[rows_at, :]
    for which in range(3):
        held, transposed = ((tok_held, False), (grad_held, True))[which // 2]
        pair = weights[2 * which : 2 * which + 2]
        for at, end in spans(messages[0].shape[2]):
            total = pair_product(held, pair, at, end, transposed).astype(jnp.bfloat16)
            for i, message in enumerate(messages):
                message[which, :, at:end] = total[i * 2 * PIECE : (i + 1) * 2 * PIECE]


def partial_kernel(ins, outs, tok_held, grad_held):
    pieces = Place().second()
    for i, held in enumerate((tok_held, grad_held)):
        rows = ins[i]
        for slot, rows_at in enumerate(pieces):
            held[slot * PIECE : (slot + 1) * PIECE, :] = rows[rows_at, :]
        own, away = outs[1 + i], outs[3 + i]
        half = own.shape[1]
        own[...] = rows[:, :half]
        away[...] = rows[:, half:]
    for which in range(3):
        held, transposed = ((tok_held, False), (grad_held, True))[which // 2]
        pair = ins[2 + 2 * which : 4 + 2 * which]
        for at, end in spans(outs[0].shape[2]):
            outs[0][which, :, at:end] = pair_product(held, pair, at, end, transposed)


def second_kernel(ins, outs):
    place = Place()
    products, *heard = ins
    near, far = place.half(place.x), place.half(place.other)
    one = place.core == 1
    for which in range(3):
        for at, end in spans(outs[0].shape[2]):
            near2 = heard[1][which, near, at:end].astype(jnp.float32)
            far1, far2, far3 = [h[which, far, at:end].astype(jnp.float32) for h in heard]
            part1, part2, part3 = [
                products[which, slot * PIECE : (slot + 1) * PIECE, at:end] for slot in range(3)
            ]
            sum1 = part1 + far1 + jnp.where(one, far2 + far3, 0.0)
            high = sum1.astype(jnp.bfloat16)
            rest = sum1 - high.astype(jnp.float32)
            outs[0][which, :, at:end] = high
            outs[1][which, :, at:end] = jnp.where(one, rest, part2 + near2).astype(jnp.bfloat16)
            outs[2][which, :, at:end] = (part3 + far2).astype(jnp.bfloat16)


def unit_kernel(ins, outs):
    place = Place()
    products, first, second = ins[0], ins[1:4], ins[4:7]
    hidden, both = outs
    near, one = place.half(place.x), place.core == 1
    for at, end in spans(hidden.shape[1]):

        def summed(which):
            near1, near2, near3 = [h[which, near, at:end].astype(jnp.float32) for h in first]
            total = products[which, 3 * PIECE :, at:end] + near1
            total = total + jnp.where(one, near2 + near3, 0.0)
            return total + sum(h[which, :, at:end].astype(jnp.float32) for h in second)

        gate, up, d_hidden = [summed(which) for which in range(3)]
        sig_gate = jax.nn.sigmoid(gate)
        hidden[:, at:end] = (gate * sig_gate * up).astype(jnp.bfloat16)
        slope = d_hidden * up * sig_gate * (1.0 + gate * (1.0 - sig_gate))
        both[0, :, at:end] = slope.astype(jnp.bfloat16)
        both[1, :, at:end] = (d_hidden * gate * sig_gate).astype(jnp.bfloat16)


def weave_kernel(ins, outs):
    core = Place().core
    for rows, at_core in zip(ins, (core, 1 - core)):
        for piece in range(NY * NX):
            start = pl.multiple_of((piece * NC + at_core) * PIECE, PIECE)
            outs[0][pl.ds(start, PIECE), :] = rows[piece * PIECE : (piece + 1) * PIECE, :]


def pack_kernel(ins, outs):
    own, near1, near2, near3 = ins
    first, second, third = outs
    core0 = Place().core == 0
    for out in (first, third):
        out[:, :PIECE] = own[...]
        out[:, PIECE:] = near1[...]
    second[:, :PIECE] = jnp.where(core0, near2[...], own[...])
    second[:, PIECE:] = jnp.where(core0, near3[...], near1[...])


def layer_kernel(ins, outs, held):
    hidden, *weights = ins
    core = Place().core
    width = weights[0].shape[1]
    for piece in range(NY * NX):
        start = pl.multiple_of((piece * NC + core) * PIECE, PIECE)
        held[piece * PIECE : (piece + 1) * PIECE, :] = hidden[pl.ds(start, PIECE), :]
    for side, weight in enumerate(weights):
        for at, end in spans(width):
            outs[0][:, side * width + at : side * width + end] = product(
                held[...], weight[:, at:end], False
            )


def input_kernel(ins, outs):
    place = Place()
    layer, own, near1, near2, near3, far1, far2, far3 = ins[:8]
    weights = ins[8:]
    *messages, d_set, kept = outs
    core0 = place.core == 0
    pieces = place.gathered()
    values = [own[...], near1[...], far1[:, :PIECE], far1[:, PIECE:], far2[:, :PIECE], far2[:, PIECE:]]
    values.append(jnp.where(core0, near2[...], far3[:, :PIECE]))
    values.append(jnp.where(core0, near3[...], far3[:, PIECE:]))
    for rows_at, value in zip(pieces, values):
        d_set[:, rows_at, :] = value
    depth = weights[0].shape[0]
    block = NX * PIECE
    for side in range(2):
        for at, end in spans(depth):
            gate, up = [weights[2 * side + i][at:end, :] for i in range(2)]
            total = product(d_set[0], gate, True) + product(d_set[1], up, True)
            columns = slice(side * depth + at, side * depth + end)
            for i, term in enumerate((layer[:, columns], total)):
                kept[i, :, columns] = term[:block]
                for k in range(NZ):
                    rows = term[k * block : (k + 1) * block]
                    messages[k][i, :, columns] = rows.astype(jnp.bfloat16)


def send_first(sent):
    return (
        lax.ppermute(sent[0], "row", row_perm(over_x, over_y(1))),
        lax.ppermute(sent[1], "row", row_perm(over_x, over_y(-1))),
        lax.ppermute(sent[2], "row", row_perm(None, over_y(2))),
    )


def send_second(sent, core1=over_x):
    third = lax.ppermute(sent[2], "row", row_perm(over_y(2), None))
    first = lax.ppermute(sent[0], "row", row_perm(over_y(1), over_x))
    return first, lax.ppermute(sent[1], "row", row_perm(over_y(-1), core1)), third


def body(tokens, gate_weight, up_weight, down_weight, grad_output):
    core = lax.axis_index("row") % NC
    flip = lambda value: lax.ppermute(value, "row", CORE_FLIP)
    after = lambda value, *others: lax.optimization_barrier((value, *others))[0]
    width, ff_width = gate_weight.shape
    half_rows = NY * NX * PIECE
    rows = tokens.shape[0]

    tok_theirs, grad_theirs = flip(tokens), flip(grad_output)
    (mine,) = call(mine_kernel, [tokens, grad_output], [shape((2, rows, width))])
    (own_block,) = call(
        block_kernel, [mine, tok_theirs, grad_theirs], [shape((2, rows, 2 * width))]
    )
    to_flip = lax.optimization_barrier((gate_weight, up_weight, down_weight, tok_theirs, grad_theirs))
    gate_other, up_other, down_other = [flip(weight) for weight in to_flip[:3]]
    own = lax.optimization_barrier((gate_weight, up_weight, down_weight, own_block))[:3]
    gate_own, up_own, down_own = call(keep_kernel, own, [shape(weight.shape) for weight in own])
    early = own_block
    late = [after(own_block, gate_other, gate_own), after(own_block, up_other, gate_own)]
    starts = [late[1], early, late[0], early]
    blocks = [lax.ppermute(starts[step], BOTH, gather_perm(step)) for step in range(NZ)]

    weights = [gate_own, gate_other, up_own, up_other, down_own, down_other]
    held = lambda pieces: [pltpu.VMEM((pieces * PIECE, 2 * width), jnp.bfloat16)] * 2
    tok_half, grad_half, *sent = call(
        first_kernel,
        [own_block, *blocks, *weights],
        [shape((half_rows, 2 * width))] * 2 + [shape((3, 2 * PIECE, ff_width))] * 3,
        held(6),
    )
    heard = send_first(sent)
    products, tok_own, grad_own, tok_away, grad_away = call(
        partial_kernel,
        [tok_half, grad_half, *weights],
        [shape((3, 4 * PIECE, ff_width), jnp.float32)] + [shape((half_rows, width))] * 4,
        held(4),
    )
    tok_other, grad_other = flip(tok_away), flip(grad_away)
    (grad_all,) = call(weave_kernel, [grad_own, grad_other], [shape((2 * half_rows, width))])
    *heard, grad_all, tok_other = lax.optimization_barrier((*heard, grad_all, tok_other))
    sent = call(second_kernel, [products, *heard], [shape((3, PIECE, ff_width))] * 3)
    hidden, d_own = call(
        unit_kernel,
        [products, *heard, *send_second(sent)],
        [shape((PIECE, ff_width)), shape((2, PIECE, ff_width))],
    )
    hidden = lax.all_gather(hidden, "row", axis=0, tiled=True)

    near = send_second([d_own] * 3, None)
    packed = call(pack_kernel, [d_own, *near], [shape((2, 2 * PIECE, ff_width))] * 3)
    far = send_first(packed)
    hidden = after(hidden, far[0])
    (layer,) = call(
        layer_kernel,
        [hidden, down_weight, down_other],
        [shape((half_rows, 2 * width), jnp.float32)],
        [pltpu.VMEM((half_rows, ff_width), jnp.bfloat16)],
    )
    block = (2, rows, 2 * width)
    *messages, d_set, kept = call(
        input_kernel,
        [layer, d_own, *near, *far, gate_weight, up_weight, gate_other, up_other],
        [shape(block)] * 4 + [shape((2, half_rows, ff_width)), shape(block, jnp.float32)],
    )
    heard = {k: lax.ppermute(messages[k], BOTH, scatter_perm(k)) for k in (2, 1, 3, 0)}
    messages = [heard[k] for k in range(NZ)]
    grad_gate, grad_up = call(
        gradient_kernel,
        [tok_own, tok_other, d_set, flip(d_set)],
        [shape((width, ff_width))] * 2,
        [pltpu.VMEM((width, half_rows), jnp.bfloat16)] * 2,
    )
    (grad_down,) = call(down_kernel, [hidden, grad_all], [shape((ff_width, width))])
    *messages, grad_gate, grad_up, grad_down = lax.optimization_barrier(
        (*messages, grad_gate, grad_up, grad_down)
    )
    total = jnp.where(core == 0, kept, 0.0)
    for message in messages:
        total = total + message.astype(jnp.float32)
    total = (total[:, :, :width] + flip(total[:, :, width:])).astype(jnp.bfloat16)
    return (total[0], total[1], grad_gate, grad_up, grad_down)


def solution(mesh):
    placed = (P("col", "row"), P("row", "col"), P("row", "col"), P("col", "row"), P("col", "row"))
    return jax.shard_map(
        body,
        mesh=mesh,
        in_specs=placed,
        out_specs=(
            P("col", "row"),
            P("col", "row"),
            P("row", "col"),
            P("row", "col"),
            P("col", "row"),
        ),
        check_vma=False,
    )
```

```python
import functools

import jax
import jax.numpy as jnp
from jax import lax
from jax.experimental import pallas as pl
from jax.experimental.pallas import tpu as pltpu
from jax.sharding import PartitionSpec as P

NY, NX, NC, NZ = 4, 2, 2, 4
PIECE = 64
BOTH = ("row", "col")


def row_at(y, x, core):
    return ((y % NY) * NX + x) * NC + core


def row_perm(core0, core1):
    pairs = []
    for y in range(NY):
        for x in range(NX):
            for core, move in ((0, core0), (1, core1)):
                if move is not None:
                    to_y, to_x = move(y, x)
                    pairs.append((row_at(y, x, core), row_at(to_y, to_x, core)))
    return pairs


def over_x(y, x):
    return y, 1 - x


def over_y(step):
    return lambda y, x: (y + step, x)


CORE_FLIP = [(i, i ^ 1) for i in range(NY * NX * NC)]


def gather_perm(step):
    pairs = []
    for row in range(NY * NX * NC):
        core = row % NC
        if core == 0 and step == 0:
            continue
        for hi in range(2):
            for z in range(NZ):
                source = (hi ^ core) * NZ + (z + step) % NZ
                pairs.append((row * 8 + source, row * 8 + hi * NZ + z))
    return pairs


def scatter_perm(step):
    return [(to, source) for source, to in gather_perm(step)]


def product(left, right, transposed):
    dims = (((1,), (1 if transposed else 0,)), ((), ()))
    return lax.dot_general(left, right, dims, preferred_element_type=jnp.float32)


def spans(width):
    return [(at, min(at + 256, width)) for at in range(0, width, 256)]


def shape(dims, dtype=jnp.bfloat16):
    return jax.ShapeDtypeStruct(dims, dtype)


def call(kernel, operands, out_shape, scratch=()):
    n_in, n_out = len(operands), len(out_shape)

    def run(*refs):
        kernel(refs[:n_in], refs[n_in : n_in + n_out], *refs[n_in + n_out :])

    vmem = pl.BlockSpec(memory_space=pltpu.VMEM)
    return pl.pallas_call(
        run,
        in_specs=[vmem] * n_in,
        out_specs=[vmem] * n_out,
        out_shape=out_shape,
        scratch_shapes=scratch,
        compiler_params=pltpu.CompilerParams(vmem_limit_bytes=12 * 2**20),
        cost_estimate=pl.CostEstimate(flops=1, bytes_accessed=1, transcendentals=0),
    )(*operands)


class Place:
    def __init__(self):
        row = lax.axis_index("row")
        self.core, self.x, self.y = row % NC, (row // NC) % NX, row // (NC * NX)
        self.other = 1 - self.x

    def piece(self, step, x):
        return ((self.y + step) % NY) * NX + x

    def choose(self, core0, core1):
        pieces = [jnp.where(self.core == 0, self.piece(*a), self.piece(*b)) for a, b in zip(core0, core1)]
        return [pl.ds(pl.multiple_of(piece * PIECE, PIECE), PIECE) for piece in pieces]

    def first(self):
        o = self.other
        core0 = [(o, o), (1 - o, o), (3 - o, o), (2 + o, o), (0, self.x), (0, self.x)]
        return self.choose(core0, [(step, x) for step in (1, 3, 2) for x in (0, 1)])

    def second(self):
        x, o = self.x, self.other
        return self.choose([(1, x), (3, x), (2, x), (0, x)], [(0, o), (0, x), (0, x), (0, x)])

    def gathered(self):
        x, o = self.x, self.other
        core0 = [(0, x), (3, x), (0, o), (3, o), (1, o), (2, o), (1, x), (2, x)]
        return self.choose(core0, [(0, x), (0, o)] + [(step, at) for step in (3, 1, 2) for at in (x, o)])

    def half(self, x):
        return pl.ds(pl.multiple_of(x * PIECE, PIECE), PIECE)


def pair_product(held, pair, at, end, transposed):
    half = held.shape[1] // 2
    chunk = (slice(at, end), slice(None)) if transposed else (slice(None), slice(at, end))
    own, other = [ref[chunk] for ref in pair]
    return product(held[:, :half], own, transposed) + product(held[:, half:], other, transposed)


def block_kernel(ins, outs):
    mine, *theirs = ins
    (block,) = outs
    half = block.shape[2] // 2
    for i in range(2):
        block[i, :, :half] = mine[i]
        block[i, :, half:] = theirs[i][...]


def keep_kernel(ins, outs):
    for source, out in zip(ins, outs):
        out[...] = source[...]


def gradient_kernel(ins, outs, own_turned, other_turned):
    tok_own, tok_other, d_own, d_other = ins
    own_turned[...] = tok_own[...].T
    other_turned[...] = tok_other[...].T
    for i, out in enumerate(outs):
        for at, end in spans(out.shape[1]):
            total = product(own_turned[...], d_own[i, :, at:end], False)
            total += product(other_turned[...], d_other[i, :, at:end], False)
            out[:, at:end] = total.astype(jnp.bfloat16)


def down_kernel(ins, outs):
    hidden, grad_all = ins
    for at, end in spans(hidden.shape[1]):
        total = product(hidden[:, at:end].T, grad_all[...], False)
        outs[0][at:end, :] = total.astype(jnp.bfloat16)


def first_kernel(ins, outs, tok_held, grad_held):
    place = Place()
    block, *blocks = ins[: NZ + 1]
    weights, messages = ins[NZ + 1 :], outs[2:]
    rows = block.shape[1]
    pieces = place.first()
    for i, held in enumerate((tok_held, grad_held)):
        acts = outs[i]
        acts[:rows] = jnp.where(place.core == 0, block[i], blocks[0][i])
        for k in range(1, NZ):
            acts[k * rows : (k + 1) * rows] = blocks[k][i]
        for slot, rows_at in enumerate(pieces):
            held[slot * PIECE : (slot + 1) * PIECE, :] = acts[rows_at, :]
    for which in range(3):
        held, transposed = ((tok_held, False), (grad_held, True))[which // 2]
        pair = weights[2 * which : 2 * which + 2]
        for at, end in spans(messages[0].shape[2]):
            total = pair_product(held, pair, at, end, transposed).astype(jnp.bfloat16)
            for i, message in enumerate(messages):
                message[which, :, at:end] = total[i * 2 * PIECE : (i + 1) * 2 * PIECE]


def partial_kernel(ins, outs, tok_held, grad_held):
    pieces = Place().second()
    for i, held in enumerate((tok_held, grad_held)):
        rows = ins[i]
        for slot, rows_at in enumerate(pieces):
            held[slot * PIECE : (slot + 1) * PIECE, :] = rows[rows_at, :]
        own, away = outs[1 + i], outs[3 + i]
        half = own.shape[1]
        own[...] = rows[:, :half]
        away[...] = rows[:, half:]
    for which in range(3):
        held, transposed = ((tok_held, False), (grad_held, True))[which // 2]
        pair = ins[2 + 2 * which : 4 + 2 * which]
        for at, end in spans(outs[0].shape[2]):
            outs[0][which, :, at:end] = pair_product(held, pair, at, end, transposed)


def second_kernel(ins, outs):
    place = Place()
    products, *heard = ins
    near, far = place.half(place.x), place.half(place.other)
    one = place.core == 1
    for which in range(3):
        for at, end in spans(outs[0].shape[2]):
            near2 = heard[1][which, near, at:end].astype(jnp.float32)
            far1, far2, far3 = [h[which, far, at:end].astype(jnp.float32) for h in heard]
            part1, part2, part3 = [
                products[which, slot * PIECE : (slot + 1) * PIECE, at:end] for slot in range(3)
            ]
            sum1 = part1 + far1 + jnp.where(one, far2 + far3, 0.0)
            high = sum1.astype(jnp.bfloat16)
            rest = sum1 - high.astype(jnp.float32)
            outs[0][which, :, at:end] = high
            outs[1][which, :, at:end] = jnp.where(one, rest, part2 + near2).astype(jnp.bfloat16)
            outs[2][which, :, at:end] = (part3 + far2).astype(jnp.bfloat16)


def unit_kernel(ins, outs):
    place = Place()
    products, first, second = ins[0], ins[1:4], ins[4:7]
    hidden, both = outs
    near, one = place.half(place.x), place.core == 1
    for at, end in spans(hidden.shape[1]):

        def summed(which):
            near1, near2, near3 = [h[which, near, at:end].astype(jnp.float32) for h in first]
            total = products[which, 3 * PIECE :, at:end] + near1
            total = total + jnp.where(one, near2 + near3, 0.0)
            return total + sum(h[which, :, at:end].astype(jnp.float32) for h in second)

        gate, up, d_hidden = [summed(which) for which in range(3)]
        sig_gate = jax.nn.sigmoid(gate)
        hidden[:, at:end] = (gate * sig_gate * up).astype(jnp.bfloat16)
        slope = d_hidden * up * sig_gate * (1.0 + gate * (1.0 - sig_gate))
        both[0, :, at:end] = slope.astype(jnp.bfloat16)
        both[1, :, at:end] = (d_hidden * gate * sig_gate).astype(jnp.bfloat16)


def weave_kernel(ins, outs):
    core = Place().core
    for rows, at_core in zip(ins, (core, 1 - core)):
        for piece in range(NY * NX):
            start = pl.multiple_of((piece * NC + at_core) * PIECE, PIECE)
            outs[0][pl.ds(start, PIECE), :] = rows[piece * PIECE : (piece + 1) * PIECE, :]


def pack_kernel(ins, outs):
    own, near1, near2, near3 = ins
    first, second, third = outs
    core0 = Place().core == 0
    for out in (first, third):
        out[:, :PIECE] = own[...]
        out[:, PIECE:] = near1[...]
    second[:, :PIECE] = jnp.where(core0, near2[...], own[...])
    second[:, PIECE:] = jnp.where(core0, near3[...], near1[...])


def layer_kernel(ins, outs, held):
    hidden, *weights = ins
    messages, kept = outs[:NZ], outs[NZ]
    core = Place().core
    block = kept.shape[0]
    width = weights[0].shape[1]
    for piece in range(NY * NX):
        start = pl.multiple_of((piece * NC + core) * PIECE, PIECE)
        held[piece * PIECE : (piece + 1) * PIECE, :] = hidden[pl.ds(start, PIECE), :]
    for side, weight in enumerate(weights):
        for at, end in spans(width):
            term = product(held[...], weight[:, at:end], False)
            columns = slice(side * width + at, side * width + end)
            kept[:, columns] = term[:block]
            for k in range(NZ):
                rows = term[k * block : (k + 1) * block]
                messages[k][:, columns] = rows.astype(jnp.bfloat16)


def input_kernel(ins, outs):
    place = Place()
    layer, layer_kept = ins[:NZ], ins[NZ]
    own, near1, near2, near3, far1, far2, far3 = ins[NZ + 1 : NZ + 8]
    weights = ins[NZ + 8 :]
    *messages, d_set, kept = outs
    core0 = place.core == 0
    pieces = place.gathered()
    values = [own[...], near1[...], far1[:, :PIECE], far1[:, PIECE:], far2[:, :PIECE], far2[:, PIECE:]]
    values.append(jnp.where(core0, near2[...], far3[:, :PIECE]))
    values.append(jnp.where(core0, near3[...], far3[:, PIECE:]))
    for rows_at, value in zip(pieces, values):
        d_set[:, rows_at, :] = value
    depth = weights[0].shape[0]
    block = NX * PIECE
    kept[0] = layer_kept[...]
    for k in range(NZ):
        messages[k][0] = layer[k][...]
    for side in range(2):
        for at, end in spans(depth):
            gate, up = [weights[2 * side + i][at:end, :] for i in range(2)]
            total = product(d_set[0], gate, True) + product(d_set[1], up, True)
            columns = slice(side * depth + at, side * depth + end)
            kept[1, :, columns] = total[:block]
            for k in range(NZ):
                rows = total[k * block : (k + 1) * block]
                messages[k][1, :, columns] = rows.astype(jnp.bfloat16)


def last_kernel(ins, outs):
    kept, *messages = ins
    own, away = outs
    width = own.shape[2]
    core0 = Place().core == 0
    for i in range(2):
        total = jnp.where(core0, kept[i], 0.0)
        for message in messages:
            total = total + message[i].astype(jnp.float32)
        own[i] = total[:, :width]
        away[i] = total[:, width:]


def send_first(sent):
    return (
        lax.ppermute(sent[0], "row", row_perm(over_x, over_y(1))),
        lax.ppermute(sent[1], "row", row_perm(over_x, over_y(-1))),
        lax.ppermute(sent[2], "row", row_perm(None, over_y(2))),
    )


def send_second(sent, core1=over_x):
    third = lax.ppermute(sent[2], "row", row_perm(over_y(2), None))
    first = lax.ppermute(sent[0], "row", row_perm(over_y(1), over_x))
    return first, lax.ppermute(sent[1], "row", row_perm(over_y(-1), core1)), third


def body(tokens, gate_weight, up_weight, down_weight, grad_output):
    flip = lambda value: lax.ppermute(value, "row", CORE_FLIP)
    after = lambda value, *others: lax.optimization_barrier((value, *others))[0]
    width, ff_width = gate_weight.shape
    half_rows = NY * NX * PIECE
    rows = tokens.shape[0]

    tok_theirs, grad_theirs = flip(tokens), flip(grad_output)
    (own_block,) = call(
        block_kernel,
        [jnp.stack([tokens, grad_output]), tok_theirs, grad_theirs],
        [shape((2, rows, 2 * width))],
    )
    to_flip = lax.optimization_barrier((gate_weight, up_weight, down_weight, tok_theirs, grad_theirs))
    gate_other, up_other, down_other = [flip(weight) for weight in to_flip[:3]]
    own = lax.optimization_barrier((gate_weight, up_weight, down_weight, own_block))[:3]
    gate_own, up_own, down_own = call(keep_kernel, own, [shape(weight.shape) for weight in own])
    early = own_block
    late = [after(own_block, gate_other, gate_own), after(own_block, up_other, gate_own)]
    starts = [late[1], early, late[0], early]
    blocks = [lax.ppermute(starts[step], BOTH, gather_perm(step)) for step in range(NZ)]

    weights = [gate_own, gate_other, up_own, up_other, down_own, down_other]
    held = lambda pieces: [pltpu.VMEM((pieces * PIECE, 2 * width), jnp.bfloat16)] * 2
    tok_half, grad_half, *sent = call(
        first_kernel,
        [own_block, *blocks, *weights],
        [shape((half_rows, 2 * width))] * 2 + [shape((3, 2 * PIECE, ff_width))] * 3,
        held(6),
    )
    heard = send_first(sent)
    products, tok_own, grad_own, tok_away, grad_away = call(
        partial_kernel,
        [tok_half, grad_half, *weights],
        [shape((3, 4 * PIECE, ff_width), jnp.float32)] + [shape((half_rows, width))] * 4,
        held(4),
    )
    tok_other, grad_other = flip(tok_away), flip(grad_away)
    (grad_all,) = call(weave_kernel, [grad_own, grad_other], [shape((2 * half_rows, width))])
    *heard, grad_all, tok_other = lax.optimization_barrier((*heard, grad_all, tok_other))
    sent = call(second_kernel, [products, *heard], [shape((3, PIECE, ff_width))] * 3)
    hidden, d_own = call(
        unit_kernel,
        [products, *heard, *send_second(sent)],
        [shape((PIECE, ff_width)), shape((2, PIECE, ff_width))],
    )
    hidden = lax.all_gather(hidden, "row", axis=0, tiled=True)

    near = send_second([d_own] * 3, None)
    packed = call(pack_kernel, [d_own, *near], [shape((2, 2 * PIECE, ff_width))] * 3)
    far = send_first(packed)
    hidden = after(hidden, far[0])
    layer = call(
        layer_kernel,
        [hidden, down_weight, down_other],
        [shape((rows, 2 * width))] * NZ + [shape((rows, 2 * width), jnp.float32)],
        [pltpu.VMEM((half_rows, ff_width), jnp.bfloat16)],
    )
    block = (2, rows, 2 * width)
    *messages, d_set, kept = call(
        input_kernel,
        [*layer, d_own, *near, *far, gate_weight, up_weight, gate_other, up_other],
        [shape(block)] * 4 + [shape((2, half_rows, ff_width)), shape(block, jnp.float32)],
    )
    heard = {k: lax.ppermute(messages[k], BOTH, scatter_perm(k)) for k in (2, 1, 3, 0)}
    messages = [heard[k] for k in range(NZ)]
    grad_gate, grad_up = call(
        gradient_kernel,
        [tok_own, tok_other, d_set, flip(d_set)],
        [shape((width, ff_width))] * 2,
        [pltpu.VMEM((width, half_rows), jnp.bfloat16)] * 2,
    )
    (grad_down,) = call(down_kernel, [hidden, grad_all], [shape((ff_width, width))])
    *messages, grad_gate, grad_up, grad_down = lax.optimization_barrier(
        (*messages, grad_gate, grad_up, grad_down)
    )
    own, away = call(
        last_kernel, [kept, *messages], [shape((2, rows, width), jnp.float32)] * 2
    )
    total = (own + flip(away)).astype(jnp.bfloat16)
    return (total[0], total[1], grad_gate, grad_up, grad_down)


def solution(mesh):
    placed = (P("col", "row"), P("row", "col"), P("row", "col"), P("col", "row"), P("col", "row"))
    return jax.shard_map(
        body,
        mesh=mesh,
        in_specs=placed,
        out_specs=(
            P("col", "row"),
            P("col", "row"),
            P("row", "col"),
            P("row", "col"),
            P("col", "row"),
        ),
        check_vma=False,
    )
```

```python
import functools

import jax
import jax.numpy as jnp
from jax import lax
from jax.experimental import pallas as pl
from jax.experimental.pallas import tpu as pltpu
from jax.sharding import PartitionSpec as P

NY, NX, NC, NZ = 4, 2, 2, 4
PIECE = 64
BOTH = ("row", "col")


def row_at(y, x, core):
    return ((y % NY) * NX + x) * NC + core


def row_perm(core0, core1):
    pairs = []
    for y in range(NY):
        for x in range(NX):
            for core, move in ((0, core0), (1, core1)):
                if move is not None:
                    to_y, to_x = move(y, x)
                    pairs.append((row_at(y, x, core), row_at(to_y, to_x, core)))
    return pairs


def over_x(y, x):
    return y, 1 - x


def over_y(step):
    return lambda y, x: (y + step, x)


CORE_FLIP = [(i, i ^ 1) for i in range(NY * NX * NC)]


def gather_perm(step):
    pairs = []
    for row in range(NY * NX * NC):
        core = row % NC
        if core == 0 and step == 0:
            continue
        for hi in range(2):
            for z in range(NZ):
                source = (hi ^ core) * NZ + (z + step) % NZ
                pairs.append((row * 8 + source, row * 8 + hi * NZ + z))
    return pairs


def scatter_perm(step):
    return [(to, source) for source, to in gather_perm(step)]


def product(left, right, transposed):
    dims = (((1,), (1 if transposed else 0,)), ((), ()))
    return lax.dot_general(left, right, dims, preferred_element_type=jnp.float32)


def spans(width):
    return [(at, min(at + 256, width)) for at in range(0, width, 256)]


def shape(dims, dtype=jnp.bfloat16):
    return jax.ShapeDtypeStruct(dims, dtype)


def call(kernel, operands, out_shape, scratch=()):
    n_in, n_out = len(operands), len(out_shape)

    def run(*refs):
        kernel(refs[:n_in], refs[n_in : n_in + n_out], *refs[n_in + n_out :])

    vmem = pl.BlockSpec(memory_space=pltpu.VMEM)
    return pl.pallas_call(
        run,
        in_specs=[vmem] * n_in,
        out_specs=[vmem] * n_out,
        out_shape=out_shape,
        scratch_shapes=scratch,
        compiler_params=pltpu.CompilerParams(vmem_limit_bytes=12 * 2**20),
        cost_estimate=pl.CostEstimate(flops=1, bytes_accessed=1, transcendentals=0),
    )(*operands)


class Place:
    def __init__(self):
        row = lax.axis_index("row")
        self.core, self.x, self.y = row % NC, (row // NC) % NX, row // (NC * NX)
        self.other = 1 - self.x

    def piece(self, step, x):
        return ((self.y + step) % NY) * NX + x

    def choose(self, core0, core1):
        pieces = [jnp.where(self.core == 0, self.piece(*a), self.piece(*b)) for a, b in zip(core0, core1)]
        return [pl.ds(pl.multiple_of(piece * PIECE, PIECE), PIECE) for piece in pieces]

    def first(self):
        o = self.other
        core0 = [(o, o), (1 - o, o), (3 - o, o), (2 + o, o), (0, self.x), (0, self.x)]
        return self.choose(core0, [(step, x) for step in (1, 3, 2) for x in (0, 1)])

    def second(self):
        x, o = self.x, self.other
        return self.choose([(1, x), (3, x), (2, x), (0, x)], [(0, o), (0, x), (0, x), (0, x)])

    def gathered(self):
        x, o = self.x, self.other
        core0 = [(0, x), (3, x), (0, o), (3, o), (1, o), (2, o), (1, x), (2, x)]
        return self.choose(core0, [(0, x), (0, o)] + [(step, at) for step in (3, 1, 2) for at in (x, o)])

    def half(self, x):
        return pl.ds(pl.multiple_of(x * PIECE, PIECE), PIECE)


def pair_product(held, pair, at, end, transposed):
    half = held.shape[1] // 2
    chunk = (slice(at, end), slice(None)) if transposed else (slice(None), slice(at, end))
    own, other = [ref[chunk] for ref in pair]
    return product(held[:, :half], own, transposed) + product(held[:, half:], other, transposed)


def block_kernel(ins, outs):
    mine, *theirs = ins
    (block,) = outs
    half = block.shape[2] // 2
    for i in range(2):
        block[i, :, :half] = mine[i]
        block[i, :, half:] = theirs[i][...]


def keep_kernel(ins, outs):
    for source, out in zip(ins, outs):
        out[...] = source[...]


def gradient_kernel(ins, outs, own_turned, other_turned):
    tok_own, tok_other, d_own, d_other = ins
    own_turned[...] = tok_own[...].T
    other_turned[...] = tok_other[...].T
    for i, out in enumerate(outs):
        for at, end in spans(out.shape[1]):
            total = product(own_turned[...], d_own[i, :, at:end], False)
            total += product(other_turned[...], d_other[i, :, at:end], False)
            out[:, at:end] = total.astype(jnp.bfloat16)


def down_kernel(ins, outs):
    hidden, grad_all = ins
    for at, end in spans(hidden.shape[1]):
        total = product(hidden[:, at:end].T, grad_all[...], False)
        outs[0][at:end, :] = total.astype(jnp.bfloat16)


def first_kernel(ins, outs, tok_held, grad_held):
    place = Place()
    block, *blocks = ins[: NZ + 1]
    weights, messages = ins[NZ + 1 :], outs[2:]
    rows = block.shape[1]
    pieces = place.first()
    for i, held in enumerate((tok_held, grad_held)):
        acts = outs[i]
        acts[:rows] = jnp.where(place.core == 0, block[i], blocks[0][i])
        for k in range(1, NZ):
            acts[k * rows : (k + 1) * rows] = blocks[k][i]
        for slot, rows_at in enumerate(pieces):
            held[slot * PIECE : (slot + 1) * PIECE, :] = acts[rows_at, :]
    for which in range(3):
        held, transposed = ((tok_held, False), (grad_held, True))[which // 2]
        pair = weights[2 * which : 2 * which + 2]
        for at, end in spans(messages[0].shape[2]):
            total = pair_product(held, pair, at, end, transposed).astype(jnp.bfloat16)
            for i, message in enumerate(messages):
                message[which, :, at:end] = total[i * 2 * PIECE : (i + 1) * 2 * PIECE]


def partial_kernel(ins, outs, tok_held, grad_held):
    pieces = Place().second()
    for i, held in enumerate((tok_held, grad_held)):
        rows = ins[i]
        for slot, rows_at in enumerate(pieces):
            held[slot * PIECE : (slot + 1) * PIECE, :] = rows[rows_at, :]
        own, away = outs[1 + i], outs[3 + i]
        half = own.shape[1]
        own[...] = rows[:, :half]
        away[...] = rows[:, half:]
    for which in range(3):
        held, transposed = ((tok_held, False), (grad_held, True))[which // 2]
        pair = ins[2 + 2 * which : 4 + 2 * which]
        for at, end in spans(outs[0].shape[2]):
            outs[0][which, :, at:end] = pair_product(held, pair, at, end, transposed)


def second_kernel(ins, outs):
    place = Place()
    products, *heard = ins
    near, far = place.half(place.x), place.half(place.other)
    one = place.core == 1
    for which in range(3):
        for at, end in spans(outs[0].shape[2]):
            near2 = heard[1][which, near, at:end].astype(jnp.float32)
            far1, far2, far3 = [h[which, far, at:end].astype(jnp.float32) for h in heard]
            part1, part2, part3 = [
                products[which, slot * PIECE : (slot + 1) * PIECE, at:end] for slot in range(3)
            ]
            sum1 = part1 + far1 + jnp.where(one, far2 + far3, 0.0)
            high = sum1.astype(jnp.bfloat16)
            rest = sum1 - high.astype(jnp.float32)
            outs[0][which, :, at:end] = high
            outs[1][which, :, at:end] = jnp.where(one, rest, part2 + near2).astype(jnp.bfloat16)
            outs[2][which, :, at:end] = (part3 + far2).astype(jnp.bfloat16)


def unit_kernel(ins, outs):
    place = Place()
    products, first, second = ins[0], ins[1:4], ins[4:7]
    hidden, both = outs
    near, one = place.half(place.x), place.core == 1
    for at, end in spans(hidden.shape[1]):

        def summed(which):
            near1, near2, near3 = [h[which, near, at:end].astype(jnp.float32) for h in first]
            total = products[which, 3 * PIECE :, at:end] + near1
            total = total + jnp.where(one, near2 + near3, 0.0)
            return total + sum(h[which, :, at:end].astype(jnp.float32) for h in second)

        gate, up, d_hidden = [summed(which) for which in range(3)]
        sig_gate = jax.nn.sigmoid(gate)
        hidden[:, at:end] = (gate * sig_gate * up).astype(jnp.bfloat16)
        slope = d_hidden * up * sig_gate * (1.0 + gate * (1.0 - sig_gate))
        both[0, :, at:end] = slope.astype(jnp.bfloat16)
        both[1, :, at:end] = (d_hidden * gate * sig_gate).astype(jnp.bfloat16)


def weave_kernel(ins, outs):
    core = Place().core
    for rows, at_core in zip(ins, (core, 1 - core)):
        for piece in range(NY * NX):
            start = pl.multiple_of((piece * NC + at_core) * PIECE, PIECE)
            outs[0][pl.ds(start, PIECE), :] = rows[piece * PIECE : (piece + 1) * PIECE, :]


def pack_kernel(ins, outs):
    own, near1, near2, near3 = ins
    first, second, third = outs
    core0 = Place().core == 0
    for out in (first, third):
        out[:, :PIECE] = own[...]
        out[:, PIECE:] = near1[...]
    second[:, :PIECE] = jnp.where(core0, near2[...], own[...])
    second[:, PIECE:] = jnp.where(core0, near3[...], near1[...])


def layer_kernel(ins, outs, held):
    hidden, *weights = ins
    messages, kept = outs[:NZ], outs[NZ]
    core = Place().core
    block = kept.shape[0]
    width = weights[0].shape[1]
    for piece in range(NY * NX):
        start = pl.multiple_of((piece * NC + core) * PIECE, PIECE)
        held[piece * PIECE : (piece + 1) * PIECE, :] = hidden[pl.ds(start, PIECE), :]
    for side, weight in enumerate(weights):
        for at, end in spans(width):
            term = product(held[...], weight[:, at:end], False)
            columns = slice(side * width + at, side * width + end)
            kept[:, columns] = term[:block]
            for k in range(NZ):
                rows = term[k * block : (k + 1) * block]
                messages[k][:, columns] = rows.astype(jnp.bfloat16)


def input_kernel(ins, outs):
    place = Place()
    layer, layer_kept = ins[:NZ], ins[NZ]
    own, near1, near2, near3, far1, far2, far3 = ins[NZ + 1 : NZ + 8]
    weights = ins[NZ + 8 :]
    *messages, d_set, kept = outs
    core0 = place.core == 0
    pieces = place.gathered()
    values = [own[...], near1[...], far1[:, :PIECE], far1[:, PIECE:], far2[:, :PIECE], far2[:, PIECE:]]
    values.append(jnp.where(core0, near2[...], far3[:, :PIECE]))
    values.append(jnp.where(core0, near3[...], far3[:, PIECE:]))
    for rows_at, value in zip(pieces, values):
        d_set[:, rows_at, :] = value
    depth = weights[0].shape[0]
    block = NX * PIECE
    kept[0] = layer_kept[...]
    for k in range(NZ):
        messages[k][0] = layer[k][...]
    for side in range(2):
        for at, end in spans(depth):
            gate, up = [weights[2 * side + i][at:end, :] for i in range(2)]
            total = product(d_set[0], gate, True) + product(d_set[1], up, True)
            columns = slice(side * depth + at, side * depth + end)
            kept[1, :, columns] = total[:block]
            for k in range(NZ):
                rows = total[k * block : (k + 1) * block]
                messages[k][1, :, columns] = rows.astype(jnp.bfloat16)


def send_first(sent):
    return (
        lax.ppermute(sent[0], "row", row_perm(over_x, over_y(1))),
        lax.ppermute(sent[1], "row", row_perm(over_x, over_y(-1))),
        lax.ppermute(sent[2], "row", row_perm(None, over_y(2))),
    )


def send_second(sent, core1=over_x):
    third = lax.ppermute(sent[2], "row", row_perm(over_y(2), None))
    first = lax.ppermute(sent[0], "row", row_perm(over_y(1), over_x))
    return first, lax.ppermute(sent[1], "row", row_perm(over_y(-1), core1)), third


def body(tokens, gate_weight, up_weight, down_weight, grad_output):
    flip = lambda value: lax.ppermute(value, "row", CORE_FLIP)
    after = lambda value, *others: lax.optimization_barrier((value, *others))[0]
    width, ff_width = gate_weight.shape
    half_rows = NY * NX * PIECE
    rows = tokens.shape[0]

    tok_theirs, grad_theirs = flip(tokens), flip(grad_output)
    (own_block,) = call(
        block_kernel,
        [jnp.stack([tokens, grad_output]), tok_theirs, grad_theirs],
        [shape((2, rows, 2 * width))],
    )
    to_flip = lax.optimization_barrier((gate_weight, up_weight, down_weight, tok_theirs, grad_theirs))
    gate_other, up_other, down_other = [flip(weight) for weight in to_flip[:3]]
    own = lax.optimization_barrier((gate_weight, up_weight, down_weight, own_block))[:3]
    gate_own, up_own, down_own = call(keep_kernel, own, [shape(weight.shape) for weight in own])
    early = own_block
    late = [after(own_block, gate_other, gate_own), after(own_block, up_other, gate_own)]
    starts = [late[1], early, late[0], early]
    blocks = [lax.ppermute(starts[step], BOTH, gather_perm(step)) for step in range(NZ)]

    weights = [gate_own, gate_other, up_own, up_other, down_own, down_other]
    held = lambda pieces: [pltpu.VMEM((pieces * PIECE, 2 * width), jnp.bfloat16)] * 2
    tok_half, grad_half, *sent = call(
        first_kernel,
        [own_block, *blocks, *weights],
        [shape((half_rows, 2 * width))] * 2 + [shape((3, 2 * PIECE, ff_width))] * 3,
        held(6),
    )
    heard = send_first(sent)
    products, tok_own, grad_own, tok_away, grad_away = call(
        partial_kernel,
        [tok_half, grad_half, *weights],
        [shape((3, 4 * PIECE, ff_width), jnp.float32)] + [shape((half_rows, width))] * 4,
        held(4),
    )
    tok_other, grad_other = flip(tok_away), flip(grad_away)
    (grad_all,) = call(weave_kernel, [grad_own, grad_other], [shape((2 * half_rows, width))])
    *heard, grad_all, tok_other = lax.optimization_barrier((*heard, grad_all, tok_other))
    sent = call(second_kernel, [products, *heard], [shape((3, PIECE, ff_width))] * 3)
    hidden, d_own = call(
        unit_kernel,
        [products, *heard, *send_second(sent)],
        [shape((PIECE, ff_width)), shape((2, PIECE, ff_width))],
    )
    hidden = lax.all_gather(hidden, "row", axis=0, tiled=True)

    near = send_second([d_own] * 3)
    packed = call(pack_kernel, [d_own, *near], [shape((2, 2 * PIECE, ff_width))] * 3)
    far = send_first(packed)
    hidden = after(hidden, far[0])
    layer = call(
        layer_kernel,
        [hidden, down_weight, down_other],
        [shape((rows, 2 * width))] * NZ + [shape((rows, 2 * width), jnp.float32)],
        [pltpu.VMEM((half_rows, ff_width), jnp.bfloat16)],
    )
    block = (2, rows, 2 * width)
    *messages, d_set, kept = call(
        input_kernel,
        [*layer, d_own, *near, *far, gate_weight, up_weight, gate_other, up_other],
        [shape(block)] * 4 + [shape((2, half_rows, ff_width)), shape(block, jnp.float32)],
    )
    heard = {k: lax.ppermute(messages[k], BOTH, scatter_perm(k)) for k in (2, 1, 3, 0)}
    messages = [heard[k] for k in range(NZ)]
    grad_gate, grad_up = call(
        gradient_kernel,
        [tok_own, tok_other, d_set, flip(d_set)],
        [shape((width, ff_width))] * 2,
        [pltpu.VMEM((width, half_rows), jnp.bfloat16)] * 2,
    )
    (grad_down,) = call(down_kernel, [hidden, grad_all], [shape((ff_width, width))])
    *messages, grad_gate, grad_up, grad_down = lax.optimization_barrier(
        (*messages, grad_gate, grad_up, grad_down)
    )
    total = jnp.where(lax.axis_index("row") % NC == 0, kept, 0.0)
    for message in messages:
        total = total + message.astype(jnp.float32)
    total = (total[:, :, :width] + flip(total[:, :, width:])).astype(jnp.bfloat16)
    return (total[0], total[1], grad_gate, grad_up, grad_down)


def solution(mesh):
    placed = (P("col", "row"), P("row", "col"), P("row", "col"), P("col", "row"), P("col", "row"))
    return jax.shard_map(
        body,
        mesh=mesh,
        in_specs=placed,
        out_specs=(
            P("col", "row"),
            P("col", "row"),
            P("row", "col"),
            P("row", "col"),
            P("col", "row"),
        ),
        check_vma=False,
    )
```

```python
import functools

import jax
import jax.numpy as jnp
from jax import lax
from jax.experimental import pallas as pl
from jax.experimental.pallas import tpu as pltpu
from jax.sharding import PartitionSpec as P

NY, NX, NC, NZ = 4, 2, 2, 4
PIECE = 64
BOTH = ("row", "col")


def row_at(y, x, core):
    return ((y % NY) * NX + x) * NC + core


def row_perm(core0, core1):
    pairs = []
    for y in range(NY):
        for x in range(NX):
            for core, move in ((0, core0), (1, core1)):
                if move is not None:
                    to_y, to_x = move(y, x)
                    pairs.append((row_at(y, x, core), row_at(to_y, to_x, core)))
    return pairs


def over_x(y, x):
    return y, 1 - x


def over_y(step):
    return lambda y, x: (y + step, x)


CORE_FLIP = [(i, i ^ 1) for i in range(NY * NX * NC)]


def gather_perm(step):
    pairs = []
    for row in range(NY * NX * NC):
        core = row % NC
        if core == 0 and step == 0:
            continue
        for hi in range(2):
            for z in range(NZ):
                source = (hi ^ core) * NZ + (z + step) % NZ
                pairs.append((row * 8 + source, row * 8 + hi * NZ + z))
    return pairs


def scatter_perm(step):
    return [(to, source) for source, to in gather_perm(step)]


def product(left, right, transposed):
    dims = (((1,), (1 if transposed else 0,)), ((), ()))
    return lax.dot_general(left, right, dims, preferred_element_type=jnp.float32)


def spans(width):
    return [(at, min(at + 256, width)) for at in range(0, width, 256)]


def shape(dims, dtype=jnp.bfloat16):
    return jax.ShapeDtypeStruct(dims, dtype)


def call(kernel, operands, out_shape, scratch=()):
    n_in, n_out = len(operands), len(out_shape)

    def run(*refs):
        kernel(refs[:n_in], refs[n_in : n_in + n_out], *refs[n_in + n_out :])

    vmem = pl.BlockSpec(memory_space=pltpu.VMEM)
    return pl.pallas_call(
        run,
        in_specs=[vmem] * n_in,
        out_specs=[vmem] * n_out,
        out_shape=out_shape,
        scratch_shapes=scratch,
        compiler_params=pltpu.CompilerParams(vmem_limit_bytes=12 * 2**20),
        cost_estimate=pl.CostEstimate(flops=1, bytes_accessed=1, transcendentals=0),
    )(*operands)


class Place:
    def __init__(self):
        row = lax.axis_index("row")
        self.core, self.x, self.y = row % NC, (row // NC) % NX, row // (NC * NX)
        self.other = 1 - self.x

    def piece(self, step, x):
        return ((self.y + step) % NY) * NX + x

    def choose(self, core0, core1):
        pieces = [jnp.where(self.core == 0, self.piece(*a), self.piece(*b)) for a, b in zip(core0, core1)]
        return [pl.ds(pl.multiple_of(piece * PIECE, PIECE), PIECE) for piece in pieces]

    def first(self):
        o = self.other
        core0 = [(o, o), (1 - o, o), (3 - o, o), (2 + o, o), (0, self.x), (0, self.x)]
        return self.choose(core0, [(step, x) for step in (1, 3, 2) for x in (0, 1)])

    def second(self):
        x, o = self.x, self.other
        return self.choose([(1, x), (3, x), (2, x), (0, x)], [(0, o), (0, x), (0, x), (0, x)])

    def gathered(self):
        x, o = self.x, self.other
        core0 = [(0, x), (3, x), (0, o), (3, o), (1, o), (2, o), (1, x), (2, x)]
        return self.choose(core0, [(0, x), (0, o)] + [(step, at) for step in (3, 1, 2) for at in (x, o)])

    def half(self, x):
        return pl.ds(pl.multiple_of(x * PIECE, PIECE), PIECE)


def pair_product(held, pair, at, end, transposed):
    half = held.shape[1] // 2
    chunk = (slice(at, end), slice(None)) if transposed else (slice(None), slice(at, end))
    own, other = [ref[chunk] for ref in pair]
    return product(held[:, :half], own, transposed) + product(held[:, half:], other, transposed)


def block_kernel(ins, outs):
    mine, *theirs = ins
    (block,) = outs
    half = block.shape[2] // 2
    for i in range(2):
        block[i, :, :half] = mine[i]
        block[i, :, half:] = theirs[i][...]


def keep_kernel(ins, outs):
    for source, out in zip(ins, outs):
        out[...] = source[...]


def gradient_kernel(ins, outs, own_turned, other_turned):
    tok_own, tok_other, d_own, d_other = ins
    own_turned[...] = tok_own[...].T
    other_turned[...] = tok_other[...].T
    for i, out in enumerate(outs):
        for at, end in spans(out.shape[1]):
            total = product(own_turned[...], d_own[i, :, at:end], False)
            total += product(other_turned[...], d_other[i, :, at:end], False)
            out[:, at:end] = total.astype(jnp.bfloat16)


def down_kernel(ins, outs):
    hidden, grad_all = ins
    for at, end in spans(hidden.shape[1]):
        total = product(hidden[:, at:end].T, grad_all[...], False)
        outs[0][at:end, :] = total.astype(jnp.bfloat16)


def first_kernel(ins, outs, tok_held, grad_held):
    place = Place()
    block, *blocks = ins[: NZ + 1]
    weights, messages = ins[NZ + 1 :], outs[2:]
    rows = block.shape[1]
    pieces = place.first()
    for i, held in enumerate((tok_held, grad_held)):
        acts = outs[i]
        acts[:rows] = jnp.where(place.core == 0, block[i], blocks[0][i])
        for k in range(1, NZ):
            acts[k * rows : (k + 1) * rows] = blocks[k][i]
        for slot, rows_at in enumerate(pieces):
            held[slot * PIECE : (slot + 1) * PIECE, :] = acts[rows_at, :]
    for which in range(3):
        held, transposed = ((tok_held, False), (grad_held, True))[which // 2]
        pair = weights[2 * which : 2 * which + 2]
        for at, end in spans(messages[0].shape[2]):
            total = pair_product(held, pair, at, end, transposed).astype(jnp.bfloat16)
            for i, message in enumerate(messages):
                message[which, :, at:end] = total[i * 2 * PIECE : (i + 1) * 2 * PIECE]


def partial_kernel(ins, outs, tok_held, grad_held):
    pieces = Place().second()
    for i, held in enumerate((tok_held, grad_held)):
        rows = ins[i]
        for slot, rows_at in enumerate(pieces):
            held[slot * PIECE : (slot + 1) * PIECE, :] = rows[rows_at, :]
        own, away = outs[1 + i], outs[3 + i]
        half = own.shape[1]
        own[...] = rows[:, :half]
        away[...] = rows[:, half:]
    for which in range(3):
        held, transposed = ((tok_held, False), (grad_held, True))[which // 2]
        pair = ins[2 + 2 * which : 4 + 2 * which]
        for at, end in spans(outs[0].shape[2]):
            outs[0][which, :, at:end] = pair_product(held, pair, at, end, transposed)


def second_kernel(ins, outs):
    place = Place()
    products, *heard = ins
    near, far = place.half(place.x), place.half(place.other)
    one = place.core == 1
    for which in range(3):
        for at, end in spans(outs[0].shape[2]):
            near2 = heard[1][which, near, at:end].astype(jnp.float32)
            far1, far2, far3 = [h[which, far, at:end].astype(jnp.float32) for h in heard]
            part1, part2, part3 = [
                products[which, slot * PIECE : (slot + 1) * PIECE, at:end] for slot in range(3)
            ]
            sum1 = part1 + far1 + jnp.where(one, far2 + far3, 0.0)
            high = sum1.astype(jnp.bfloat16)
            rest = sum1 - high.astype(jnp.float32)
            outs[0][which, :, at:end] = high
            outs[1][which, :, at:end] = jnp.where(one, rest, part2 + near2).astype(jnp.bfloat16)
            outs[2][which, :, at:end] = (part3 + far2).astype(jnp.bfloat16)


def unit_kernel(ins, outs):
    place = Place()
    products, first, second = ins[0], ins[1:4], ins[4:7]
    hidden, both = outs
    near, one = place.half(place.x), place.core == 1
    for at, end in spans(hidden.shape[1]):

        def summed(which):
            near1, near2, near3 = [h[which, near, at:end].astype(jnp.float32) for h in first]
            total = products[which, 3 * PIECE :, at:end] + near1
            total = total + jnp.where(one, near2 + near3, 0.0)
            return total + sum(h[which, :, at:end].astype(jnp.float32) for h in second)

        gate, up, d_hidden = [summed(which) for which in range(3)]
        sig_gate = jax.nn.sigmoid(gate)
        hidden[:, at:end] = (gate * sig_gate * up).astype(jnp.bfloat16)
        slope = d_hidden * up * sig_gate * (1.0 + gate * (1.0 - sig_gate))
        both[0, :, at:end] = slope.astype(jnp.bfloat16)
        both[1, :, at:end] = (d_hidden * gate * sig_gate).astype(jnp.bfloat16)


def weave_kernel(ins, outs):
    core = Place().core
    for rows, at_core in zip(ins, (core, 1 - core)):
        for piece in range(NY * NX):
            start = pl.multiple_of((piece * NC + at_core) * PIECE, PIECE)
            outs[0][pl.ds(start, PIECE), :] = rows[piece * PIECE : (piece + 1) * PIECE, :]


def pack_kernel(ins, outs):
    own, near1, near2, near3 = ins
    first, second, third = outs
    core0 = Place().core == 0
    for out in (first, third):
        out[:, :PIECE] = own[...]
        out[:, PIECE:] = near1[...]
    second[:, :PIECE] = jnp.where(core0, near2[...], own[...])
    second[:, PIECE:] = jnp.where(core0, near3[...], near1[...])


def layer_kernel(ins, outs, held):
    hidden, *weights = ins
    messages, kept = outs[:NZ], outs[NZ]
    core = Place().core
    block = kept.shape[0]
    width = weights[0].shape[1]
    for piece in range(NY * NX):
        start = pl.multiple_of((piece * NC + core) * PIECE, PIECE)
        held[piece * PIECE : (piece + 1) * PIECE, :] = hidden[pl.ds(start, PIECE), :]
    for side, weight in enumerate(weights):
        for at, end in spans(width):
            term = product(held[...], weight[:, at:end], False)
            columns = slice(side * width + at, side * width + end)
            kept[:, columns] = term[:block]
            for k in range(NZ):
                rows = term[k * block : (k + 1) * block]
                messages[k][:, columns] = rows.astype(jnp.bfloat16)


def input_kernel(ins, outs):
    place = Place()
    layer, layer_kept = ins[:NZ], ins[NZ]
    own, near1, near2, near3, far1, far2, far3 = ins[NZ + 1 : NZ + 8]
    weights = ins[NZ + 8 :]
    *messages, d_set, kept = outs
    core0 = place.core == 0
    pieces = place.gathered()
    values = [own[...], near1[...], far1[:, :PIECE], far1[:, PIECE:], far2[:, :PIECE], far2[:, PIECE:]]
    values.append(jnp.where(core0, near2[...], far3[:, :PIECE]))
    values.append(jnp.where(core0, near3[...], far3[:, PIECE:]))
    for rows_at, value in zip(pieces, values):
        d_set[:, rows_at, :] = value
    depth = weights[0].shape[0]
    block = NX * PIECE
    kept[0] = layer_kept[...]
    for k in range(NZ):
        messages[k][0] = layer[k][...]
    for side in range(2):
        for at, end in spans(depth):
            gate, up = [weights[2 * side + i][at:end, :] for i in range(2)]
            total = product(d_set[0], gate, True) + product(d_set[1], up, True)
            columns = slice(side * depth + at, side * depth + end)
            kept[1, :, columns] = total[:block]
            for k in range(NZ):
                rows = total[k * block : (k + 1) * block]
                messages[k][1, :, columns] = rows.astype(jnp.bfloat16)


def last_kernel(ins, outs):
    kept, *messages = ins
    own, away = outs
    width = own.shape[2]
    core0 = Place().core == 0
    for i in range(2):
        total = jnp.where(core0, kept[i], 0.0)
        for message in messages:
            total = total + message[i].astype(jnp.float32)
        own[i] = total[:, :width]
        away[i] = total[:, width:]


def send_first(sent):
    return (
        lax.ppermute(sent[0], "row", row_perm(over_x, over_y(1))),
        lax.ppermute(sent[1], "row", row_perm(over_x, over_y(-1))),
        lax.ppermute(sent[2], "row", row_perm(None, over_y(2))),
    )


def send_second(sent, core1=over_x):
    third = lax.ppermute(sent[2], "row", row_perm(over_y(2), None))
    first = lax.ppermute(sent[0], "row", row_perm(over_y(1), over_x))
    return first, lax.ppermute(sent[1], "row", row_perm(over_y(-1), core1)), third


def body(tokens, gate_weight, up_weight, down_weight, grad_output):
    flip = lambda value: lax.ppermute(value, "row", CORE_FLIP)
    after = lambda value, *others: lax.optimization_barrier((value, *others))[0]
    width, ff_width = gate_weight.shape
    half_rows = NY * NX * PIECE
    rows = tokens.shape[0]

    tok_theirs, grad_theirs = flip(tokens), flip(grad_output)
    (own_block,) = call(
        block_kernel,
        [jnp.stack([tokens, grad_output]), tok_theirs, grad_theirs],
        [shape((2, rows, 2 * width))],
    )
    to_flip = lax.optimization_barrier((gate_weight, up_weight, down_weight, tok_theirs, grad_theirs))
    gate_other, up_other, down_other = [flip(weight) for weight in to_flip[:3]]
    own = lax.optimization_barrier((gate_weight, up_weight, down_weight, own_block))[:3]
    gate_own, up_own, down_own = call(keep_kernel, own, [shape(weight.shape) for weight in own])
    early = own_block
    late = [after(own_block, gate_other, gate_own), after(own_block, up_other, gate_own)]
    starts = [late[1], early, late[0], early]
    blocks = [lax.ppermute(starts[step], BOTH, gather_perm(step)) for step in range(NZ)]

    weights = [gate_own, gate_other, up_own, up_other, down_own, down_other]
    held = lambda pieces: [pltpu.VMEM((pieces * PIECE, 2 * width), jnp.bfloat16)] * 2
    tok_half, grad_half, *sent = call(
        first_kernel,
        [own_block, *blocks, *weights],
        [shape((half_rows, 2 * width))] * 2 + [shape((3, 2 * PIECE, ff_width))] * 3,
        held(6),
    )
    heard = send_first(sent)
    products, tok_own, grad_own, tok_away, grad_away = call(
        partial_kernel,
        [tok_half, grad_half, *weights],
        [shape((3, 4 * PIECE, ff_width), jnp.float32)] + [shape((half_rows, width))] * 4,
        held(4),
    )
    tok_other, grad_other = flip(tok_away), flip(grad_away)
    (grad_all,) = call(weave_kernel, [grad_own, grad_other], [shape((2 * half_rows, width))])
    *heard, grad_all, tok_other = lax.optimization_barrier((*heard, grad_all, tok_other))
    sent = call(second_kernel, [products, *heard], [shape((3, PIECE, ff_width))] * 3)
    hidden, d_own = call(
        unit_kernel,
        [products, *heard, *send_second(sent)],
        [shape((PIECE, ff_width)), shape((2, PIECE, ff_width))],
    )
    hidden = lax.all_gather(hidden, "row", axis=0, tiled=True)

    near = send_second([d_own] * 3)
    packed = call(pack_kernel, [d_own, *near], [shape((2, 2 * PIECE, ff_width))] * 3)
    far = send_first(packed)
    hidden = after(hidden, far[0])
    layer = call(
        layer_kernel,
        [hidden, down_weight, down_other],
        [shape((rows, 2 * width))] * NZ + [shape((rows, 2 * width), jnp.float32)],
        [pltpu.VMEM((half_rows, ff_width), jnp.bfloat16)],
    )
    block = (2, rows, 2 * width)
    *messages, d_set, kept = call(
        input_kernel,
        [*layer, d_own, *near, *far, gate_weight, up_weight, gate_other, up_other],
        [shape(block)] * 4 + [shape((2, half_rows, ff_width)), shape(block, jnp.float32)],
    )
    heard = {k: lax.ppermute(messages[k], BOTH, scatter_perm(k)) for k in (2, 1, 3, 0)}
    messages = [heard[k] for k in range(NZ)]
    grad_gate, grad_up = call(
        gradient_kernel,
        [tok_own, tok_other, d_set, flip(d_set)],
        [shape((width, ff_width))] * 2,
        [pltpu.VMEM((width, half_rows), jnp.bfloat16)] * 2,
    )
    (grad_down,) = call(down_kernel, [hidden, grad_all], [shape((ff_width, width))])
    *messages, grad_gate, grad_up, grad_down = lax.optimization_barrier(
        (*messages, grad_gate, grad_up, grad_down)
    )
    own, away = call(
        last_kernel, [kept, *messages], [shape((2, rows, width), jnp.float32)] * 2
    )
    total = (own + flip(away)).astype(jnp.bfloat16)
    return (total[0], total[1], grad_gate, grad_up, grad_down)


def solution(mesh):
    placed = (P("col", "row"), P("row", "col"), P("row", "col"), P("col", "row"), P("col", "row"))
    return jax.shard_map(
        body,
        mesh=mesh,
        in_specs=placed,
        out_specs=(
            P("col", "row"),
            P("col", "row"),
            P("row", "col"),
            P("row", "col"),
            P("col", "row"),
        ),
        check_vma=False,
    )
```

```python
import functools

import jax
import jax.numpy as jnp
from jax import lax
from jax.experimental import pallas as pl
from jax.experimental.pallas import tpu as pltpu
from jax.sharding import PartitionSpec as P

NY, NX, NC, NZ = 4, 2, 2, 4
PIECE = 64
BOTH = ("row", "col")


def row_at(y, x, core):
    return ((y % NY) * NX + x) * NC + core


def row_perm(core0, core1):
    pairs = []
    for y in range(NY):
        for x in range(NX):
            for core, move in ((0, core0), (1, core1)):
                if move is not None:
                    to_y, to_x = move(y, x)
                    pairs.append((row_at(y, x, core), row_at(to_y, to_x, core)))
    return pairs


def over_x(y, x):
    return y, 1 - x


def over_y(step):
    return lambda y, x: (y + step, x)


CORE_FLIP = [(i, i ^ 1) for i in range(NY * NX * NC)]


def gather_perm(step):
    pairs = []
    for row in range(NY * NX * NC):
        core = row % NC
        if core == 0 and step == 0:
            continue
        for hi in range(2):
            for z in range(NZ):
                source = (hi ^ core) * NZ + (z + step) % NZ
                pairs.append((row * 8 + source, row * 8 + hi * NZ + z))
    return pairs


def scatter_perm(step):
    return [(to, source) for source, to in gather_perm(step)]


def product(left, right, transposed):
    dims = (((1,), (1 if transposed else 0,)), ((), ()))
    return lax.dot_general(left, right, dims, preferred_element_type=jnp.float32)


def spans(width):
    return [(at, min(at + 256, width)) for at in range(0, width, 256)]


def shape(dims, dtype=jnp.bfloat16):
    return jax.ShapeDtypeStruct(dims, dtype)


def call(kernel, operands, out_shape, scratch=()):
    n_in, n_out = len(operands), len(out_shape)

    def run(*refs):
        kernel(refs[:n_in], refs[n_in : n_in + n_out], *refs[n_in + n_out :])

    vmem = pl.BlockSpec(memory_space=pltpu.VMEM)
    return pl.pallas_call(
        run,
        in_specs=[vmem] * n_in,
        out_specs=[vmem] * n_out,
        out_shape=out_shape,
        scratch_shapes=scratch,
        compiler_params=pltpu.CompilerParams(vmem_limit_bytes=12 * 2**20),
        cost_estimate=pl.CostEstimate(flops=1, bytes_accessed=1, transcendentals=0),
    )(*operands)


class Place:
    def __init__(self):
        row = lax.axis_index("row")
        self.core, self.x, self.y = row % NC, (row // NC) % NX, row // (NC * NX)
        self.other = 1 - self.x

    def piece(self, step, x):
        return ((self.y + step) % NY) * NX + x

    def choose(self, core0, core1):
        pieces = [jnp.where(self.core == 0, self.piece(*a), self.piece(*b)) for a, b in zip(core0, core1)]
        return [pl.ds(pl.multiple_of(piece * PIECE, PIECE), PIECE) for piece in pieces]

    def first(self):
        o = self.other
        core0 = [(o, o), (1 - o, o), (3 - o, o), (2 + o, o), (0, self.x), (0, self.x)]
        return self.choose(core0, [(step, x) for step in (1, 3, 2) for x in (0, 1)])

    def second(self):
        x, o = self.x, self.other
        return self.choose([(1, x), (3, x), (2, x), (0, x)], [(0, o), (0, x), (0, x), (0, x)])

    def gathered(self):
        x, o = self.x, self.other
        core0 = [(0, x), (3, x), (0, o), (3, o), (1, o), (2, o), (1, x), (2, x)]
        return self.choose(core0, [(0, x), (0, o)] + [(step, at) for step in (3, 1, 2) for at in (x, o)])

    def half(self, x):
        return pl.ds(pl.multiple_of(x * PIECE, PIECE), PIECE)


def pair_product(held, pair, at, end, transposed):
    half = held.shape[1] // 2
    chunk = (slice(at, end), slice(None)) if transposed else (slice(None), slice(at, end))
    own, other = [ref[chunk] for ref in pair]
    return product(held[:, :half], own, transposed) + product(held[:, half:], other, transposed)


def mine_kernel(ins, outs):
    for i in range(2):
        outs[0][i] = ins[i][...]


def block_kernel(ins, outs):
    mine, *theirs = ins
    (block,) = outs
    half = block.shape[2] // 2
    for i in range(2):
        block[i, :, :half] = mine[i]
        block[i, :, half:] = theirs[i][...]


def keep_kernel(ins, outs):
    for source, out in zip(ins, outs):
        out[...] = source[...]


def gradient_kernel(ins, outs, own_turned, other_turned):
    tok_own, tok_other, d_own, d_other = ins
    own_turned[...] = tok_own[...].T
    other_turned[...] = tok_other[...].T
    for i, out in enumerate(outs):
        for at, end in spans(out.shape[1]):
            total = product(own_turned[...], d_own[i, :, at:end], False)
            total += product(other_turned[...], d_other[i, :, at:end], False)
            out[:, at:end] = total.astype(jnp.bfloat16)


def down_kernel(ins, outs):
    hidden, grad_all = ins
    for at, end in spans(hidden.shape[1]):
        total = product(hidden[:, at:end].T, grad_all[...], False)
        outs[0][at:end, :] = total.astype(jnp.bfloat16)


def first_kernel(ins, outs, tok_held, grad_held):
    place = Place()
    block, *blocks = ins[: NZ + 1]
    weights, messages = ins[NZ + 1 :], outs[2:]
    rows = block.shape[1]
    pieces = place.first()
    for i, held in enumerate((tok_held, grad_held)):
        acts = outs[i]
        acts[:rows] = jnp.where(place.core == 0, block[i], blocks[0][i])
        for k in range(1, NZ):
            acts[k * rows : (k + 1) * rows] = blocks[k][i]
        for slot, rows_at in enumerate(pieces):
            held[slot * PIECE : (slot + 1) * PIECE, :] = acts[rows_at, :]
    for which in range(3):
        held, transposed = ((tok_held, False), (grad_held, True))[which // 2]
        pair = weights[2 * which : 2 * which + 2]
        for at, end in spans(messages[0].shape[2]):
            total = pair_product(held, pair, at, end, transposed).astype(jnp.bfloat16)
            for i, message in enumerate(messages):
                message[which, :, at:end] = total[i * 2 * PIECE : (i + 1) * 2 * PIECE]


def partial_kernel(ins, outs, tok_held, grad_held):
    pieces = Place().second()
    for i, held in enumerate((tok_held, grad_held)):
        rows = ins[i]
        for slot, rows_at in enumerate(pieces):
            held[slot * PIECE : (slot + 1) * PIECE, :] = rows[rows_at, :]
        own, away = outs[1 + i], outs[3 + i]
        half = own.shape[1]
        own[...] = rows[:, :half]
        away[...] = rows[:, half:]
    for which in range(3):
        held, transposed = ((tok_held, False), (grad_held, True))[which // 2]
        pair = ins[2 + 2 * which : 4 + 2 * which]
        for at, end in spans(outs[0].shape[2]):
            outs[0][which, :, at:end] = pair_product(held, pair, at, end, transposed)


def second_kernel(ins, outs):
    place = Place()
    products, *heard = ins
    near, far = place.half(place.x), place.half(place.other)
    one = place.core == 1
    for which in range(3):
        for at, end in spans(outs[0].shape[2]):
            near2 = heard[1][which, near, at:end].astype(jnp.float32)
            far1, far2, far3 = [h[which, far, at:end].astype(jnp.float32) for h in heard]
            part1, part2, part3 = [
                products[which, slot * PIECE : (slot + 1) * PIECE, at:end] for slot in range(3)
            ]
            sum1 = part1 + far1 + jnp.where(one, far2 + far3, 0.0)
            high = sum1.astype(jnp.bfloat16)
            rest = sum1 - high.astype(jnp.float32)
            outs[0][which, :, at:end] = high
            outs[1][which, :, at:end] = jnp.where(one, rest, part2 + near2).astype(jnp.bfloat16)
            outs[2][which, :, at:end] = (part3 + far2).astype(jnp.bfloat16)


def unit_kernel(ins, outs):
    place = Place()
    products, first, second = ins[0], ins[1:4], ins[4:7]
    hidden, both = outs
    near, one = place.half(place.x), place.core == 1
    for at, end in spans(hidden.shape[1]):

        def summed(which):
            near1, near2, near3 = [h[which, near, at:end].astype(jnp.float32) for h in first]
            total = products[which, 3 * PIECE :, at:end] + near1
            total = total + jnp.where(one, near2 + near3, 0.0)
            return total + sum(h[which, :, at:end].astype(jnp.float32) for h in second)

        gate, up, d_hidden = [summed(which) for which in range(3)]
        sig_gate = jax.nn.sigmoid(gate)
        hidden[:, at:end] = (gate * sig_gate * up).astype(jnp.bfloat16)
        slope = d_hidden * up * sig_gate * (1.0 + gate * (1.0 - sig_gate))
        both[0, :, at:end] = slope.astype(jnp.bfloat16)
        both[1, :, at:end] = (d_hidden * gate * sig_gate).astype(jnp.bfloat16)


def weave_kernel(ins, outs):
    core = Place().core
    for rows, at_core in zip(ins, (core, 1 - core)):
        for piece in range(NY * NX):
            start = pl.multiple_of((piece * NC + at_core) * PIECE, PIECE)
            outs[0][pl.ds(start, PIECE), :] = rows[piece * PIECE : (piece + 1) * PIECE, :]


def pack_kernel(ins, outs):
    own, near1, near2, near3 = ins
    first, second = outs
    core0 = Place().core == 0
    first[:, :PIECE] = own[...]
    first[:, PIECE:] = near1[...]
    second[:, :PIECE] = jnp.where(core0, near2[...], own[...])
    second[:, PIECE:] = jnp.where(core0, near3[...], near1[...])


def layer_kernel(ins, outs, held):
    hidden, *weights = ins
    core = Place().core
    width = weights[0].shape[1]
    for piece in range(NY * NX):
        start = pl.multiple_of((piece * NC + core) * PIECE, PIECE)
        held[piece * PIECE : (piece + 1) * PIECE, :] = hidden[pl.ds(start, PIECE), :]
    for side, weight in enumerate(weights):
        for at, end in spans(width):
            outs[0][:, side * width + at : side * width + end] = product(
                held[...], weight[:, at:end], False
            )


def input_kernel(ins, outs):
    place = Place()
    layer, own, near1, near2, near3, far1, far2, far3 = ins[:8]
    weights = ins[8:]
    *messages, d_set, kept = outs
    core0 = place.core == 0
    pieces = place.gathered()
    values = [own[...], near1[...], far1[:, :PIECE], far1[:, PIECE:], far2[:, :PIECE], far2[:, PIECE:]]
    values.append(jnp.where(core0, near2[...], far3[:, :PIECE]))
    values.append(jnp.where(core0, near3[...], far3[:, PIECE:]))
    for rows_at, value in zip(pieces, values):
        d_set[:, rows_at, :] = value
    depth = weights[0].shape[0]
    block = NX * PIECE
    for side in range(2):
        for at, end in spans(depth):
            gate, up = [weights[2 * side + i][at:end, :] for i in range(2)]
            total = product(d_set[0], gate, True) + product(d_set[1], up, True)
            columns = slice(side * depth + at, side * depth + end)
            for i, term in enumerate((layer[:, columns], total)):
                kept[i, :, columns] = term[:block]
                for k in range(NZ):
                    rows = term[k * block : (k + 1) * block]
                    messages[k][i, :, columns] = rows.astype(jnp.bfloat16)


def send_first(sent):
    return (
        lax.ppermute(sent[0], "row", row_perm(over_x, over_y(1))),
        lax.ppermute(sent[1], "row", row_perm(over_x, over_y(-1))),
        lax.ppermute(sent[2], "row", row_perm(None, over_y(2))),
    )


def send_second(sent):
    third = lax.ppermute(sent[2], "row", row_perm(over_y(2), None))
    first = lax.ppermute(sent[0], "row", row_perm(over_y(1), over_x))
    return first, lax.ppermute(sent[1], "row", row_perm(over_y(-1), over_x)), third


def body(tokens, gate_weight, up_weight, down_weight, grad_output):
    core = lax.axis_index("row") % NC
    flip = lambda value: lax.ppermute(value, "row", CORE_FLIP)
    after = lambda value, *others: lax.optimization_barrier((value, *others))[0]
    width, ff_width = gate_weight.shape
    half_rows = NY * NX * PIECE
    rows = tokens.shape[0]

    tok_theirs, grad_theirs = flip(tokens), flip(grad_output)
    (mine,) = call(mine_kernel, [tokens, grad_output], [shape((2, rows, width))])
    (own_block,) = call(
        block_kernel, [mine, tok_theirs, grad_theirs], [shape((2, rows, 2 * width))]
    )
    to_flip = lax.optimization_barrier((gate_weight, up_weight, down_weight, tok_theirs, grad_theirs))
    gate_other, up_other, down_other = [flip(weight) for weight in to_flip[:3]]
    own = lax.optimization_barrier((gate_weight, up_weight, down_weight, own_block))[:3]
    gate_own, up_own, down_own = call(keep_kernel, own, [shape(weight.shape) for weight in own])
    early = own_block
    late = [after(own_block, gate_other, gate_own), after(own_block, up_other, gate_own)]
    starts = [late[1], early, late[0], early]
    blocks = [lax.ppermute(starts[step], BOTH, gather_perm(step)) for step in range(NZ)]

    weights = [gate_own, gate_other, up_own, up_other, down_own, down_other]
    held = lambda pieces: [pltpu.VMEM((pieces * PIECE, 2 * width), jnp.bfloat16)] * 2
    tok_half, grad_half, *sent = call(
        first_kernel,
        [own_block, *blocks, *weights],
        [shape((half_rows, 2 * width))] * 2 + [shape((3, 2 * PIECE, ff_width))] * 3,
        held(6),
    )
    heard = send_first(sent)
    products, tok_own, grad_own, tok_away, grad_away = call(
        partial_kernel,
        [tok_half, grad_half, *weights],
        [shape((3, 4 * PIECE, ff_width), jnp.float32)] + [shape((half_rows, width))] * 4,
        held(4),
    )
    tok_other, grad_other = flip(tok_away), flip(grad_away)
    (grad_all,) = call(weave_kernel, [grad_own, grad_other], [shape((2 * half_rows, width))])
    *heard, grad_all, tok_other = lax.optimization_barrier((*heard, grad_all, tok_other))
    sent = call(second_kernel, [products, *heard], [shape((3, PIECE, ff_width))] * 3)
    hidden, d_own = call(
        unit_kernel,
        [products, *heard, *send_second(sent)],
        [shape((PIECE, ff_width)), shape((2, PIECE, ff_width))],
    )

    near = send_second([d_own] * 3)
    hidden = lax.all_gather(after(hidden, near[0]), "row", axis=0, tiled=True)
    first, second = call(pack_kernel, [d_own, *near], [shape((2, 2 * PIECE, ff_width))] * 2)
    far = send_first([first, second, first])
    hidden = after(hidden, far[0])
    (layer,) = call(
        layer_kernel,
        [hidden, down_weight, down_other],
        [shape((half_rows, 2 * width), jnp.float32)],
        [pltpu.VMEM((half_rows, ff_width), jnp.bfloat16)],
    )
    block = (2, rows, 2 * width)
    *messages, d_set, kept = call(
        input_kernel,
        [layer, d_own, *near, *far, gate_weight, up_weight, gate_other, up_other],
        [shape(block)] * 4 + [shape((2, half_rows, ff_width)), shape(block, jnp.float32)],
    )
    heard = {k: lax.ppermute(messages[k], BOTH, scatter_perm(k)) for k in (2, 1, 3, 0)}
    messages = [heard[k] for k in range(NZ)]
    grad_gate, grad_up = call(
        gradient_kernel,
        [tok_own, tok_other, d_set, flip(d_set)],
        [shape((width, ff_width))] * 2,
        [pltpu.VMEM((width, half_rows), jnp.bfloat16)] * 2,
    )
    (grad_down,) = call(down_kernel, [hidden, grad_all], [shape((ff_width, width))])
    *messages, grad_gate, grad_up, grad_down = lax.optimization_barrier(
        (*messages, grad_gate, grad_up, grad_down)
    )
    total = jnp.where(core == 0, kept, 0.0)
    for message in messages:
        total = total + message.astype(jnp.float32)
    total = (total[:, :, :width] + flip(total[:, :, width:])).astype(jnp.bfloat16)
    return (total[0], total[1], grad_gate, grad_up, grad_down)


def solution(mesh):
    placed = (P("col", "row"), P("row", "col"), P("row", "col"), P("col", "row"), P("col", "row"))
    return jax.shard_map(
        body,
        mesh=mesh,
        in_specs=placed,
        out_specs=(
            P("col", "row"),
            P("col", "row"),
            P("row", "col"),
            P("row", "col"),
            P("col", "row"),
        ),
        check_vma=False,
    )
```
